32 devices in a mesh: blk: 4 (over y, x), tones: 8 (over z, core).
Axes of the slice: x: 2, y: 2, z: 4, core: 2. Of those that a mesh axis runs over, the one named last changes fastest.
Arguments:
- channel: float32 [256, 2, 256, 1024], P('tones', None, None, 'blk'), may hold values from -0.25 to 0.25
- received: float32 [256, 2, 448, 1024], P('tones', None, None, 'blk'), may hold values from -6 to 6
- step_sizes: float32 [4, 2], P('blk'), may hold values from 0.1 to 0.4
- hop_offset: int32 [8], replicated, may hold values from 0 to 3
- user_order: int32 [256], replicated, may hold values from 0 to 255, each once
Outputs:
- soft_symbols: float32 [256, 2, 448, 256], P(('blk', 'tones'))
The draws below stay inside these ranges and needn't reach their ends.
Inputs may be any that keep to these rules, and one draw needn't show every extreme that they name: `user_order`: each user appears exactly once.
All inputs are finite; a program needn't handle non-finite values.
Results may differ from the reference program's by a relative error of at most 0.0003.
Values sent between devices are 32-bit elements; how exact they have to be, the bound alone decides.
No kernel may reach another device: no remote copies, remote signals or barrier semaphores. Data moves between devices by JAX's collectives and lax.ppermute only.
A program may use at most 192 MiB of HBM per device.

```python
import jax
import jax.numpy as jnp
from jax import lax

USER_COUNT = 256
SUBARRAY_WIDTH = 256
TRANSFORM_LENGTH = 256
SYMBOL_COUNT = 448
SUBS = 4
TOTAL_ANTENNAS = 1024
TONE_DEV = 32
N_TONES = 8


def touch_ends(array, own_key, least, top_value):
    longest = array.shape.index(max(array.shape))
    spots = []
    for shift in (0, 1):
        where = [jax.random.randint(jax.random.fold_in(own_key, axis), (), 0, length) for axis, length in enumerate(array.shape)]
        where[longest] = (where[longest] + shift) % array.shape[longest]
        spots.append(tuple(where))
    return array.at[spots[0]].set(least).at[spots[1]].set(top_value)


def block_scale(rng, extent, shards, least, largest):
    def one(axis_at, shards_of):
        steps = jax.random.uniform(jax.random.fold_in(jax.random.fold_in(rng, 6), axis_at), (shards_of,), jnp.float32, least / len(shards), largest / len(shards))
        return jnp.repeat(jnp.exp(steps), extent[axis_at] // shards_of).reshape((-1,) + (1,) * (len(extent) - axis_at - 1))

    factor_of = one(*shards[0])
    for cut in shards[1:]:
        factor_of = factor_of * one(*cut)
    return factor_of


def bell_draw(rng, extent, width, most, shards=(), held_as=jnp.bfloat16):
    result = jax.random.normal(rng, extent, jnp.float32) * width
    if len(shards) > 0:
        result = block_scale(rng, extent, shards, -0.22, 0.18) * result
    return jnp.clip(result, min=-most, max=most).astype(held_as)


def setup_inputs(seed: int = 0) -> dict:
    streams_of = jax.random.split(jax.random.key(seed), 6)
    return {
        "channel": bell_draw(streams_of[0], (TRANSFORM_LENGTH, 2, USER_COUNT, TOTAL_ANTENNAS), (2 * SUBARRAY_WIDTH) ** -0.5, 0.25, ((0, 8), (3, 4)), jnp.float32),
        "received": bell_draw(streams_of[1], (TRANSFORM_LENGTH, 2, SYMBOL_COUNT, TOTAL_ANTENNAS), 1.0, 6.0, ((0, 8), (3, 4)), jnp.float32),
        "step_sizes": jnp.clip(0.1 + 0.3 * jax.random.uniform(streams_of[2], (SUBS, 2), jnp.float32) ** block_scale(streams_of[2], (SUBS, 2), ((0, 4),), -0.2, 0.2), 0.1, 0.4),
        "hop_offset": touch_ends(jax.random.randint(streams_of[3], (N_TONES,), 0, SUBS), jax.random.fold_in(streams_of[3], 1), 0, SUBS - 1).astype(jnp.int32),
        "user_order": jax.random.permutation(streams_of[4], USER_COUNT).astype(jnp.int32),
    }


def forward(left, right):
    return jnp.einsum('...su,...ub->...sb', left, right, precision=lax.Precision.HIGHEST)

def adjoint(left, right):
    return jnp.einsum('...sb,...ub->...su', left, right, precision=lax.Precision.HIGHEST)

def gradient_step(estimate, chan, recv, step_rate):
    est_real = estimate[..., 0, :, :]
    est_imag = estimate[..., 1, :, :]
    chan_real = chan[..., 0, :, :]
    channel_imaginary = chan[..., 1, :, :]
    res_real = recv[..., 0, :, :] - (forward(est_real, chan_real) - forward(est_imag, channel_imaginary))
    res_imag = recv[..., 1, :, :] - (forward(est_real, channel_imaginary) + forward(est_imag, chan_real))
    grad_real = adjoint(res_real, chan_real) + adjoint(res_imag, channel_imaginary)
    grad_imag = adjoint(res_imag, chan_real) - adjoint(res_real, channel_imaginary)
    return jnp.tanh(jnp.stack([est_real + step_rate * grad_real, est_imag + step_rate * grad_imag], axis=-3))

def tables(length):
    index_row = jnp.arange(length, dtype=jnp.int32)
    products = index_row[:, None] * index_row[None, :] % length
    angle = 2.0 * jnp.pi / length * products.astype(jnp.float32)
    scale = 1.0 / jnp.sqrt(jnp.float32(length))
    return (jnp.cos(angle) * scale, jnp.sin(angle) * scale)

def despread(spread):
    cosine_table, sine_table = tables(spread.shape[-1])
    spread_real = spread[:, 0]
    spread_imag = spread[:, 1]
    highest = lax.Precision.HIGHEST
    out_real = jnp.einsum('isk,kn->isn', spread_real, cosine_table, precision=highest) - jnp.einsum('isk,kn->isn', spread_imag, sine_table, precision=highest)
    out_imag = jnp.einsum('isk,kn->isn', spread_real, sine_table, precision=highest) + jnp.einsum('isk,kn->isn', spread_imag, cosine_table, precision=highest)
    return jnp.tanh(jnp.stack([out_real, out_imag], axis=1))

def reference(channel, received, step_sizes, hop_offset, user_order):
    chain_len = SUBS
    block_rows = SYMBOL_COUNT // SUBS
    chan_all = channel.reshape(N_TONES, TONE_DEV, 2, USER_COUNT, chain_len, SUBARRAY_WIDTH)
    recv_all = received.reshape(N_TONES, TONE_DEV, 2, chain_len, block_rows, chain_len, SUBARRAY_WIDTH)

    def one_group(inputs):
        chan_group, recv_group, offset = inputs
        chan_group = jnp.transpose(chan_group, (3, 0, 1, 2, 4))
        recv_group = jnp.transpose(recv_group, (4, 2, 0, 1, 3, 5))
        blocks = jnp.arange(chain_len, dtype=jnp.int32)
        estimate = jnp.zeros((chain_len, TONE_DEV, 2, block_rows, USER_COUNT), jnp.float32)
        for hop_index in range(chain_len):
            subarray = (blocks + offset + hop_index) % chain_len
            chan_sel = chan_group[subarray]
            received_selected = recv_group[subarray, blocks]
            rate_sel = step_sizes[subarray]
            for substep in range(2):
                estimate = gradient_step(estimate, chan_sel, received_selected, rate_sel[:, substep][:, None, None, None])
        return estimate
    est_all = lax.map(one_group, (chan_all, recv_all, hop_offset))
    spread = jnp.transpose(est_all, (5, 3, 1, 4, 0, 2)).reshape(USER_COUNT, 2, SYMBOL_COUNT, TRANSFORM_LENGTH)
    spread = jnp.take(spread, user_order, axis=0)
    return despread(spread)
```

```python
import functools

import jax
import jax.numpy as jnp
import ml_dtypes
import numpy as np
from jax import lax
from jax.experimental import pallas as pl
from jax.experimental.pallas import tpu as pltpu
from jax.sharding import PartitionSpec as P

F32 = jnp.float32
BF16 = jnp.bfloat16
VMEM_LIMIT = 56 * 1024 * 1024
ANY = pl.BlockSpec(memory_space=pl.ANY)
SMEM = pl.BlockSpec(memory_space=pltpu.SMEM)


def split(value):
    high = value.astype(BF16)
    return high, (value - high.astype(F32)).astype(BF16)


def dot(left, right, contract):
    return lax.dot_general(left, right, ((contract[:1], contract[1:]), ((), ())), preferred_element_type=F32)


def dot3(left, right, contract):
    left_high, left_low = left
    right_high, right_low = right
    return (
        dot(left_high, right_high, contract)
        + dot(left_high, right_low, contract)
        + dot(left_low, right_high, contract)
    )


def triangle(users):
    row = lax.broadcasted_iota(jnp.int32, (users, users), 0)
    column = lax.broadcasted_iota(jnp.int32, (users, users), 1)
    return row, column


def prepare_body(start, chan, recv, *refs):
    out = refs[-1]
    users = chan.shape[2]
    symbols = recv.shape[2]
    left_real = split(jnp.concatenate([chan[0, 0], recv[0, 0]], 0))
    left_imag = split(jnp.concatenate([chan[0, 1], recv[0, 1]], 0))
    right = tuple(
        jnp.concatenate([real[:users], imag[:users]], 1) for real, imag in zip(left_real, left_imag)
    )
    real = dot3(tuple(jnp.concatenate(pair, 1) for pair in zip(left_real, left_imag)), right, (1, 1))
    imag = dot3(
        tuple(jnp.concatenate([b, -a], 1) for a, b in zip(left_real, left_imag)), right, (1, 1)
    )
    row, column = triangle(users)
    out[0, :users] = jnp.where(row <= column, real[:users], imag[:users])
    out[0, users : users + symbols] = real[users:]
    out[0, users + symbols :] = imag[users:]


def prepare(channel, received, start, count, after):
    _, _, users, width = channel.shape
    symbols = received.shape[2]
    rows = users + 2 * symbols
    return pl.pallas_call(
        prepare_body,
        out_shape=jax.ShapeDtypeStruct((count, rows, users), F32),
        grid_spec=pltpu.PrefetchScalarGridSpec(
            num_scalar_prefetch=1,
            grid=(count,),
            in_specs=[
                pl.BlockSpec((1, 2, users, width), lambda i, start: (start[0] + i, 0, 0, 0)),
                pl.BlockSpec((1, 2, symbols, width), lambda i, start: (start[0] + i, 0, 0, 0)),
            ]
            + [ANY] * len(after),
            out_specs=pl.BlockSpec((1, rows, users), lambda i, start: (i, 0, 0)),
        ),
        compiler_params=pltpu.CompilerParams(vmem_limit_bytes=VMEM_LIMIT),
        cost_estimate=pl.CostEstimate(
            flops=count * 2 * 12 * (users + symbols) * width * users,
            bytes_accessed=4 * count * (2 * (users + symbols) * width + rows * users),
            transcendentals=0,
        ),
        name="prepare",
    )(start, channel, received, *after)


def unpack(packed, gram, sub):
    users = packed.shape[0]
    row, column = triangle(users)
    turned = packed.T
    real = split(jnp.where(row <= column, packed, turned))
    imag = split(jnp.where(row > column, packed, jnp.where(row < column, -turned, 0.0)))
    for part in range(2):
        gram[sub, part, :users, :users] = real[part]
        gram[sub, part, :users, users:] = imag[part]
        gram[sub, part, users:, :users] = -imag[part]
        gram[sub, part, users:, users:] = real[part]


def step(estimate, matched, gram, sub, rate):
    product = dot3(split(estimate), (gram[sub, 0], gram[sub, 1]), (1, 0))
    return jnp.tanh(estimate + rate * (matched - product))


def filtered(ref, users, symbols, rows, block):
    parts = []
    for part in range(2):
        first = pl.multiple_of(users + part * symbols + block * rows, 8)
        parts.append(ref[0, pl.ds(first, rows), :])
    return jnp.concatenate(parts, 1)


def chain_body(round_index, kind, symbols, scalars, rates, own, peer, *refs):
    users = own.shape[2]
    rows = symbols // kind["blocks"]
    side = scalars[0]
    even_block = scalars[1 + 2 * round_index]
    odd_block = scalars[2 + 2 * round_index]
    gram, matched = refs[-2:]
    for ref, sub in ((own, side), (peer, 1 - side)):
        unpack(ref[0, :users], gram, sub)
        for slot, block in enumerate((even_block, odd_block)):
            matched[sub, slot * rows : (slot + 1) * rows] = filtered(ref, users, symbols, rows, block)

    if round_index == 0:
        out = refs[-3:-2]
        even = jnp.tanh(rates[0, 0] * matched[0, :rows])
        even = step(even, matched[0, :rows], gram, 0, rates[0, 1])
        even = step(even, matched[1, :rows], gram, 1, rates[1, 0])
        odd = jnp.tanh(rates[1, 0] * matched[1, rows:])
        both = step(jnp.concatenate([even, odd], 0), matched[1], gram, 1, rates[1, 1])
    else:
        out = refs[-4:-2] if kind["last"] else refs[-3:-2]
        came = refs[0]
        both = jnp.concatenate(
            [jnp.concatenate([came[0, slot, 0], came[0, slot, 1]], 1) for slot in range(2)], 0
        )
        for sub in range(2):
            for substep in range(2):
                both = step(both, matched[sub], gram, sub, rates[sub, substep])
    for slot in range(2):
        for part in range(2):
            piece = both[slot * rows : (slot + 1) * rows, part * users : (part + 1) * users]
            if len(out) == 2:
                out[slot][0, part] = piece
            else:
                out[0][0, slot, part] = piece


def chain(round_index, last, blocks, scalars, rates, own, peer, came, after):
    count, packed_rows, users = own.shape
    symbols = (packed_rows - users) // 2
    rows = symbols // blocks
    packed_spec = pl.BlockSpec((1, packed_rows, users), lambda i, s: (i, 0, 0))
    both_spec = pl.BlockSpec((1, 2, 2, rows, users), lambda i, s: (i, 0, 0, 0, 0))
    one_spec = pl.BlockSpec((1, 2, rows, users), lambda i, s: (i, 0, 0, 0))
    both_shape = jax.ShapeDtypeStruct((count, 2, 2, rows, users), F32)
    one_shape = jax.ShapeDtypeStruct((count, 2, rows, users), F32)
    return pl.pallas_call(
        functools.partial(chain_body, round_index, {"blocks": blocks, "last": last}, symbols),
        out_shape=[one_shape, one_shape] if last else both_shape,
        grid_spec=pltpu.PrefetchScalarGridSpec(
            num_scalar_prefetch=1,
            grid=(count,),
            in_specs=[SMEM, packed_spec, packed_spec] + [both_spec] * len(came) + [ANY] * len(after),
            out_specs=[one_spec, one_spec] if last else both_spec,
            scratch_shapes=[
                pltpu.VMEM((2, 2, 2 * users, 2 * users), BF16),
                pltpu.VMEM((2, 2 * rows, 2 * users), F32),
            ],
        ),
        compiler_params=pltpu.CompilerParams(vmem_limit_bytes=VMEM_LIMIT),
        cost_estimate=pl.CostEstimate(
            flops=count * 2 * 12 * 8 * rows * users * users,
            bytes_accessed=4 * count * (2 * packed_rows + 8 * rows) * users,
            transcendentals=count * 16 * rows * users,
        ),
        name="chain%d" % round_index,
    )(scalars, rates, own, peer, *came, *after)


def finish_body(round_index, count, rows, symbols, scalars, rates, own, peer, even, odd, order, *refs):
    users = own.shape[2]
    out, gram, gathered = refs[-3:]
    tone = pl.program_id(0)
    side = scalars[0]
    block = scalars[2 + 2 * round_index]
    even_slot = scalars[1 + 2 * (round_index + 1)]

    @pl.when(side == 0)
    def _():
        unpack(own[0, :users], gram, 0)

    @pl.when(side != 0)
    def _():
        unpack(peer[0, :users], gram, 0)

    matched = jnp.where(
        side == 0,
        filtered(own, users, symbols, rows, block),
        filtered(peer, users, symbols, rows, block),
    )
    estimate = jnp.concatenate([odd[0, 0], odd[0, 1]], 1)
    for substep in range(2):
        estimate = step(estimate, matched, gram, 0, rates[0, substep])
    for part in range(2):
        first = (tone * 2 + part) * 2
        odd_row = pl.multiple_of((first + 1 - even_slot) * rows, 8)
        even_row = pl.multiple_of((first + even_slot) * rows, 8)
        gathered[pl.ds(odd_row, rows), :] = estimate[:, part * users : (part + 1) * users]
        gathered[pl.ds(even_row, rows), :] = even[0, part]

    @pl.when(tone == count - 1)
    def _():
        high, low = split(gathered[...])
        turned = dot(order[...], high, (1, 1)) + dot(order[...], low, (1, 1))
        out[...] = turned.reshape(out.shape)


def finish(round_index, blocks, owners, scalars, rates, own, peer, even, odd, order, after):
    count, packed_rows, users = own.shape
    symbols = (packed_rows - users) // 2
    rows = symbols // blocks
    packed_spec = pl.BlockSpec((1, packed_rows, users), lambda i, s: (i, 0, 0))
    one_spec = pl.BlockSpec((1, 2, rows, users), lambda i, s: (i, 0, 0, 0))
    shape = (owners, users // owners, count * 4 * rows)
    return pl.pallas_call(
        functools.partial(finish_body, round_index, count, rows, symbols),
        out_shape=jax.ShapeDtypeStruct(shape, F32),
        grid_spec=pltpu.PrefetchScalarGridSpec(
            num_scalar_prefetch=1,
            grid=(count,),
            in_specs=[
                SMEM,
                packed_spec,
                packed_spec,
                one_spec,
                one_spec,
                pl.BlockSpec((users, users), lambda i, s: (0, 0)),
            ]
            + [ANY] * len(after),
            out_specs=pl.BlockSpec(shape, lambda i, s: (0, 0, 0)),
            scratch_shapes=[
                pltpu.VMEM((1, 2, 2 * users, 2 * users), BF16),
                pltpu.VMEM((count * 4 * rows, users), F32),
            ],
        ),
        compiler_params=pltpu.CompilerParams(vmem_limit_bytes=VMEM_LIMIT),
        cost_estimate=pl.CostEstimate(
            flops=count * 2 * 12 * 3 * rows * users * users,
            bytes_accessed=4 * count * (2 * packed_rows + 8 * rows) * users,
            transcendentals=count * 4 * rows * users,
        ),
        name="finish",
    )(scalars, rates, own, peer, even, odd, order, *after)


def despread_body(groups, half, sizes, rows, source, table, *refs):
    pieces = refs[: len(sizes)]
    out, tones_first, symbols_first = refs[len(sizes) :]
    items = out.shape[0]
    length = groups * 2 * half
    pair = pl.program_id(0)
    for slot in range(2):
        block = 2 * pair + slot

        def gather(group, carry):
            position = source[block * groups + group]
            for side in range(2):
                start = group * 2 * half + side * half
                for piece, size in zip(pieces, sizes):
                    src = (2 * position + side) * groups + group
                    for tone in range(size):
                        for part in range(2):
                            lane = ((tone * 2 + part) * 2 + slot) * rows
                            tones_first[part, start + tone, :, :rows] = piece[src, :, lane : lane + rows]
                    start = start + size
            return carry

        lax.fori_loop(0, groups, gather, 0)
        for item in range(items):
            for part in range(2):
                turned = split(tones_first[part, :, item, :].T[:rows])
                for precision in range(2):
                    symbols_first[
                        precision, item * rows : (item + 1) * rows, part * length : (part + 1) * length
                    ] = turned[precision]
        result = jnp.tanh(
            dot3((symbols_first[0], symbols_first[1]), (table[0], table[1]), (1, 0))
        )
        for item in range(items):
            for part in range(2):
                out[item, part, slot * rows : (slot + 1) * rows, :] = result[
                    item * rows : (item + 1) * rows, part * length : (part + 1) * length
                ]


def despread(pieces, sizes, groups, half, blocks, rows, source):
    items = pieces[0].shape[1]
    length = groups * 2 * half
    lanes = -(-rows // 128) * 128
    index = np.arange(length)
    angle = 2.0 * np.pi / length * (index[:, None] * index[None, :] % length)
    cosine, sine = np.cos(angle) / np.sqrt(length), np.sin(angle) / np.sqrt(length)
    table = np.block([[cosine, sine], [-sine, cosine]])
    high = table.astype(ml_dtypes.bfloat16)
    table = np.stack([high, (table - high.astype(np.float64)).astype(ml_dtypes.bfloat16)])
    return pl.pallas_call(
        functools.partial(despread_body, groups, half, sizes, rows),
        out_shape=jax.ShapeDtypeStruct((items, 2, blocks * rows, length), F32),
        grid_spec=pltpu.PrefetchScalarGridSpec(
            num_scalar_prefetch=1,
            grid=(blocks // 2,),
            in_specs=[pl.BlockSpec(table.shape, lambda i, s: (0, 0, 0))]
            + [pl.BlockSpec(piece.shape, lambda i, s: (0, 0, 0)) for piece in pieces],
            out_specs=pl.BlockSpec((items, 2, 2 * rows, length), lambda i, s: (0, 0, i, 0)),
            scratch_shapes=[
                pltpu.VMEM((2, length, items, lanes), F32),
                pltpu.VMEM((2, items * rows, 2 * length), BF16),
            ],
        ),
        compiler_params=pltpu.CompilerParams(vmem_limit_bytes=VMEM_LIMIT),
        cost_estimate=pl.CostEstimate(
            flops=2 * 12 * items * blocks * rows * length * length,
            bytes_accessed=16 * items * blocks * rows * length,
            transcendentals=2 * items * blocks * rows * length,
        ),
        name="despread",
    )(source, jnp.asarray(table), *pieces)


def on_device(channel, received, step_sizes, hop_offset, user_order):
    blocks = lax.axis_size("blk")
    groups = lax.axis_size("tones")
    pairs = blocks // 2
    half = channel.shape[0] // 2
    users = channel.shape[2]
    rows = received.shape[2] // blocks
    owners = blocks * groups
    position = lax.axis_index("blk")
    offset = hop_offset[lax.axis_index("tones")]
    side = position % 2
    pair = position // 2

    swap = [(p, p ^ 1) for p in range(blocks)]
    onward = [(p, (p + 2) % blocks) for p in range(blocks)]

    size = 2 if half % 2 == 0 else 1
    sizes = [size] * (half // size)
    starts = [sum(sizes[:c]) for c in range(len(sizes))]
    chunks = len(sizes)

    scalars = [side]
    for r in range(pairs + 1):
        scalars += [(2 * (pair - r) - offset) % blocks, (2 * (pair - r) + 1 - offset) % blocks]
    scalars.append((offset + 0) % 2)
    scalars = jnp.stack(scalars).astype(jnp.int32)
    peer_rates = lax.ppermute(step_sizes, "blk", swap)
    rates = jnp.where(
        side == 0,
        jnp.concatenate([step_sizes, peer_rates], 0),
        jnp.concatenate([peer_rates, step_sizes], 0),
    )
    order = (user_order[:, None] == jnp.arange(users, dtype=jnp.int32)[None, :]).astype(BF16)

    begins = (jnp.arange(blocks, dtype=jnp.int32)[:, None] + hop_offset[None, :]) % blocks
    source = jnp.where(begins % 2 == 0, begins // 2 + pairs - 1, begins // 2) % pairs

    own, peer, came, pieces = {}, {}, {}, []

    def ready_peer(c, after):
        start = ((1 - side) * half + starts[c]).astype(jnp.int32).reshape(1)
        sent = prepare(channel, received, start, sizes[c], after)
        peer[c] = lax.ppermute(sent, "blk", swap)
        return sent

    def ready_own(c, after):
        start = (side * half + starts[c]).astype(jnp.int32).reshape(1)
        own[c] = prepare(channel, received, start, sizes[c], after)
        return own[c]

    last = ready_peer(0, [])
    if chunks > 1:
        last = ready_peer(1, [last])
    last = ready_own(0, [last])
    for c in range(chunks):
        last = chain(0, False, blocks, scalars, rates, own[c], peer[c], [], [last])
        both = lax.ppermute(last, "blk", onward)
        if c + 2 < chunks:
            last = ready_peer(c + 2, [last])
        if c + 1 < chunks:
            last = ready_own(c + 1, [last])
        for r in range(1, pairs):
            done = chain(r, r == pairs - 1, blocks, scalars, rates, own[c], peer[c], [both], [last])
            if r < pairs - 1:
                both = lax.ppermute(done, "blk", onward)
                last = done
        even, odd = done
        odd = lax.ppermute(odd, "blk", onward)
        last = finish(pairs, blocks, owners, scalars, rates, own[c], peer[c], even, odd, order, [])
        pieces.append(
            lax.all_to_all(last, ("blk", "tones"), split_axis=0, concat_axis=0, tiled=True)
        )
    return despread(pieces, sizes, groups, half, blocks, rows, source.reshape(-1))


def solution(mesh):
    in_specs = (
        P("tones", None, None, "blk"),
        P("tones", None, None, "blk"),
        P("blk", None),
        P(),
        P(),
    )
    out_specs = P(("blk", "tones"), None, None, None)
    return jax.shard_map(
        on_device, mesh=mesh, in_specs=in_specs, out_specs=out_specs, check_vma=False
    )
```

```python
import functools

import jax
import jax.numpy as jnp
import ml_dtypes
import numpy as np
from jax import lax
from jax.experimental import pallas as pl
from jax.experimental.pallas import tpu as pltpu
from jax.sharding import PartitionSpec as P

F32 = jnp.float32
BF16 = jnp.bfloat16
VMEM_LIMIT = 56 * 1024 * 1024
ANY = pl.BlockSpec(memory_space=pl.ANY)
SMEM = pl.BlockSpec(memory_space=pltpu.SMEM)


def split(value):
    high = value.astype(BF16)
    return high, (value - high.astype(F32)).astype(BF16)


def dot(left, right, contract):
    return lax.dot_general(left, right, ((contract[:1], contract[1:]), ((), ())), preferred_element_type=F32)


def dot3(left, right, contract):
    left_high, left_low = left
    right_high, right_low = right
    return (
        dot(left_high, right_high, contract)
        + dot(left_high, right_low, contract)
        + dot(left_low, right_high, contract)
    )


def triangle(users):
    row = lax.broadcasted_iota(jnp.int32, (users, users), 0)
    column = lax.broadcasted_iota(jnp.int32, (users, users), 1)
    return row, column


def prepare_body(carry, start, rates, chan, recv, *refs):
    out = refs[-1]
    users = chan.shape[2]
    symbols = recv.shape[2]
    left_real = split(jnp.concatenate([chan[0, 0], recv[0, 0]], 0))
    left_imag = split(jnp.concatenate([chan[0, 1], recv[0, 1]], 0))
    right = tuple(
        jnp.concatenate([real[:users], imag[:users]], 1) for real, imag in zip(left_real, left_imag)
    )
    real = dot3(tuple(jnp.concatenate(pair, 1) for pair in zip(left_real, left_imag)), right, (1, 1))
    imag = dot3(
        tuple(jnp.concatenate([b, -a], 1) for a, b in zip(left_real, left_imag)), right, (1, 1)
    )
    row, column = triangle(users)
    out[0, :users] = jnp.where(row <= column, real[:users], imag[:users])
    rows = users + 2 * symbols
    out[0, users : users + symbols] = real[users:]
    out[0, users + symbols : rows] = imag[users:]
    if carry:
        lane = lax.broadcasted_iota(jnp.int32, (carry, users), 1)
        out[0, rows:] = jnp.where(lane == 0, rates[0, 0], rates[0, 1])


def prepare(channel, received, step_sizes, start, count, carry, after):
    _, _, users, width = channel.shape
    symbols = received.shape[2]
    rows = users + 2 * symbols + carry
    return pl.pallas_call(
        functools.partial(prepare_body, carry),
        out_shape=jax.ShapeDtypeStruct((count, rows, users), F32),
        grid_spec=pltpu.PrefetchScalarGridSpec(
            num_scalar_prefetch=1,
            grid=(count,),
            in_specs=[
                SMEM,
                pl.BlockSpec((1, 2, users, width), lambda i, start: (start[0] + i, 0, 0, 0)),
                pl.BlockSpec((1, 2, symbols, width), lambda i, start: (start[0] + i, 0, 0, 0)),
            ]
            + [ANY] * len(after),
            out_specs=pl.BlockSpec((1, rows, users), lambda i, start: (i, 0, 0)),
        ),
        compiler_params=pltpu.CompilerParams(vmem_limit_bytes=VMEM_LIMIT),
        cost_estimate=pl.CostEstimate(
            flops=count * 2 * 12 * (users + symbols) * width * users,
            bytes_accessed=4 * count * (2 * (users + symbols) * width + rows * users),
            transcendentals=0,
        ),
        name="prepare",
    )(start, step_sizes, channel, received, *after)


def unpack(packed, gram, sub):
    users = packed.shape[0]
    row, column = triangle(users)
    turned = packed.T
    real = split(jnp.where(row <= column, packed, turned))
    imag = split(jnp.where(row > column, packed, jnp.where(row < column, -turned, 0.0)))
    for part in range(2):
        gram[sub, part, :users, :users] = real[part]
        gram[sub, part, :users, users:] = imag[part]
        gram[sub, part, users:, :users] = -imag[part]
        gram[sub, part, users:, users:] = real[part]


def step(estimate, matched, gram, sub, rate):
    product = dot3(split(estimate), (gram[sub, 0], gram[sub, 1]), (1, 0))
    return jnp.tanh(estimate + rate * (matched - product))


def filtered(ref, users, symbols, rows, block):
    parts = []
    for part in range(2):
        first = pl.multiple_of(users + part * symbols + block * rows, 8)
        parts.append(ref[0, pl.ds(first, rows), :])
    return jnp.concatenate(parts, 1)


def chain_body(round_index, kind, symbols, scalars, rates, own, peer, *refs):
    users = own.shape[2]
    rows = symbols // kind["blocks"]
    side = scalars[0]
    even_block = scalars[1 + 2 * round_index]
    odd_block = scalars[2 + 2 * round_index]
    gram, matched = refs[-2:]
    for ref, sub in ((own, side), (peer, 1 - side)):
        unpack(ref[0, :users], gram, sub)
        for slot, block in enumerate((even_block, odd_block)):
            matched[sub, slot * rows : (slot + 1) * rows] = filtered(ref, users, symbols, rows, block)

    if round_index == 0:
        out = refs[-3:-2]
        even = jnp.tanh(rates[0, 0] * matched[0, :rows])
        even = step(even, matched[0, :rows], gram, 0, rates[0, 1])
        even = step(even, matched[1, :rows], gram, 1, rates[1, 0])
        odd = jnp.tanh(rates[1, 0] * matched[1, rows:])
        both = step(jnp.concatenate([even, odd], 0), matched[1], gram, 1, rates[1, 1])
    else:
        out = refs[-4:-2] if kind["last"] else refs[-3:-2]
        came = refs[0]
        both = jnp.concatenate(
            [jnp.concatenate([came[0, slot, 0], came[0, slot, 1]], 1) for slot in range(2)], 0
        )
        for sub in range(2):
            for substep in range(2):
                both = step(both, matched[sub], gram, sub, rates[sub, substep])
    for slot in range(2):
        for part in range(2):
            piece = both[slot * rows : (slot + 1) * rows, part * users : (part + 1) * users]
            if len(out) == 2:
                out[slot][0, part] = piece
            else:
                out[0][0, slot, part] = piece


def chain(round_index, last, blocks, scalars, rates, own, peer, came, after):
    count, packed_rows, users = own.shape
    symbols = (packed_rows - users) // 2
    rows = symbols // blocks
    packed_spec = pl.BlockSpec((1, packed_rows, users), lambda i, s: (i, 0, 0))
    both_spec = pl.BlockSpec((1, 2, 2, rows, users), lambda i, s: (i, 0, 0, 0, 0))
    one_spec = pl.BlockSpec((1, 2, rows, users), lambda i, s: (i, 0, 0, 0))
    both_shape = jax.ShapeDtypeStruct((count, 2, 2, rows, users), F32)
    one_shape = jax.ShapeDtypeStruct((count, 2, rows, users), F32)
    return pl.pallas_call(
        functools.partial(chain_body, round_index, {"blocks": blocks, "last": last}, symbols),
        out_shape=[one_shape, one_shape] if last else both_shape,
        grid_spec=pltpu.PrefetchScalarGridSpec(
            num_scalar_prefetch=1,
            grid=(count,),
            in_specs=[SMEM, packed_spec, packed_spec] + [both_spec] * len(came) + [ANY] * len(after),
            out_specs=[one_spec, one_spec] if last else both_spec,
            scratch_shapes=[
                pltpu.VMEM((2, 2, 2 * users, 2 * users), BF16),
                pltpu.VMEM((2, 2 * rows, 2 * users), F32),
            ],
        ),
        compiler_params=pltpu.CompilerParams(vmem_limit_bytes=VMEM_LIMIT),
        cost_estimate=pl.CostEstimate(
            flops=count * 2 * 12 * 8 * rows * users * users,
            bytes_accessed=4 * count * (2 * packed_rows + 8 * rows) * users,
            transcendentals=count * 16 * rows * users,
        ),
        name="chain%d" % round_index,
    )(scalars, rates, own, peer, *came, *after)


def finish_body(round_index, count, rows, symbols, scalars, rates, own, peer, even, odd, order, *refs):
    users = own.shape[2]
    out, gram, gathered = refs[-3:]
    tone = pl.program_id(0)
    side = scalars[0]
    block = scalars[2 + 2 * round_index]
    even_slot = scalars[1 + 2 * (round_index + 1)]

    @pl.when(side == 0)
    def _():
        unpack(own[0, :users], gram, 0)

    @pl.when(side != 0)
    def _():
        unpack(peer[0, :users], gram, 0)

    matched = jnp.where(
        side == 0,
        filtered(own, users, symbols, rows, block),
        filtered(peer, users, symbols, rows, block),
    )
    estimate = jnp.concatenate([odd[0, 0], odd[0, 1]], 1)
    for substep in range(2):
        estimate = step(estimate, matched, gram, 0, rates[0, substep])
    for part in range(2):
        first = (tone * 2 + part) * 2
        odd_row = pl.multiple_of((first + 1 - even_slot) * rows, 8)
        even_row = pl.multiple_of((first + even_slot) * rows, 8)
        gathered[pl.ds(odd_row, rows), :] = estimate[:, part * users : (part + 1) * users]
        gathered[pl.ds(even_row, rows), :] = even[0, part]

    @pl.when(tone == count - 1)
    def _():
        high, low = split(gathered[...])
        turned = dot(order[...], high, (1, 1)) + dot(order[...], low, (1, 1))
        out[...] = turned.reshape(out.shape)


def finish(round_index, blocks, owners, scalars, rates, own, peer, even, odd, order, after):
    count, packed_rows, users = own.shape
    symbols = (packed_rows - users) // 2
    rows = symbols // blocks
    packed_spec = pl.BlockSpec((1, packed_rows, users), lambda i, s: (i, 0, 0))
    one_spec = pl.BlockSpec((1, 2, rows, users), lambda i, s: (i, 0, 0, 0))
    shape = (owners, users // owners, count * 4 * rows)
    return pl.pallas_call(
        functools.partial(finish_body, round_index, count, rows, symbols),
        out_shape=jax.ShapeDtypeStruct(shape, F32),
        grid_spec=pltpu.PrefetchScalarGridSpec(
            num_scalar_prefetch=1,
            grid=(count,),
            in_specs=[
                SMEM,
                packed_spec,
                packed_spec,
                one_spec,
                one_spec,
                pl.BlockSpec((users, users), lambda i, s: (0, 0)),
            ]
            + [ANY] * len(after),
            out_specs=pl.BlockSpec(shape, lambda i, s: (0, 0, 0)),
            scratch_shapes=[
                pltpu.VMEM((1, 2, 2 * users, 2 * users), BF16),
                pltpu.VMEM((count * 4 * rows, users), F32),
            ],
        ),
        compiler_params=pltpu.CompilerParams(vmem_limit_bytes=VMEM_LIMIT),
        cost_estimate=pl.CostEstimate(
            flops=count * 2 * 12 * 3 * rows * users * users,
            bytes_accessed=4 * count * (2 * packed_rows + 8 * rows) * users,
            transcendentals=count * 4 * rows * users,
        ),
        name="finish",
    )(scalars, rates, own, peer, even, odd, order, *after)


def despread_body(groups, sizes, rows, folded, first, last, source, table, *refs):
    pieces = refs[: len(sizes)]
    if not first:
        total = refs[len(sizes)]
    out, tones_first, symbols_first = refs[-3:]
    items = out.shape[0]
    length = out.shape[3]
    tones = sum(sizes)
    pair = pl.program_id(0)
    for slot in range(2):
        block = 2 * pair + slot

        def gather(group, carry):
            position = source[block * groups + group]
            for side in range(2):
                place = (group * 2 + side) * tones * 2
                src = (2 * position + side) * groups + group
                for piece, size in zip(pieces, sizes):
                    for tone in range(2 * size):
                        lane = (tone * 2 + slot) * rows
                        tones_first[place + tone, :, :rows] = piece[src, :, lane : lane + rows]
                    place = place + 2 * size
            return carry

        lax.fori_loop(0, groups, gather, 0)
        for item in range(items):
            high, low = split(tones_first[:, item, :])
            if folded:
                high = high.astype(F32)
                joined = jnp.concatenate([high, high, low.astype(F32)], 0)
                parts = [joined.T[:rows].astype(BF16)]
            else:
                parts = [high.astype(F32).T[:rows].astype(BF16), low.astype(F32).T[:rows].astype(BF16)]
            for k, value in enumerate(parts):
                symbols_first[k, item * rows : (item + 1) * rows, :] = value
        if folded:
            result = dot(symbols_first[0], table[0], (1, 0))
        else:
            result = dot3((symbols_first[0], symbols_first[1]), (table[0], table[1]), (1, 0))
        for item in range(items):
            for part in range(2):
                value = result[item * rows : (item + 1) * rows, part * length : (part + 1) * length]
                if not first:
                    value = value + total[item, part, slot * rows : (slot + 1) * rows, :]
                out[item, part, slot * rows : (slot + 1) * rows, :] = jnp.tanh(value) if last else value


def despread(pieces, starts, groups, half, blocks, rows, source, total, last, after):
    items = pieces[0].shape[1]
    length = groups * 2 * half
    lanes = -(-rows // 128) * 128
    sizes = [piece.shape[2] // (4 * rows) for piece in pieces]
    local = np.concatenate([np.arange(begin, begin + size) for begin, size in zip(starts, sizes)])
    index = (np.arange(groups * 2)[:, None] * half + local[None, :]).reshape(-1)
    angle = 2.0 * np.pi / length * (index[:, None] * np.arange(length)[None, :] % length)
    cosine, sine = np.cos(angle) / np.sqrt(length), np.sin(angle) / np.sqrt(length)
    real, imag = np.concatenate([cosine, sine], 1), np.concatenate([-sine, cosine], 1)
    table = np.stack([real, imag], 1).reshape(2 * len(index), 2 * length)
    high = table.astype(ml_dtypes.bfloat16)
    low = (table - high.astype(np.float64)).astype(ml_dtypes.bfloat16)
    depth = len(table)
    folded = 3 * depth <= 256
    table = np.concatenate([high, low, high])[None] if folded else np.stack([high, low])
    block_spec = pl.BlockSpec((items, 2, 2 * rows, length), lambda i, s: (0, 0, i, 0))
    totals = [] if total is None else [total]
    return pl.pallas_call(
        functools.partial(despread_body, groups, sizes, rows, folded, total is None, last),
        out_shape=jax.ShapeDtypeStruct((items, 2, blocks * rows, length), F32),
        grid_spec=pltpu.PrefetchScalarGridSpec(
            num_scalar_prefetch=1,
            grid=(blocks // 2,),
            in_specs=[pl.BlockSpec(table.shape, lambda i, s: (0, 0, 0))]
            + [pl.BlockSpec(piece.shape, lambda i, s: (0, 0, 0)) for piece in pieces]
            + [block_spec] * len(totals)
            + [ANY] * len(after),
            out_specs=block_spec,
            scratch_shapes=[
                pltpu.VMEM((depth, items, lanes), F32),
                pltpu.VMEM((table.shape[0], items * rows, table.shape[1]), BF16),
            ],
        ),
        compiler_params=pltpu.CompilerParams(vmem_limit_bytes=VMEM_LIMIT),
        cost_estimate=pl.CostEstimate(
            flops=2 * 6 * items * blocks * rows * depth * length,
            bytes_accessed=16 * items * blocks * rows * length,
            transcendentals=2 * items * blocks * rows * length,
        ),
        name="despread",
    )(source, jnp.asarray(table), *pieces, *totals, *after)


def on_device(channel, received, step_sizes, hop_offset, user_order):
    blocks = lax.axis_size("blk")
    groups = lax.axis_size("tones")
    pairs = blocks // 2
    half = channel.shape[0] // 2
    users = channel.shape[2]
    rows = received.shape[2] // blocks
    owners = blocks * groups
    position = lax.axis_index("blk")
    offset = hop_offset[lax.axis_index("tones")]
    side = position % 2
    pair = position // 2

    swap = [(p, p ^ 1) for p in range(blocks)]
    onward = [(p, (p + 2) % blocks) for p in range(blocks)]

    sizes = [1] + [2] * ((half - 2) // 2) + [1]
    sizes += [1] * (half - sum(sizes))
    starts = [sum(sizes[:c]) for c in range(len(sizes))]
    chunks = len(sizes)

    scalars = [side]
    for r in range(pairs + 1):
        scalars += [(2 * (pair - r) - offset) % blocks, (2 * (pair - r) + 1 - offset) % blocks]
    scalars.append((offset + 0) % 2)
    scalars = jnp.stack(scalars).astype(jnp.int32)
    order = (user_order[:, None] == jnp.arange(users, dtype=jnp.int32)[None, :]).astype(BF16)

    begins = (jnp.arange(blocks, dtype=jnp.int32)[:, None] + hop_offset[None, :]) % blocks
    source = jnp.where(begins % 2 == 0, begins // 2 + pairs - 1, begins // 2) % pairs

    own, peer, odd, pieces = {}, {}, {}, []

    def ready_peer(c, after):
        start = ((1 - side) * half + starts[c]).astype(jnp.int32).reshape(1)
        carry = 8 if c == 0 else 0
        sent = prepare(channel, received, step_sizes, start, sizes[c], carry, after)
        peer[c] = lax.ppermute(sent, "blk", swap)
        return sent

    def ready_own(c, after):
        start = (side * half + starts[c]).astype(jnp.int32).reshape(1)
        own[c] = prepare(channel, received, step_sizes, start, sizes[c], 0, after)
        return own[c]

    def complete(c, after):
        even, moved = odd[c]
        done = finish(
            pairs, blocks, owners, scalars, rates, own[c], peer[c], even, moved, order, after
        )
        pieces.append(
            lax.all_to_all(done, ("blk", "tones"), split_axis=0, concat_axis=0, tiled=True)
        )
        return done

    def bring_together(begin, end, total, last, after):
        return despread(
            pieces[begin:end],
            starts[begin:end],
            groups,
            half,
            blocks,
            rows,
            source.reshape(-1),
            total,
            last,
            after,
        )

    before = ready_peer(0, [])
    if chunks > 1:
        before = ready_peer(1, [before])
    before = ready_own(0, [before])
    peer_rates = peer[0][0, users + 2 * received.shape[2], :2].reshape(1, 2)
    rates = jnp.where(
        side == 0,
        jnp.concatenate([step_sizes, peer_rates], 0),
        jnp.concatenate([peer_rates, step_sizes], 0),
    )
    early = max(chunks - 4, 0)
    total = None
    for c in range(chunks):
        before = chain(0, False, blocks, scalars, rates, own[c], peer[c], [], [before])
        both = lax.ppermute(before, "blk", onward)
        if c + 2 < chunks:
            before = ready_peer(c + 2, [before])
        if c > 0:
            before = complete(c - 1, [before])
        if c + 1 < chunks:
            before = ready_own(c + 1, [before])
        for r in range(1, pairs):
            done = chain(r, r == pairs - 1, blocks, scalars, rates, own[c], peer[c], [both], [before])
            if r < pairs - 1:
                both = lax.ppermute(done, "blk", onward)
                before = done
        even, moving = done
        odd[c] = (even, lax.ppermute(moving, "blk", onward))
        before = even
        if early and c == early + 1:
            total = bring_together(0, early, None, False, [before])
            before = total
    before = complete(chunks - 1, [before])
    if early < chunks - 1:
        total = bring_together(early, chunks - 1, total, False, [before])
    return bring_together(chunks - 1, chunks, total, True, [])


def solution(mesh):
    in_specs = (
        P("tones", None, None, "blk"),
        P("tones", None, None, "blk"),
        P("blk", None),
        P(),
        P(),
    )
    out_specs = P(("blk", "tones"), None, None, None)
    return jax.shard_map(
        on_device, mesh=mesh, in_specs=in_specs, out_specs=out_specs, check_vma=False
    )
```

```python
import functools

import jax
import jax.numpy as jnp
import ml_dtypes
import numpy as np
from jax import lax
from jax.experimental import pallas as pl
from jax.experimental.pallas import tpu as pltpu
from jax.sharding import PartitionSpec as P

F32 = jnp.float32
BF16 = jnp.bfloat16
VMEM_LIMIT = 56 * 1024 * 1024
HEAVY = pl.CostEstimate(flops=10**13, bytes_accessed=10**10, transcendentals=0)
ANY = pl.BlockSpec(memory_space=pl.ANY)
SMEM = pl.BlockSpec(memory_space=pltpu.SMEM)


def split(value):
    high = value.astype(BF16)
    return high, (value - high.astype(F32)).astype(BF16)


def dot(left, right, contract):
    return lax.dot_general(left, right, ((contract[:1], contract[1:]), ((), ())), preferred_element_type=F32)


def dot3(left, right, contract):
    left_high, left_low = left
    right_high, right_low = right
    return (
        dot(left_high, right_high, contract)
        + dot(left_high, right_low, contract)
        + dot(left_low, right_high, contract)
    )


def triangle(users):
    row = lax.broadcasted_iota(jnp.int32, (users, users), 0)
    column = lax.broadcasted_iota(jnp.int32, (users, users), 1)
    return row, column


def prepare_body(carry, start, rates, chan, recv, *refs):
    out = refs[-1]
    users = chan.shape[2]
    symbols = recv.shape[2]
    left_real = split(jnp.concatenate([chan[0, 0], recv[0, 0]], 0))
    left_imag = split(jnp.concatenate([chan[0, 1], recv[0, 1]], 0))
    right = tuple(
        jnp.concatenate([real[:users], imag[:users]], 1) for real, imag in zip(left_real, left_imag)
    )
    real = dot3(tuple(jnp.concatenate(pair, 1) for pair in zip(left_real, left_imag)), right, (1, 1))
    imag = dot3(
        tuple(jnp.concatenate([b, -a], 1) for a, b in zip(left_real, left_imag)), right, (1, 1)
    )
    row, column = triangle(users)
    out[0, :users] = jnp.where(row <= column, real[:users], imag[:users])
    rows = users + 2 * symbols
    out[0, users : users + symbols] = real[users:]
    out[0, users + symbols : rows] = imag[users:]
    if carry:
        lane = lax.broadcasted_iota(jnp.int32, (carry, users), 1)
        out[0, rows:] = jnp.where(lane == 0, rates[0, 0], rates[0, 1])


def prepare(channel, received, step_sizes, start, count, carry, after):
    _, _, users, width = channel.shape
    symbols = received.shape[2]
    rows = users + 2 * symbols + carry
    return pl.pallas_call(
        functools.partial(prepare_body, carry),
        out_shape=jax.ShapeDtypeStruct((count, rows, users), F32),
        grid_spec=pltpu.PrefetchScalarGridSpec(
            num_scalar_prefetch=1,
            grid=(count,),
            in_specs=[
                SMEM,
                pl.BlockSpec((1, 2, users, width), lambda i, start: (start[0] + i, 0, 0, 0)),
                pl.BlockSpec((1, 2, symbols, width), lambda i, start: (start[0] + i, 0, 0, 0)),
            ]
            + [ANY] * len(after),
            out_specs=pl.BlockSpec((1, rows, users), lambda i, start: (i, 0, 0)),
        ),
        compiler_params=pltpu.CompilerParams(vmem_limit_bytes=VMEM_LIMIT),
        cost_estimate=HEAVY,
        name="prepare",
    )(start, step_sizes, channel, received, *after)


def unpack(packed, gram, sub):
    users = packed.shape[0]
    row, column = triangle(users)
    turned = packed.T
    real = split(jnp.where(row <= column, packed, turned))
    imag = split(jnp.where(row > column, packed, jnp.where(row < column, -turned, 0.0)))
    for part in range(2):
        gram[sub, part, :users, :users] = real[part]
        gram[sub, part, :users, users:] = imag[part]
        gram[sub, part, users:, :users] = -imag[part]
        gram[sub, part, users:, users:] = real[part]


def step(estimate, matched, gram, sub, rate):
    product = dot3(split(estimate), (gram[sub, 0], gram[sub, 1]), (1, 0))
    return jnp.tanh(estimate + rate * (matched - product))


def filtered(ref, users, symbols, rows, block):
    parts = []
    for part in range(2):
        first = pl.multiple_of(users + part * symbols + block * rows, 8)
        parts.append(ref[0, pl.ds(first, rows), :])
    return jnp.concatenate(parts, 1)


def chain_body(round_index, kind, symbols, scalars, rates, own, peer, *refs):
    users = own.shape[2]
    rows = symbols // kind["blocks"]
    side = scalars[0]
    even_block = scalars[1 + 2 * round_index]
    odd_block = scalars[2 + 2 * round_index]
    gram, matched = refs[-2:]
    for ref, sub in ((own, side), (peer, 1 - side)):
        unpack(ref[0, :users], gram, sub)
        for slot, block in enumerate((even_block, odd_block)):
            matched[sub, slot * rows : (slot + 1) * rows] = filtered(ref, users, symbols, rows, block)

    if round_index == 0:
        out = refs[-3:-2]
        even = jnp.tanh(rates[0, 0] * matched[0, :rows])
        even = step(even, matched[0, :rows], gram, 0, rates[0, 1])
        even = step(even, matched[1, :rows], gram, 1, rates[1, 0])
        odd = jnp.tanh(rates[1, 0] * matched[1, rows:])
        both = step(jnp.concatenate([even, odd], 0), matched[1], gram, 1, rates[1, 1])
    else:
        out = refs[-4:-2] if kind["last"] else refs[-3:-2]
        came = refs[0]
        both = jnp.concatenate(
            [jnp.concatenate([came[0, slot, 0], came[0, slot, 1]], 1) for slot in range(2)], 0
        )
        for sub in range(2):
            for substep in range(2):
                both = step(both, matched[sub], gram, sub, rates[sub, substep])
    for slot in range(2):
        for part in range(2):
            piece = both[slot * rows : (slot + 1) * rows, part * users : (part + 1) * users]
            if len(out) == 2:
                out[slot][0, part] = piece
            else:
                out[0][0, slot, part] = piece


def chain(round_index, last, blocks, scalars, rates, own, peer, came, after):
    count, packed_rows, users = own.shape
    symbols = (packed_rows - users) // 2
    rows = symbols // blocks
    packed_spec = pl.BlockSpec((1, packed_rows, users), lambda i, s: (i, 0, 0))
    both_spec = pl.BlockSpec((1, 2, 2, rows, users), lambda i, s: (i, 0, 0, 0, 0))
    one_spec = pl.BlockSpec((1, 2, rows, users), lambda i, s: (i, 0, 0, 0))
    both_shape = jax.ShapeDtypeStruct((count, 2, 2, rows, users), F32)
    one_shape = jax.ShapeDtypeStruct((count, 2, rows, users), F32)
    return pl.pallas_call(
        functools.partial(chain_body, round_index, {"blocks": blocks, "last": last}, symbols),
        out_shape=[one_shape, one_shape] if last else both_shape,
        grid_spec=pltpu.PrefetchScalarGridSpec(
            num_scalar_prefetch=1,
            grid=(count,),
            in_specs=[SMEM, packed_spec, packed_spec] + [both_spec] * len(came) + [ANY] * len(after),
            out_specs=[one_spec, one_spec] if last else both_spec,
            scratch_shapes=[
                pltpu.VMEM((2, 2, 2 * users, 2 * users), BF16),
                pltpu.VMEM((2, 2 * rows, 2 * users), F32),
            ],
        ),
        compiler_params=pltpu.CompilerParams(vmem_limit_bytes=VMEM_LIMIT),
        cost_estimate=HEAVY,
        name="chain%d" % round_index,
    )(scalars, rates, own, peer, *came, *after)


def finish_body(round_index, count, rows, symbols, scalars, rates, own, peer, even, odd, order, *refs):
    users = own.shape[2]
    out, gram, gathered = refs[-3:]
    tone = pl.program_id(0)
    side = scalars[0]
    block = scalars[2 + 2 * round_index]
    even_slot = scalars[1 + 2 * (round_index + 1)]

    @pl.when(side == 0)
    def _():
        unpack(own[0, :users], gram, 0)

    @pl.when(side != 0)
    def _():
        unpack(peer[0, :users], gram, 0)

    matched = jnp.where(
        side == 0,
        filtered(own, users, symbols, rows, block),
        filtered(peer, users, symbols, rows, block),
    )
    estimate = jnp.concatenate([odd[0, 0], odd[0, 1]], 1)
    for substep in range(2):
        estimate = step(estimate, matched, gram, 0, rates[0, substep])
    for part in range(2):
        first = (tone * 2 + part) * 2
        odd_row = pl.multiple_of((first + 1 - even_slot) * rows, 8)
        even_row = pl.multiple_of((first + even_slot) * rows, 8)
        gathered[pl.ds(odd_row, rows), :] = estimate[:, part * users : (part + 1) * users]
        gathered[pl.ds(even_row, rows), :] = even[0, part]

    @pl.when(tone == count - 1)
    def _():
        high, low = split(gathered[...])
        turned = dot(order[...], high, (1, 1)) + dot(order[...], low, (1, 1))
        out[...] = turned.reshape(out.shape)


def finish(round_index, blocks, owners, scalars, rates, own, peer, even, odd, order, after):
    count, packed_rows, users = own.shape
    symbols = (packed_rows - users) // 2
    rows = symbols // blocks
    packed_spec = pl.BlockSpec((1, packed_rows, users), lambda i, s: (i, 0, 0))
    one_spec = pl.BlockSpec((1, 2, rows, users), lambda i, s: (i, 0, 0, 0))
    shape = (owners, users // owners, count * 4 * rows)
    return pl.pallas_call(
        functools.partial(finish_body, round_index, count, rows, symbols),
        out_shape=jax.ShapeDtypeStruct(shape, F32),
        grid_spec=pltpu.PrefetchScalarGridSpec(
            num_scalar_prefetch=1,
            grid=(count,),
            in_specs=[
                SMEM,
                packed_spec,
                packed_spec,
                one_spec,
                one_spec,
                pl.BlockSpec((users, users), lambda i, s: (0, 0)),
            ]
            + [ANY] * len(after),
            out_specs=pl.BlockSpec(shape, lambda i, s: (0, 0, 0)),
            scratch_shapes=[
                pltpu.VMEM((1, 2, 2 * users, 2 * users), BF16),
                pltpu.VMEM((count * 4 * rows, users), F32),
            ],
        ),
        compiler_params=pltpu.CompilerParams(vmem_limit_bytes=VMEM_LIMIT),
        cost_estimate=HEAVY,
        name="finish",
    )(scalars, rates, own, peer, even, odd, order, *after)


def despread_body(groups, sizes, rows, folded, first, last, source, table, *refs):
    pieces = refs[: len(sizes)]
    if not first:
        total = refs[len(sizes)]
    out, tones_first, symbols_first = refs[-3:]
    items = out.shape[0]
    length = out.shape[3]
    tones = sum(sizes)
    pair = pl.program_id(0)
    for slot in range(2):
        block = 2 * pair + slot

        def gather(group, carry):
            position = source[block * groups + group]
            for side in range(2):
                place = (group * 2 + side) * tones * 2
                src = (2 * position + side) * groups + group
                for piece, size in zip(pieces, sizes):
                    for tone in range(2 * size):
                        lane = (tone * 2 + slot) * rows
                        tones_first[place + tone, :, :rows] = piece[src, :, lane : lane + rows]
                    place = place + 2 * size
            return carry

        lax.fori_loop(0, groups, gather, 0)
        for item in range(items):
            high, low = split(tones_first[:, item, :].T[:rows])
            here = slice(item * rows, (item + 1) * rows)
            if folded:
                depth = high.shape[1]
                for k, value in enumerate((high, high, low)):
                    symbols_first[0, here, k * depth : (k + 1) * depth] = value
            else:
                symbols_first[0, here] = high
                symbols_first[1, here] = low
        if folded:
            result = dot(symbols_first[0], table[0], (1, 0))
        else:
            result = dot3((symbols_first[0], symbols_first[1]), (table[0], table[1]), (1, 0))
        for item in range(items):
            for part in range(2):
                value = result[item * rows : (item + 1) * rows, part * length : (part + 1) * length]
                if not first:
                    value = value + total[item, part, slot * rows : (slot + 1) * rows, :]
                out[item, part, slot * rows : (slot + 1) * rows, :] = jnp.tanh(value) if last else value


def despread(pieces, starts, groups, half, blocks, rows, source, total, last, after):
    items = pieces[0].shape[1]
    length = groups * 2 * half
    lanes = -(-rows // 128) * 128
    sizes = [piece.shape[2] // (4 * rows) for piece in pieces]
    local = np.concatenate([np.arange(begin, begin + size) for begin, size in zip(starts, sizes)])
    index = (np.arange(groups * 2)[:, None] * half + local[None, :]).reshape(-1)
    angle = 2.0 * np.pi / length * (index[:, None] * np.arange(length)[None, :] % length)
    cosine, sine = np.cos(angle) / np.sqrt(length), np.sin(angle) / np.sqrt(length)
    real, imag = np.concatenate([cosine, sine], 1), np.concatenate([-sine, cosine], 1)
    table = np.stack([real, imag], 1).reshape(2 * len(index), 2 * length)
    high = table.astype(ml_dtypes.bfloat16)
    low = (table - high.astype(np.float64)).astype(ml_dtypes.bfloat16)
    depth = len(table)
    folded = 3 * depth <= 256
    table = np.concatenate([high, low, high])[None] if folded else np.stack([high, low])
    block_spec = pl.BlockSpec((items, 2, 2 * rows, length), lambda i, s: (0, 0, i, 0))
    totals = [] if total is None else [total]
    return pl.pallas_call(
        functools.partial(despread_body, groups, sizes, rows, folded, total is None, last),
        out_shape=jax.ShapeDtypeStruct((items, 2, blocks * rows, length), F32),
        grid_spec=pltpu.PrefetchScalarGridSpec(
            num_scalar_prefetch=1,
            grid=(blocks // 2,),
            in_specs=[pl.BlockSpec(table.shape, lambda i, s: (0, 0, 0))]
            + [pl.BlockSpec(piece.shape, lambda i, s: (0, 0, 0)) for piece in pieces]
            + [block_spec] * len(totals)
            + [ANY] * len(after),
            out_specs=block_spec,
            scratch_shapes=[
                pltpu.VMEM((depth, items, lanes), F32),
                pltpu.VMEM((table.shape[0], items * rows, table.shape[1]), BF16),
            ],
        ),
        compiler_params=pltpu.CompilerParams(vmem_limit_bytes=VMEM_LIMIT),
        cost_estimate=HEAVY,
        name="despread",
    )(source, jnp.asarray(table), *pieces, *totals, *after)


def on_device(channel, received, step_sizes, hop_offset, user_order):
    blocks = lax.axis_size("blk")
    groups = lax.axis_size("tones")
    pairs = blocks // 2
    half = channel.shape[0] // 2
    users = channel.shape[2]
    rows = received.shape[2] // blocks
    owners = blocks * groups
    position = lax.axis_index("blk")
    offset = hop_offset[lax.axis_index("tones")]
    side = position % 2
    pair = position // 2

    swap = [(p, p ^ 1) for p in range(blocks)]
    onward = [(p, (p + 2) % blocks) for p in range(blocks)]

    sizes = [1] + [2] * ((half - 2) // 2) + [1]
    sizes += [1] * (half - sum(sizes))
    starts = [sum(sizes[:c]) for c in range(len(sizes))]
    chunks = len(sizes)

    scalars = [side]
    for r in range(pairs + 1):
        scalars += [(2 * (pair - r) - offset) % blocks, (2 * (pair - r) + 1 - offset) % blocks]
    scalars.append((offset + 0) % 2)
    scalars = jnp.stack(scalars).astype(jnp.int32)
    order = (user_order[:, None] == jnp.arange(users, dtype=jnp.int32)[None, :]).astype(BF16)

    begins = (jnp.arange(blocks, dtype=jnp.int32)[:, None] + hop_offset[None, :]) % blocks
    source = jnp.where(begins % 2 == 0, begins // 2 + pairs - 1, begins // 2) % pairs

    own, peer, odd, pieces = {}, {}, {}, []

    def ready_peer(c, after):
        start = ((1 - side) * half + starts[c]).astype(jnp.int32).reshape(1)
        carry = 8 if c == 0 else 0
        sent = prepare(channel, received, step_sizes, start, sizes[c], carry, after)
        peer[c] = lax.ppermute(sent, "blk", swap)
        return sent

    def ready_own(c, after):
        start = (side * half + starts[c]).astype(jnp.int32).reshape(1)
        own[c] = prepare(channel, received, step_sizes, start, sizes[c], 0, after)
        return own[c]

    def complete(c, after):
        even, moved = odd[c]
        done = finish(
            pairs, blocks, owners, scalars, rates, own[c], peer[c], even, moved, order, after
        )
        pieces.append(
            lax.all_to_all(done, ("blk", "tones"), split_axis=0, concat_axis=0, tiled=True)
        )
        return done

    def bring_together(begin, end, total, last, after):
        return despread(
            pieces[begin:end],
            starts[begin:end],
            groups,
            half,
            blocks,
            rows,
            source.reshape(-1),
            total,
            last,
            after,
        )

    before = ready_peer(0, [])
    if chunks > 1:
        before = ready_peer(1, [before])
    before = ready_own(0, [before])
    peer_rates = peer[0][0, users + 2 * received.shape[2], :2].reshape(1, 2)
    rates = jnp.where(
        side == 0,
        jnp.concatenate([step_sizes, peer_rates], 0),
        jnp.concatenate([peer_rates, step_sizes], 0),
    )
    early = max(chunks - 4, 0)
    total = None
    for c in range(chunks):
        after = [before] + pieces[max(c - 2, 0) : c - 1]
        before = chain(0, False, blocks, scalars, rates, own[c], peer[c], [], after)
        both = lax.ppermute(before, "blk", onward)
        if c + 2 < chunks:
            before = ready_peer(c + 2, [before])
        if c > 0:
            before = complete(c - 1, [before])
        if c + 1 < chunks:
            before = ready_own(c + 1, [before])
        for r in range(1, pairs):
            done = chain(r, r == pairs - 1, blocks, scalars, rates, own[c], peer[c], [both], [before])
            if r < pairs - 1:
                both = lax.ppermute(done, "blk", onward)
                before = done
        even, moving = done
        odd[c] = (even, lax.ppermute(moving, "blk", onward))
        before = even
        if early and c == early + 1:
            total = bring_together(0, early, None, False, [before])
            before = total
    before = complete(chunks - 1, [before] + pieces[-1:])
    if early < chunks - 1:
        total = bring_together(early, chunks - 1, total, False, [before])
    return bring_together(chunks - 1, chunks, total, True, [])


def solution(mesh):
    in_specs = (
        P("tones", None, None, "blk"),
        P("tones", None, None, "blk"),
        P("blk", None),
        P(),
        P(),
    )
    out_specs = P(("blk", "tones"), None, None, None)
    return jax.shard_map(
        on_device, mesh=mesh, in_specs=in_specs, out_specs=out_specs, check_vma=False
    )
```

```python
import functools

import jax
import jax.numpy as jnp
import ml_dtypes
import numpy as np
from jax import lax
from jax.experimental import pallas as pl
from jax.experimental.pallas import tpu as pltpu
from jax.sharding import PartitionSpec as P

F32 = jnp.float32
BF16 = jnp.bfloat16
VMEM_LIMIT = 56 * 1024 * 1024
HEAVY = pl.CostEstimate(flops=10**13, bytes_accessed=10**10, transcendentals=0)
ANY = pl.BlockSpec(memory_space=pl.ANY)
SMEM = pl.BlockSpec(memory_space=pltpu.SMEM)


def split(value):
    high = value.astype(BF16)
    return high, (value - high.astype(F32)).astype(BF16)


def dot(left, right, contract):
    return lax.dot_general(left, right, ((contract[:1], contract[1:]), ((), ())), preferred_element_type=F32)


def dot3(left, right, contract):
    left_high, left_low = left
    right_high, right_low = right
    return (
        dot(left_high, right_high, contract)
        + dot(left_high, right_low, contract)
        + dot(left_low, right_high, contract)
    )


def triangle(users):
    row = lax.broadcasted_iota(jnp.int32, (users, users), 0)
    column = lax.broadcasted_iota(jnp.int32, (users, users), 1)
    return row, column


def prepare_body(carry, blocks, scalars, rates, chan, recv, *refs):
    outs = refs[len(refs) - blocks // 2 :]
    users = chan.shape[2]
    rows = recv.shape[2] // blocks

    def stacked(part):
        pieces = [chan[0, part]]
        for place in range(blocks):
            first = pl.multiple_of(scalars[1 + place] * rows, 8)
            pieces.append(recv[0, part, pl.ds(first, rows), :])
        return split(jnp.concatenate(pieces, 0))

    left_real = stacked(0)
    left_imag = stacked(1)
    right = tuple(
        jnp.concatenate([real[:users], imag[:users]], 1) for real, imag in zip(left_real, left_imag)
    )
    real = dot3(tuple(jnp.concatenate(pair, 1) for pair in zip(left_real, left_imag)), right, (1, 1))
    imag = dot3(
        tuple(jnp.concatenate([b, -a], 1) for a, b in zip(left_real, left_imag)), right, (1, 1)
    )
    row, column = triangle(users)
    outs[0][0, :users] = jnp.where(row <= column, real[:users], imag[:users])
    for place in range(blocks):
        base = users if place < 2 else 0
        first = users + place * rows
        for part, value in enumerate((real, imag)):
            to = base + (2 * (place % 2) + part) * rows
            outs[place // 2][0, to : to + rows] = value[first : first + rows]
    if carry:
        lane = lax.broadcasted_iota(jnp.int32, (carry, users), 1)
        outs[0][0, users + 4 * rows :] = jnp.where(lane == 0, rates[0, 0], rates[0, 1])


def prepare(channel, received, step_sizes, scalars, count, blocks, carry, after):
    _, _, users, width = channel.shape
    symbols = received.shape[2]
    rows = symbols // blocks
    heights = [users + 4 * rows + carry] + [4 * rows] * (blocks // 2 - 1)
    return pl.pallas_call(
        functools.partial(prepare_body, carry, blocks),
        out_shape=[jax.ShapeDtypeStruct((count, height, users), F32) for height in heights],
        grid_spec=pltpu.PrefetchScalarGridSpec(
            num_scalar_prefetch=1,
            grid=(count,),
            in_specs=[
                SMEM,
                pl.BlockSpec((1, 2, users, width), lambda i, s: (s[0] + i, 0, 0, 0)),
                pl.BlockSpec((1, 2, symbols, width), lambda i, s: (s[0] + i, 0, 0, 0)),
            ]
            + [ANY] * len(after),
            out_specs=[pl.BlockSpec((1, height, users), lambda i, s: (i, 0, 0)) for height in heights],
        ),
        compiler_params=pltpu.CompilerParams(vmem_limit_bytes=VMEM_LIMIT),
        cost_estimate=HEAVY,
        name="prepare",
    )(scalars, step_sizes, channel, received, *after)


def unpack(packed, gram, sub):
    users = packed.shape[0]
    row, column = triangle(users)
    turned = packed.T
    real = split(jnp.where(row <= column, packed, turned))
    imag = split(jnp.where(row > column, packed, jnp.where(row < column, -turned, 0.0)))
    for part in range(2):
        gram[sub, part, :users, :users] = real[part]
        gram[sub, part, :users, users:] = imag[part]
        gram[sub, part, users:, :users] = -imag[part]
        gram[sub, part, users:, users:] = real[part]


def step(estimate, matched, gram, sub, rate):
    product = dot3(split(estimate), (gram[sub, 0], gram[sub, 1]), (1, 0))
    return jnp.tanh(estimate + rate * (matched - product))


def filtered(ref, base, rows, slot):
    first = base + 2 * slot * rows
    return jnp.concatenate([ref[0, first : first + rows], ref[0, first + rows : first + 2 * rows]], 1)


def chain_body(round_index, last, rows, side, rates, *refs):
    own, peer = refs[:2]
    users = own.shape[2]
    rest = refs[2:]
    base = users
    grams = (own, peer)
    if round_index:
        own, peer, came = rest[:3]
        base = 0
    gram, matched = refs[-2:]
    for packed, samples, sub in ((grams[0], own, side[0]), (grams[1], peer, 1 - side[0])):
        unpack(packed[0, :users], gram, sub)
        for slot in range(2):
            matched[sub, slot * rows : (slot + 1) * rows] = filtered(samples, base, rows, slot)

    if round_index == 0:
        even = jnp.tanh(rates[0, 0] * matched[0, :rows])
        even = step(even, matched[0, :rows], gram, 0, rates[0, 1])
        even = step(even, matched[1, :rows], gram, 1, rates[1, 0])
        odd = jnp.tanh(rates[1, 0] * matched[1, rows:])
        both = step(jnp.concatenate([even, odd], 0), matched[1], gram, 1, rates[1, 1])
    else:
        both = jnp.concatenate(
            [jnp.concatenate([came[0, slot, 0], came[0, slot, 1]], 1) for slot in range(2)], 0
        )
        for sub in range(2):
            for substep in range(2):
                both = step(both, matched[sub], gram, sub, rates[sub, substep])
    out = refs[-4:-2] if last else refs[-3:-2]
    for slot in range(2):
        for part in range(2):
            piece = both[slot * rows : (slot + 1) * rows, part * users : (part + 1) * users]
            if last:
                out[slot][0, part] = piece
            else:
                out[0][0, slot, part] = piece


def chain(round_index, last, rows, side, rates, own, peer, came, after):
    count, _, users = own[0].shape
    both_spec = pl.BlockSpec((1, 2, 2, rows, users), lambda i, s: (i, 0, 0, 0, 0))
    one_spec = pl.BlockSpec((1, 2, rows, users), lambda i, s: (i, 0, 0, 0))
    both_shape = jax.ShapeDtypeStruct((count, 2, 2, rows, users), F32)
    one_shape = jax.ShapeDtypeStruct((count, 2, rows, users), F32)
    inputs = [own[0], peer[0]]
    heights = [users if round_index else users + 4 * rows] * 2
    if round_index:
        inputs += [own[round_index], peer[round_index]]
        heights += [4 * rows] * 2
    specs = [pl.BlockSpec((1, height, users), lambda i, s: (i, 0, 0)) for height in heights]
    return pl.pallas_call(
        functools.partial(chain_body, round_index, last, rows),
        out_shape=[one_shape, one_shape] if last else both_shape,
        grid_spec=pltpu.PrefetchScalarGridSpec(
            num_scalar_prefetch=1,
            grid=(count,),
            in_specs=[SMEM] + specs + [both_spec] * len(came) + [ANY] * len(after),
            out_specs=[one_spec, one_spec] if last else both_spec,
            scratch_shapes=[
                pltpu.VMEM((2, 2, 2 * users, 2 * users), BF16),
                pltpu.VMEM((2, 2 * rows, 2 * users), F32),
            ],
        ),
        compiler_params=pltpu.CompilerParams(vmem_limit_bytes=VMEM_LIMIT),
        cost_estimate=HEAVY,
        name="chain%d" % round_index,
    )(side, rates, *inputs, *came, *after)


def finish_body(count, rows, scalars, rates, own, peer, even, odd, order, *refs):
    users = own.shape[2]
    out, gram, gathered = refs[-3:]
    tone = pl.program_id(0)
    side = scalars[0]
    even_slot = scalars[1]

    @pl.when(side == 0)
    def _():
        unpack(own[0, :users], gram, 0)

    @pl.when(side != 0)
    def _():
        unpack(peer[0, :users], gram, 0)

    matched = jnp.where(side == 0, filtered(own, users, rows, 1), filtered(peer, users, rows, 1))
    estimate = jnp.concatenate([odd[0, 0], odd[0, 1]], 1)
    for substep in range(2):
        estimate = step(estimate, matched, gram, 0, rates[0, substep])
    for part in range(2):
        first = (tone * 2 + part) * 2
        odd_row = pl.multiple_of((first + 1 - even_slot) * rows, 8)
        even_row = pl.multiple_of((first + even_slot) * rows, 8)
        gathered[pl.ds(odd_row, rows), :] = estimate[:, part * users : (part + 1) * users]
        gathered[pl.ds(even_row, rows), :] = even[0, part]

    @pl.when(tone == count - 1)
    def _():
        high, low = split(gathered[...])
        turned = dot(order[...], high, (1, 1)) + dot(order[...], low, (1, 1))
        out[...] = turned.reshape(out.shape)


def finish(rows, owners, scalars, rates, own, peer, even, odd, order, after):
    count, _, users = own[0].shape
    packed_spec = pl.BlockSpec((1, users + 4 * rows, users), lambda i, s: (i, 0, 0))
    one_spec = pl.BlockSpec((1, 2, rows, users), lambda i, s: (i, 0, 0, 0))
    shape = (owners, users // owners, count * 4 * rows)
    return pl.pallas_call(
        functools.partial(finish_body, count, rows),
        out_shape=jax.ShapeDtypeStruct(shape, F32),
        grid_spec=pltpu.PrefetchScalarGridSpec(
            num_scalar_prefetch=1,
            grid=(count,),
            in_specs=[
                SMEM,
                packed_spec,
                packed_spec,
                one_spec,
                one_spec,
                pl.BlockSpec((users, users), lambda i, s: (0, 0)),
            ]
            + [ANY] * len(after),
            out_specs=pl.BlockSpec(shape, lambda i, s: (0, 0, 0)),
            scratch_shapes=[
                pltpu.VMEM((1, 2, 2 * users, 2 * users), BF16),
                pltpu.VMEM((count * 4 * rows, users), F32),
            ],
        ),
        compiler_params=pltpu.CompilerParams(vmem_limit_bytes=VMEM_LIMIT),
        cost_estimate=HEAVY,
        name="finish",
    )(scalars, rates, own[0], peer[0], even, odd, order, *after)


def despread_body(groups, sizes, rows, folded, first, last, source, table, *refs):
    pieces = refs[: len(sizes)]
    if not first:
        total = refs[len(sizes)]
    out, tones_first, symbols_first = refs[-3:]
    items = out.shape[0]
    tones = sum(sizes)
    depth = tones_first.shape[0]
    pair = pl.program_id(0)
    part = pl.program_id(1)

    def turn(slot):
        block = 2 * pair + slot

        def gather(group, carry):
            position = source[block * groups + group]
            for side in range(2):
                place = (group * 2 + side) * tones * 2
                src = (2 * position + side) * groups + group
                for piece, size in zip(pieces, sizes):
                    for tone in range(2 * size):
                        lane = (tone * 2 + slot) * rows
                        tones_first[place + tone, :, :rows] = piece[src, :, lane : lane + rows]
                    place = place + 2 * size
            return carry

        lax.fori_loop(0, groups, gather, 0)
        for item in range(items):
            high, low = split(tones_first[:, item, :].T[:rows])
            here = slice((slot * items + item) * rows, (slot * items + item + 1) * rows)
            if folded:
                for k, value in enumerate((high, high, low)):
                    symbols_first[0, here, k * depth : (k + 1) * depth] = value
            else:
                symbols_first[0, here] = high
                symbols_first[1, here] = low

    @pl.when(part == 0)
    def _():
        for slot in range(2):
            turn(slot)

    if folded:
        result = dot(symbols_first[0], table[part, 0], (1, 0))
    else:
        result = dot3((symbols_first[0], symbols_first[1]), (table[part, 0], table[part, 1]), (1, 0))
    for slot in range(2):
        for item in range(items):
            value = result[(slot * items + item) * rows : (slot * items + item + 1) * rows]
            if not first:
                value = value + total[item, 0, slot * rows : (slot + 1) * rows, :]
            out[item, 0, slot * rows : (slot + 1) * rows, :] = jnp.tanh(value) if last else value


def despread(pieces, starts, groups, half, blocks, rows, source, total, last, after):
    items = pieces[0].shape[1]
    length = groups * 2 * half
    lanes = -(-rows // 128) * 128
    sizes = [piece.shape[2] // (4 * rows) for piece in pieces]
    local = np.concatenate([np.arange(begin, begin + size) for begin, size in zip(starts, sizes)])
    index = (np.arange(groups * 2)[:, None] * half + local[None, :]).reshape(-1)
    angle = 2.0 * np.pi / length * (index[:, None] * np.arange(length)[None, :] % length)
    cosine, sine = np.cos(angle) / np.sqrt(length), np.sin(angle) / np.sqrt(length)
    table = np.stack([np.stack([cosine, -sine], 1), np.stack([sine, cosine], 1)])
    table = table.reshape(2, 1, 2 * len(index), length)
    high = table.astype(ml_dtypes.bfloat16)
    low = (table - high.astype(np.float64)).astype(ml_dtypes.bfloat16)
    depth = table.shape[2]
    folded = 3 * depth <= 256
    table = np.concatenate([high, low, high], 2) if folded else np.concatenate([high, low], 1)
    block_spec = pl.BlockSpec((items, 1, 2 * rows, length), lambda i, part, s: (0, part, i, 0))
    totals = [] if total is None else [total]
    return pl.pallas_call(
        functools.partial(despread_body, groups, sizes, rows, folded, total is None, last),
        out_shape=jax.ShapeDtypeStruct((items, 2, blocks * rows, length), F32),
        grid_spec=pltpu.PrefetchScalarGridSpec(
            num_scalar_prefetch=1,
            grid=(blocks // 2, 2),
            in_specs=[pl.BlockSpec(table.shape, lambda i, part, s: (0, 0, 0, 0))]
            + [pl.BlockSpec(piece.shape, lambda i, part, s: (0, 0, 0)) for piece in pieces]
            + [block_spec] * len(totals)
            + [ANY] * len(after),
            out_specs=block_spec,
            scratch_shapes=[
                pltpu.VMEM((depth, items, lanes), F32),
                pltpu.VMEM((table.shape[1], 2 * items * rows, table.shape[2]), BF16),
            ],
        ),
        compiler_params=pltpu.CompilerParams(vmem_limit_bytes=VMEM_LIMIT),
        cost_estimate=HEAVY,
        name="despread",
    )(source, jnp.asarray(table), *pieces, *totals, *after)


def on_device(channel, received, step_sizes, hop_offset, user_order):
    blocks = lax.axis_size("blk")
    groups = lax.axis_size("tones")
    pairs = blocks // 2
    half = channel.shape[0] // 2
    users = channel.shape[2]
    rows = received.shape[2] // blocks
    owners = blocks * groups
    position = lax.axis_index("blk")
    offset = hop_offset[lax.axis_index("tones")]
    side = position % 2
    pair = position // 2

    swap = [(p, p ^ 1) for p in range(blocks)]
    onward = [(p, (p + 2) % blocks) for p in range(blocks)]

    sizes = [1] + [2] * ((half - 2) // 2) + [1]
    sizes += [1] * (half - sum(sizes))
    starts = [sum(sizes[:c]) for c in range(len(sizes))]
    chunks = len(sizes)

    order_of_blocks = []
    for r in range(pairs):
        order_of_blocks += [(2 * (pair - r) - offset) % blocks, (2 * (pair - r) + 1 - offset) % blocks]
    side_alone = side.reshape(1)
    side_and_slot = jnp.stack([side, offset % 2])
    order = (user_order[:, None] == jnp.arange(users, dtype=jnp.int32)[None, :]).astype(BF16)

    begins = (jnp.arange(blocks, dtype=jnp.int32)[:, None] + hop_offset[None, :]) % blocks
    source = jnp.where(begins % 2 == 0, begins // 2 + pairs - 1, begins // 2) % pairs

    own, peer, odd, pieces = {}, {}, {}, []

    def ready(c, first_tone, carry, after):
        scalars = jnp.stack([first_tone + starts[c]] + order_of_blocks)
        return prepare(channel, received, step_sizes, scalars, sizes[c], blocks, carry, after)

    def ready_peer(c, after):
        sent = ready(c, (1 - side) * half, 8 if c == 0 else 0, after)
        peer[c] = [lax.ppermute(value, "blk", swap) for value in sent]
        return sent[0]

    def ready_own(c, after):
        own[c] = ready(c, side * half, 0, after)
        return own[c][0]

    def complete(c, after):
        even, moved = odd[c]
        done = finish(rows, owners, side_and_slot, rates, own[c], peer[c], even, moved, order, after)
        pieces.append(
            lax.all_to_all(done, ("blk", "tones"), split_axis=0, concat_axis=0, tiled=True)
        )
        return done

    def bring_together(begin, end, total, last, after):
        return despread(
            pieces[begin:end],
            starts[begin:end],
            groups,
            half,
            blocks,
            rows,
            source.reshape(-1),
            total,
            last,
            after,
        )

    before = ready_peer(0, [])
    if chunks > 1:
        before = ready_peer(1, [before])
    before = ready_own(0, [before])
    peer_rates = peer[0][0][0, users + 4 * rows, :2].reshape(1, 2)
    rates = jnp.where(
        side == 0,
        jnp.concatenate([step_sizes, peer_rates], 0),
        jnp.concatenate([peer_rates, step_sizes], 0),
    )
    early = max(chunks - 4, 0)
    total = None
    for c in range(chunks):
        before = chain(0, False, rows, side_alone, rates, own[c], peer[c], [], [before])
        both = lax.ppermute(before, "blk", onward)
        if c > 0:
            before = complete(c - 1, [before] + pieces[-1:])
        if c + 2 < chunks:
            before = ready_peer(c + 2, [before])
        if c + 1 < chunks:
            before = ready_own(c + 1, [before])
        for r in range(1, pairs):
            done = chain(r, r == pairs - 1, rows, side_alone, rates, own[c], peer[c], [both], [before])
            if r < pairs - 1:
                both = lax.ppermute(done, "blk", onward)
                before = done
        even, moving = done
        odd[c] = (even, lax.ppermute(moving, "blk", onward))
        before = even
        if early and c == early + 1:
            total = bring_together(0, early, None, False, [before])
            before = total
    before = complete(chunks - 1, [before] + pieces[-1:])
    if early < chunks - 1:
        total = bring_together(early, chunks - 1, total, False, [before])
    return bring_together(chunks - 1, chunks, total, True, [])


def solution(mesh):
    in_specs = (
        P("tones", None, None, "blk"),
        P("tones", None, None, "blk"),
        P("blk", None),
        P(),
        P(),
    )
    out_specs = P(("blk", "tones"), None, None, None)
    return jax.shard_map(
        on_device, mesh=mesh, in_specs=in_specs, out_specs=out_specs, check_vma=False
    )
```

```python
import functools

import jax
import jax.numpy as jnp
import ml_dtypes
import numpy as np
from jax import lax
from jax.experimental import pallas as pl
from jax.experimental.pallas import tpu as pltpu
from jax.sharding import PartitionSpec as P

F32 = jnp.float32
BF16 = jnp.bfloat16
VMEM_LIMIT = 56 * 1024 * 1024
HEAVY = pl.CostEstimate(flops=10**13, bytes_accessed=10**10, transcendentals=0)
ANY = pl.BlockSpec(memory_space=pl.ANY)
SMEM = pl.BlockSpec(memory_space=pltpu.SMEM)


def split(value):
    high = value.astype(BF16)
    return high, (value - high.astype(F32)).astype(BF16)


def dot(left, right, contract):
    return lax.dot_general(left, right, ((contract[:1], contract[1:]), ((), ())), preferred_element_type=F32)


def dot3(left, right, contract):
    left_high, left_low = left
    right_high, right_low = right
    return (
        dot(left_high, right_high, contract)
        + dot(left_high, right_low, contract)
        + dot(left_low, right_high, contract)
    )


def triangle(users):
    row = lax.broadcasted_iota(jnp.int32, (users, users), 0)
    column = lax.broadcasted_iota(jnp.int32, (users, users), 1)
    return row, column


def prepare_body(carry, blocks, base, pair, group, hop_offset, rates, chan, recv, *refs):
    outs = refs[len(refs) - blocks // 2 :]
    users = chan.shape[2]
    rows = recv.shape[2] // blocks

    def stacked(part):
        pieces = [chan[0, part]]
        for place in range(blocks):
            first_hop = 2 * pair[0] + (place % 2) - 2 * (place // 2)
            block = lax.rem(first_hop - hop_offset[group[0]] + 4 * blocks, blocks)
            first = pl.multiple_of(block * rows, 8)
            pieces.append(recv[0, part, pl.ds(first, rows), :])
        return split(jnp.concatenate(pieces, 0))

    left_real = stacked(0)
    left_imag = stacked(1)
    right = tuple(
        jnp.concatenate([real[:users], imag[:users]], 1) for real, imag in zip(left_real, left_imag)
    )
    real = dot3(tuple(jnp.concatenate(pair, 1) for pair in zip(left_real, left_imag)), right, (1, 1))
    imag = dot3(
        tuple(jnp.concatenate([b, -a], 1) for a, b in zip(left_real, left_imag)), right, (1, 1)
    )
    row, column = triangle(users)
    outs[0][0, :users] = jnp.where(row <= column, real[:users], imag[:users])
    for place in range(blocks):
        base = users if place < 2 else 0
        first = users + place * rows
        for part, value in enumerate((real, imag)):
            to = base + (2 * (place % 2) + part) * rows
            outs[place // 2][0, to : to + rows] = value[first : first + rows]
    if carry:
        lane = lax.broadcasted_iota(jnp.int32, (carry, users), 1)
        outs[0][0, users + 4 * rows :] = jnp.where(lane == 0, rates[0, 0], rates[0, 1])


def prepare(channel, received, step_sizes, scalars, start, count, blocks, carry, after):
    _, _, users, width = channel.shape
    symbols = received.shape[2]
    rows = symbols // blocks
    heights = [users + 4 * rows + carry] + [4 * rows] * (blocks // 2 - 1)
    return pl.pallas_call(
        functools.partial(prepare_body, carry, blocks),
        out_shape=[jax.ShapeDtypeStruct((count, height, users), F32) for height in heights],
        grid_spec=pltpu.PrefetchScalarGridSpec(
            num_scalar_prefetch=4,
            grid=(count,),
            in_specs=[
                SMEM,
                pl.BlockSpec((1, 2, users, width), lambda i, s, *_: (s[0] + start + i, 0, 0, 0)),
                pl.BlockSpec((1, 2, symbols, width), lambda i, s, *_: (s[0] + start + i, 0, 0, 0)),
            ]
            + [ANY] * len(after),
            out_specs=[pl.BlockSpec((1, height, users), lambda i, *_: (i, 0, 0)) for height in heights],
        ),
        compiler_params=pltpu.CompilerParams(vmem_limit_bytes=VMEM_LIMIT),
        cost_estimate=HEAVY,
        name="prepare",
    )(*scalars, step_sizes, channel, received, *after)


def unpack(packed, gram, sub):
    users = packed.shape[0]
    row, column = triangle(users)
    turned = packed.T
    real = split(jnp.where(row <= column, packed, turned))
    imag = split(jnp.where(row > column, packed, jnp.where(row < column, -turned, 0.0)))
    for part in range(2):
        gram[sub, part, :users, :users] = real[part]
        gram[sub, part, :users, users:] = imag[part]
        gram[sub, part, users:, :users] = -imag[part]
        gram[sub, part, users:, users:] = real[part]


def step(estimate, matched, gram, sub, rate):
    product = dot3(split(estimate), (gram[sub, 0], gram[sub, 1]), (1, 0))
    return jnp.tanh(estimate + rate * (matched - product))


def filtered(ref, base, rows, slot):
    first = base + 2 * slot * rows
    return jnp.concatenate([ref[0, first : first + rows], ref[0, first + rows : first + 2 * rows]], 1)


def chain_body(round_index, last, rows, side, rates, *refs):
    own, peer = refs[:2]
    users = own.shape[2]
    rest = refs[2:]
    base = users
    grams = (own, peer)
    if round_index:
        own, peer, came = rest[:3]
        base = 0
    gram, matched = refs[-2:]
    for packed, samples, sub in ((grams[0], own, side[0]), (grams[1], peer, 1 - side[0])):
        unpack(packed[0, :users], gram, sub)
        for slot in range(2):
            matched[sub, slot * rows : (slot + 1) * rows] = filtered(samples, base, rows, slot)

    if round_index == 0:
        even = jnp.tanh(rates[0, 0] * matched[0, :rows])
        even = step(even, matched[0, :rows], gram, 0, rates[0, 1])
        even = step(even, matched[1, :rows], gram, 1, rates[1, 0])
        odd = jnp.tanh(rates[1, 0] * matched[1, rows:])
        both = step(jnp.concatenate([even, odd], 0), matched[1], gram, 1, rates[1, 1])
    else:
        both = jnp.concatenate(
            [jnp.concatenate([came[0, slot, 0], came[0, slot, 1]], 1) for slot in range(2)], 0
        )
        for sub in range(2):
            for substep in range(2):
                both = step(both, matched[sub], gram, sub, rates[sub, substep])
    out = refs[-4:-2] if last else refs[-3:-2]
    for slot in range(2):
        for part in range(2):
            piece = both[slot * rows : (slot + 1) * rows, part * users : (part + 1) * users]
            if last:
                out[slot][0, part] = piece
            else:
                out[0][0, slot, part] = piece


def chain(round_index, last, rows, side, rates, own, peer, came, after):
    count, _, users = own[0].shape
    both_spec = pl.BlockSpec((1, 2, 2, rows, users), lambda i, s: (i, 0, 0, 0, 0))
    one_spec = pl.BlockSpec((1, 2, rows, users), lambda i, s: (i, 0, 0, 0))
    both_shape = jax.ShapeDtypeStruct((count, 2, 2, rows, users), F32)
    one_shape = jax.ShapeDtypeStruct((count, 2, rows, users), F32)
    inputs = [own[0], peer[0]]
    heights = [users if round_index else users + 4 * rows] * 2
    if round_index:
        inputs += [own[round_index], peer[round_index]]
        heights += [4 * rows] * 2
    specs = [pl.BlockSpec((1, height, users), lambda i, s: (i, 0, 0)) for height in heights]
    return pl.pallas_call(
        functools.partial(chain_body, round_index, last, rows),
        out_shape=[one_shape, one_shape] if last else both_shape,
        grid_spec=pltpu.PrefetchScalarGridSpec(
            num_scalar_prefetch=1,
            grid=(count,),
            in_specs=[SMEM] + specs + [both_spec] * len(came) + [ANY] * len(after),
            out_specs=[one_spec, one_spec] if last else both_spec,
            scratch_shapes=[
                pltpu.VMEM((2, 2, 2 * users, 2 * users), BF16),
                pltpu.VMEM((2, 2 * rows, 2 * users), F32),
            ],
        ),
        compiler_params=pltpu.CompilerParams(vmem_limit_bytes=VMEM_LIMIT),
        cost_estimate=HEAVY,
        name="chain%d" % round_index,
    )(side, rates, *inputs, *came, *after)


def finish_body(count, rows, scalars, rates, own, peer, even, odd, order, *refs):
    users = own.shape[2]
    out, gram, gathered = refs[-3:]
    tone = pl.program_id(0)
    side = scalars[0]
    even_slot = scalars[1]

    @pl.when(side == 0)
    def _():
        unpack(own[0, :users], gram, 0)

    @pl.when(side != 0)
    def _():
        unpack(peer[0, :users], gram, 0)

    matched = jnp.where(side == 0, filtered(own, users, rows, 1), filtered(peer, users, rows, 1))
    estimate = jnp.concatenate([odd[0, 0], odd[0, 1]], 1)
    for substep in range(2):
        estimate = step(estimate, matched, gram, 0, rates[0, substep])
    for part in range(2):
        first = (tone * 2 + part) * 2
        odd_row = pl.multiple_of((first + 1 - even_slot) * rows, 8)
        even_row = pl.multiple_of((first + even_slot) * rows, 8)
        gathered[pl.ds(odd_row, rows), :] = estimate[:, part * users : (part + 1) * users]
        gathered[pl.ds(even_row, rows), :] = even[0, part]

    @pl.when(tone == count - 1)
    def _():
        high, low = split(gathered[...])
        turned = dot(order[...], high, (1, 1)) + dot(order[...], low, (1, 1))
        out[...] = turned.reshape(out.shape)


def finish(rows, owners, scalars, rates, own, peer, even, odd, order, after):
    count, _, users = own[0].shape
    packed_spec = pl.BlockSpec((1, users + 4 * rows, users), lambda i, s: (i, 0, 0))
    one_spec = pl.BlockSpec((1, 2, rows, users), lambda i, s: (i, 0, 0, 0))
    shape = (owners, users // owners, count * 4 * rows)
    return pl.pallas_call(
        functools.partial(finish_body, count, rows),
        out_shape=jax.ShapeDtypeStruct(shape, F32),
        grid_spec=pltpu.PrefetchScalarGridSpec(
            num_scalar_prefetch=1,
            grid=(count,),
            in_specs=[
                SMEM,
                packed_spec,
                packed_spec,
                one_spec,
                one_spec,
                pl.BlockSpec((users, users), lambda i, s: (0, 0)),
            ]
            + [ANY] * len(after),
            out_specs=pl.BlockSpec(shape, lambda i, s: (0, 0, 0)),
            scratch_shapes=[
                pltpu.VMEM((1, 2, 2 * users, 2 * users), BF16),
                pltpu.VMEM((count * 4 * rows, users), F32),
            ],
        ),
        compiler_params=pltpu.CompilerParams(vmem_limit_bytes=VMEM_LIMIT),
        cost_estimate=HEAVY,
        name="finish",
    )(scalars, rates, own[0], peer[0], even, odd, order, *after)


def despread_body(groups, sizes, rows, folded, first, last, source, table, *refs):
    pieces = refs[: len(sizes)]
    if not first:
        total = refs[len(sizes)]
    out, tones_first, symbols_first = refs[-3:]
    items = out.shape[0]
    tones = sum(sizes)
    pair = pl.program_id(0)
    part = pl.program_id(1)

    def turn(slot):
        block = 2 * pair + slot

        def gather(group, carry):
            position = source[block * groups + group]
            for side in range(2):
                place = (group * 2 + side) * tones * 2
                src = (2 * position + side) * groups + group
                for piece, size in zip(pieces, sizes):
                    for tone in range(2 * size):
                        lane = (tone * 2 + slot) * rows
                        tones_first[place + tone, :, :rows] = piece[src, :, lane : lane + rows]
                    place = place + 2 * size
            return carry

        lax.fori_loop(0, groups, gather, 0)
        for item in range(items):
            value = tones_first[:, item, :]
            here = slice((slot * items + item) * rows, (slot * items + item + 1) * rows)
            if folded:
                high = value.astype(BF16).astype(F32)
                joined = jnp.concatenate([high, high, value - high], 0)
                symbols_first[0, here] = joined.T[:rows].astype(BF16)
            else:
                high, low = split(value.T[:rows])
                symbols_first[0, here] = high
                symbols_first[1, here] = low

    @pl.when(part == 0)
    def _():
        for slot in range(2):
            turn(slot)

    if folded:
        result = dot(symbols_first[0], table[part, 0], (1, 0))
    else:
        result = dot3((symbols_first[0], symbols_first[1]), (table[part, 0], table[part, 1]), (1, 0))
    for slot in range(2):
        for item in range(items):
            value = result[(slot * items + item) * rows : (slot * items + item + 1) * rows]
            if not first:
                value = value + total[item, 0, slot * rows : (slot + 1) * rows, :]
            out[item, 0, slot * rows : (slot + 1) * rows, :] = jnp.tanh(value) if last else value


def despread(pieces, starts, groups, half, blocks, rows, source, total, last, after):
    items = pieces[0].shape[1]
    length = groups * 2 * half
    lanes = -(-rows // 128) * 128
    sizes = [piece.shape[2] // (4 * rows) for piece in pieces]
    local = np.concatenate([np.arange(begin, begin + size) for begin, size in zip(starts, sizes)])
    index = (np.arange(groups * 2)[:, None] * half + local[None, :]).reshape(-1)
    angle = 2.0 * np.pi / length * (index[:, None] * np.arange(length)[None, :] % length)
    cosine, sine = np.cos(angle) / np.sqrt(length), np.sin(angle) / np.sqrt(length)
    table = np.stack([np.stack([cosine, -sine], 1), np.stack([sine, cosine], 1)])
    table = table.reshape(2, 1, 2 * len(index), length)
    high = table.astype(ml_dtypes.bfloat16)
    low = (table - high.astype(np.float64)).astype(ml_dtypes.bfloat16)
    depth = table.shape[2]
    folded = 3 * depth <= 256
    table = np.concatenate([high, low, high], 2) if folded else np.concatenate([high, low], 1)
    block_spec = pl.BlockSpec((items, 1, 2 * rows, length), lambda i, part, s: (0, part, i, 0))
    totals = [] if total is None else [total]
    return pl.pallas_call(
        functools.partial(despread_body, groups, sizes, rows, folded, total is None, last),
        out_shape=jax.ShapeDtypeStruct((items, 2, blocks * rows, length), F32),
        grid_spec=pltpu.PrefetchScalarGridSpec(
            num_scalar_prefetch=1,
            grid=(blocks // 2, 2),
            in_specs=[pl.BlockSpec(table.shape, lambda i, part, s: (0, 0, 0, 0))]
            + [pl.BlockSpec(piece.shape, lambda i, part, s: (0, 0, 0)) for piece in pieces]
            + [block_spec] * len(totals)
            + [ANY] * len(after),
            out_specs=block_spec,
            scratch_shapes=[
                pltpu.VMEM((depth, items, lanes), F32),
                pltpu.VMEM((table.shape[1], 2 * items * rows, table.shape[2]), BF16),
            ],
        ),
        compiler_params=pltpu.CompilerParams(vmem_limit_bytes=VMEM_LIMIT),
        cost_estimate=HEAVY,
        name="despread",
    )(source, jnp.asarray(table), *pieces, *totals, *after)


def on_device(channel, received, step_sizes, hop_offset, user_order):
    blocks = lax.axis_size("blk")
    groups = lax.axis_size("tones")
    pairs = blocks // 2
    half = channel.shape[0] // 2
    users = channel.shape[2]
    rows = received.shape[2] // blocks
    owners = blocks * groups
    position = lax.axis_index("blk")
    offset = hop_offset[lax.axis_index("tones")]
    side = position % 2
    pair = position // 2

    swap = [(p, p ^ 1) for p in range(blocks)]
    onward = [(p, (p + 2) % blocks) for p in range(blocks)]

    doubles = max((half - 4) // 2, 0)
    sizes = [1] + [2] * doubles + [1] * (half - 1 - 2 * doubles)
    starts = [sum(sizes[:c]) for c in range(len(sizes))]
    chunks = len(sizes)

    place = (pair.reshape(1), lax.axis_index("tones").reshape(1), hop_offset)
    side_alone = side.reshape(1)
    side_and_slot = jnp.stack([side, offset % 2])
    order = (user_order[:, None] == jnp.arange(users, dtype=jnp.int32)[None, :]).astype(BF16)

    begins = (jnp.arange(blocks, dtype=jnp.int32)[:, None] + hop_offset[None, :]) % blocks
    source = jnp.where(begins % 2 == 0, begins // 2 + pairs - 1, begins // 2) % pairs

    own, peer, odd, pieces = {}, {}, {}, []

    def ready(c, first_tone, carry, after):
        scalars = (first_tone.reshape(1),) + place
        return prepare(
            channel, received, step_sizes, scalars, starts[c], sizes[c], blocks, carry, after
        )

    def ready_peer(c, after):
        sent = ready(c, (1 - side) * half, 8 if c == 0 else 0, after)
        peer[c] = [lax.ppermute(value, "blk", swap) for value in sent]
        return sent[0]

    def ready_own(c, after):
        own[c] = ready(c, side * half, 0, after)
        return own[c][0]

    def complete(c, after):
        even, moved = odd[c]
        done = finish(rows, owners, side_and_slot, rates, own[c], peer[c], even, moved, order, after)
        pieces.append(
            lax.all_to_all(done, ("blk", "tones"), split_axis=0, concat_axis=0, tiled=True)
        )
        return done

    def bring_together(begin, end, total, last, after):
        return despread(
            pieces[begin:end],
            starts[begin:end],
            groups,
            half,
            blocks,
            rows,
            source.reshape(-1),
            total,
            last,
            after,
        )

    before = ready_peer(0, [])
    if chunks > 1:
        before = ready_peer(1, [before])
    before = ready_own(0, [before])
    peer_rates = peer[0][0][0, users + 4 * rows, :2].reshape(1, 2)
    rates = jnp.where(
        side == 0,
        jnp.concatenate([step_sizes, peer_rates], 0),
        jnp.concatenate([peer_rates, step_sizes], 0),
    )
    early = max(chunks - 6, 0)
    total = None
    for c in range(chunks):
        before = chain(0, False, rows, side_alone, rates, own[c], peer[c], [], [before])
        both = lax.ppermute(before, "blk", onward)
        if early and c == early + 2:
            total = bring_together(0, early, None, False, [before])
            before = total
        if c > 0:
            before = complete(c - 1, [before] + pieces[-1:])
        if c + 2 < chunks:
            before = ready_peer(c + 2, [before])
        if c + 1 < chunks:
            before = ready_own(c + 1, [before])
        for r in range(1, pairs):
            done = chain(r, r == pairs - 1, rows, side_alone, rates, own[c], peer[c], [both], [before])
            if r < pairs - 1:
                both = lax.ppermute(done, "blk", onward)
                before = done
        even, moving = done
        odd[c] = (even, lax.ppermute(moving, "blk", onward))
        before = even
    before = complete(chunks - 1, [before] + pieces[-1:])
    if early < chunks - 1:
        total = bring_together(early, chunks - 1, total, False, [before])
    return bring_together(chunks - 1, chunks, total, True, [])


def solution(mesh):
    in_specs = (
        P("tones", None, None, "blk"),
        P("tones", None, None, "blk"),
        P("blk", None),
        P(),
        P(),
    )
    out_specs = P(("blk", "tones"), None, None, None)
    return jax.shard_map(
        on_device, mesh=mesh, in_specs=in_specs, out_specs=out_specs, check_vma=False
    )
```

```python
import functools

import jax
import jax.numpy as jnp
import ml_dtypes
import numpy as np
from jax import lax
from jax.experimental import pallas as pl
from jax.experimental.pallas import tpu as pltpu
from jax.sharding import PartitionSpec as P

F32 = jnp.float32
BF16 = jnp.bfloat16
VMEM_LIMIT = 56 * 1024 * 1024
HEAVY = pl.CostEstimate(flops=10**13, bytes_accessed=10**10, transcendentals=0)
ANY = pl.BlockSpec(memory_space=pl.ANY)
SMEM = pl.BlockSpec(memory_space=pltpu.SMEM)


def split(value):
    high = value.astype(BF16)
    return high, (value - high.astype(F32)).astype(BF16)


def dot(left, right, contract):
    return lax.dot_general(left, right, ((contract[:1], contract[1:]), ((), ())), preferred_element_type=F32)


def dot3(left, right, contract):
    left_high, left_low = left
    right_high, right_low = right
    return (
        dot(left_high, right_high, contract)
        + dot(left_high, right_low, contract)
        + dot(left_low, right_high, contract)
    )


def triangle(users):
    row = lax.broadcasted_iota(jnp.int32, (users, users), 0)
    column = lax.broadcasted_iota(jnp.int32, (users, users), 1)
    return row, column


def prepare_body(carry, blocks, base, pair, group, hop_offset, rates, chan, recv, *refs):
    outs = refs[len(refs) - blocks // 2 :]
    users = chan.shape[2]
    rows = recv.shape[2] // blocks

    def stacked(part):
        pieces = [chan[0, part]]
        for place in range(blocks):
            first_hop = 2 * pair[0] + (place % 2) - 2 * (place // 2)
            block = lax.rem(first_hop - hop_offset[group[0]] + 4 * blocks, blocks)
            first = pl.multiple_of(block * rows, 8)
            pieces.append(recv[0, part, pl.ds(first, rows), :])
        return split(jnp.concatenate(pieces, 0))

    left_real = stacked(0)
    left_imag = stacked(1)
    right = tuple(
        jnp.concatenate([real[:users], imag[:users]], 1) for real, imag in zip(left_real, left_imag)
    )
    real = dot3(tuple(jnp.concatenate(pair, 1) for pair in zip(left_real, left_imag)), right, (1, 1))
    imag = dot3(
        tuple(jnp.concatenate([b, -a], 1) for a, b in zip(left_real, left_imag)), right, (1, 1)
    )
    row, column = triangle(users)
    outs[0][0, :users] = jnp.where(row <= column, real[:users], imag[:users])
    for place in range(blocks):
        base = users if place < 2 else 0
        first = users + place * rows
        for part, value in enumerate((real, imag)):
            to = base + (2 * (place % 2) + part) * rows
            outs[place // 2][0, to : to + rows] = value[first : first + rows]
    if carry:
        lane = lax.broadcasted_iota(jnp.int32, (carry, users), 1)
        outs[0][0, users + 4 * rows :] = jnp.where(lane == 0, rates[0, 0], rates[0, 1])


def prepare(channel, received, step_sizes, scalars, start, count, blocks, carry, after):
    _, _, users, width = channel.shape
    symbols = received.shape[2]
    rows = symbols // blocks
    heights = [users + 4 * rows + carry] + [4 * rows] * (blocks // 2 - 1)
    return pl.pallas_call(
        functools.partial(prepare_body, carry, blocks),
        out_shape=[jax.ShapeDtypeStruct((count, height, users), F32) for height in heights],
        grid_spec=pltpu.PrefetchScalarGridSpec(
            num_scalar_prefetch=4,
            grid=(count,),
            in_specs=[
                SMEM,
                pl.BlockSpec((1, 2, users, width), lambda i, s, *_: (s[0] + start + i, 0, 0, 0)),
                pl.BlockSpec((1, 2, symbols, width), lambda i, s, *_: (s[0] + start + i, 0, 0, 0)),
            ]
            + [ANY] * len(after),
            out_specs=[pl.BlockSpec((1, height, users), lambda i, *_: (i, 0, 0)) for height in heights],
        ),
        compiler_params=pltpu.CompilerParams(vmem_limit_bytes=VMEM_LIMIT),
        cost_estimate=HEAVY,
        name="prepare",
    )(*scalars, step_sizes, channel, received, *after)


def unpack(packed, gram, sub):
    users = packed.shape[0]
    row, column = triangle(users)
    turned = packed.T
    real = split(jnp.where(row <= column, packed, turned))
    imag = split(jnp.where(row > column, packed, jnp.where(row < column, -turned, 0.0)))
    for part in range(2):
        gram[sub, part, :users, :users] = real[part]
        gram[sub, part, :users, users:] = imag[part]
        gram[sub, part, users:, :users] = -imag[part]
        gram[sub, part, users:, users:] = real[part]


def step(estimate, matched, gram, sub, rate):
    product = dot3(split(estimate), (gram[sub, 0], gram[sub, 1]), (1, 0))
    return jnp.tanh(estimate + rate * (matched - product))


def filtered(ref, base, rows, slot):
    first = base + 2 * slot * rows
    return jnp.concatenate([ref[0, first : first + rows], ref[0, first + rows : first + 2 * rows]], 1)


def chain_body(round_index, last, rows, side, rates, *refs):
    own, peer = refs[:2]
    users = own.shape[2]
    rest = refs[2:]
    base = users
    grams = (own, peer)
    if round_index:
        own, peer, came = rest[:3]
        base = 0
    gram, matched = refs[-2:]
    for packed, samples, sub in ((grams[0], own, side[0]), (grams[1], peer, 1 - side[0])):
        unpack(packed[0, :users], gram, sub)
        for slot in range(2):
            matched[sub, slot * rows : (slot + 1) * rows] = filtered(samples, base, rows, slot)

    if round_index == 0:
        even = jnp.tanh(rates[0, 0] * matched[0, :rows])
        even = step(even, matched[0, :rows], gram, 0, rates[0, 1])
        even = step(even, matched[1, :rows], gram, 1, rates[1, 0])
        odd = jnp.tanh(rates[1, 0] * matched[1, rows:])
        both = step(jnp.concatenate([even, odd], 0), matched[1], gram, 1, rates[1, 1])
    else:
        both = jnp.concatenate(
            [jnp.concatenate([came[0, slot, 0], came[0, slot, 1]], 1) for slot in range(2)], 0
        )
        for sub in range(2):
            for substep in range(2):
                both = step(both, matched[sub], gram, sub, rates[sub, substep])
    out = refs[-4:-2] if last else refs[-3:-2]
    for slot in range(2):
        for part in range(2):
            piece = both[slot * rows : (slot + 1) * rows, part * users : (part + 1) * users]
            if last:
                out[slot][0, part] = piece
            else:
                out[0][0, slot, part] = piece


def chain(round_index, last, rows, side, rates, own, peer, came, after):
    count, _, users = own[0].shape
    both_spec = pl.BlockSpec((1, 2, 2, rows, users), lambda i, s: (i, 0, 0, 0, 0))
    one_spec = pl.BlockSpec((1, 2, rows, users), lambda i, s: (i, 0, 0, 0))
    both_shape = jax.ShapeDtypeStruct((count, 2, 2, rows, users), F32)
    one_shape = jax.ShapeDtypeStruct((count, 2, rows, users), F32)
    inputs = [own[0], peer[0]]
    heights = [users if round_index else users + 4 * rows] * 2
    if round_index:
        inputs += [own[round_index], peer[round_index]]
        heights += [4 * rows] * 2
    specs = [pl.BlockSpec((1, height, users), lambda i, s: (i, 0, 0)) for height in heights]
    return pl.pallas_call(
        functools.partial(chain_body, round_index, last, rows),
        out_shape=[one_shape, one_shape] if last else both_shape,
        grid_spec=pltpu.PrefetchScalarGridSpec(
            num_scalar_prefetch=1,
            grid=(count,),
            in_specs=[SMEM] + specs + [both_spec] * len(came) + [ANY] * len(after),
            out_specs=[one_spec, one_spec] if last else both_spec,
            scratch_shapes=[
                pltpu.VMEM((2, 2, 2 * users, 2 * users), BF16),
                pltpu.VMEM((2, 2 * rows, 2 * users), F32),
            ],
        ),
        compiler_params=pltpu.CompilerParams(vmem_limit_bytes=VMEM_LIMIT),
        cost_estimate=HEAVY,
        name="chain%d" % round_index,
    )(side, rates, *inputs, *came, *after)


def finish_body(count, rows, scalars, rates, own, peer, even, odd, order, *refs):
    users = own.shape[2]
    out, gram, gathered = refs[-3:]
    tone = pl.program_id(0)
    side = scalars[0]
    even_slot = scalars[1]

    @pl.when(side == 0)
    def _():
        unpack(own[0, :users], gram, 0)

    @pl.when(side != 0)
    def _():
        unpack(peer[0, :users], gram, 0)

    matched = jnp.where(side == 0, filtered(own, users, rows, 1), filtered(peer, users, rows, 1))
    estimate = jnp.concatenate([odd[0, 0], odd[0, 1]], 1)
    for substep in range(2):
        estimate = step(estimate, matched, gram, 0, rates[0, substep])
    for part in range(2):
        first = (tone * 2 + part) * 2
        odd_row = pl.multiple_of((first + 1 - even_slot) * rows, 8)
        even_row = pl.multiple_of((first + even_slot) * rows, 8)
        gathered[pl.ds(odd_row, rows), :] = estimate[:, part * users : (part + 1) * users]
        gathered[pl.ds(even_row, rows), :] = even[0, part]

    @pl.when(tone == count - 1)
    def _():
        high, low = split(gathered[...])
        turned = dot(order[...], high, (1, 1)) + dot(order[...], low, (1, 1))
        out[...] = turned.reshape(out.shape)


def finish(rows, owners, scalars, rates, own, peer, even, odd, order, after):
    count, _, users = own[0].shape
    packed_spec = pl.BlockSpec((1, users + 4 * rows, users), lambda i, s: (i, 0, 0))
    one_spec = pl.BlockSpec((1, 2, rows, users), lambda i, s: (i, 0, 0, 0))
    shape = (owners, users // owners, count * 4 * rows)
    return pl.pallas_call(
        functools.partial(finish_body, count, rows),
        out_shape=jax.ShapeDtypeStruct(shape, F32),
        grid_spec=pltpu.PrefetchScalarGridSpec(
            num_scalar_prefetch=1,
            grid=(count,),
            in_specs=[
                SMEM,
                packed_spec,
                packed_spec,
                one_spec,
                one_spec,
                pl.BlockSpec((users, users), lambda i, s: (0, 0)),
            ]
            + [ANY] * len(after),
            out_specs=pl.BlockSpec(shape, lambda i, s: (0, 0, 0)),
            scratch_shapes=[
                pltpu.VMEM((1, 2, 2 * users, 2 * users), BF16),
                pltpu.VMEM((count * 4 * rows, users), F32),
            ],
        ),
        compiler_params=pltpu.CompilerParams(vmem_limit_bytes=VMEM_LIMIT),
        cost_estimate=HEAVY,
        name="finish",
    )(scalars, rates, own[0], peer[0], even, odd, order, *after)


def despread_body(groups, sizes, rows, folded, first, last, source, table, *refs):
    pieces = refs[: len(sizes)]
    if not first:
        total = refs[len(sizes)]
    out, tones_first, symbols_first = refs[-3:]
    tones = sum(sizes)
    length = out.shape[3]
    blocks = tones_first.shape[0]
    item = pl.program_id(0)

    @pl.when(item == 0)
    def _():
        for block in range(blocks):

            def gather(group, carry):
                position = source[block * groups + group]
                for side in range(2):
                    place = (group * 2 + side) * tones * 2
                    src = (2 * position + side) * groups + group
                    for piece, size in zip(pieces, sizes):
                        for tone in range(2 * size):
                            lane = (tone * 2 + block % 2) * rows
                            tones_first[block, place + tone, :, :rows] = piece[src, :, lane : lane + rows]
                        place = place + 2 * size
                return carry

            lax.fori_loop(0, groups, gather, 0)

    for block in range(blocks):
        value = tones_first[block, :, item, :]
        here = slice(block * rows, (block + 1) * rows)
        if folded:
            high = value.astype(BF16).astype(F32)
            joined = jnp.concatenate([high, high, value - high], 0)
            symbols_first[0, here] = joined.T[:rows].astype(BF16)
        else:
            high, low = split(value.T[:rows])
            symbols_first[0, here] = high
            symbols_first[1, here] = low
    if folded:
        result = dot(symbols_first[0], table[0], (1, 0))
    else:
        result = dot3((symbols_first[0], symbols_first[1]), (table[0], table[1]), (1, 0))
    for part in range(2):
        value = result[:, part * length : (part + 1) * length]
        if not first:
            value = value + total[0, part]
        out[0, part] = jnp.tanh(value) if last else value


def despread(pieces, starts, groups, half, blocks, rows, source, total, last, after):
    items = pieces[0].shape[1]
    length = groups * 2 * half
    lanes = -(-rows // 128) * 128
    sizes = [piece.shape[2] // (4 * rows) for piece in pieces]
    local = np.concatenate([np.arange(begin, begin + size) for begin, size in zip(starts, sizes)])
    index = (np.arange(groups * 2)[:, None] * half + local[None, :]).reshape(-1)
    angle = 2.0 * np.pi / length * (index[:, None] * np.arange(length)[None, :] % length)
    cosine, sine = np.cos(angle) / np.sqrt(length), np.sin(angle) / np.sqrt(length)
    real, imag = np.concatenate([cosine, sine], 1), np.concatenate([-sine, cosine], 1)
    table = np.stack([real, imag], 1).reshape(1, 2 * len(index), 2 * length)
    high = table.astype(ml_dtypes.bfloat16)
    low = (table - high.astype(np.float64)).astype(ml_dtypes.bfloat16)
    depth = table.shape[1]
    folded = 3 * depth <= 256
    table = np.concatenate([high, low, high], 1) if folded else np.concatenate([high, low], 0)
    symbols = blocks * rows
    block_spec = pl.BlockSpec((1, 2, symbols, length), lambda i, s: (i, 0, 0, 0))
    totals = [] if total is None else [total]
    return pl.pallas_call(
        functools.partial(despread_body, groups, sizes, rows, folded, total is None, last),
        out_shape=jax.ShapeDtypeStruct((items, 2, symbols, length), F32),
        grid_spec=pltpu.PrefetchScalarGridSpec(
            num_scalar_prefetch=1,
            grid=(items,),
            in_specs=[pl.BlockSpec(table.shape, lambda i, s: (0, 0, 0))]
            + [pl.BlockSpec(piece.shape, lambda i, s: (0, 0, 0)) for piece in pieces]
            + [block_spec] * len(totals)
            + [ANY] * len(after),
            out_specs=block_spec,
            scratch_shapes=[
                pltpu.VMEM((blocks, depth, items, lanes), F32),
                pltpu.VMEM((table.shape[0], symbols, table.shape[1]), BF16),
            ],
        ),
        compiler_params=pltpu.CompilerParams(vmem_limit_bytes=VMEM_LIMIT),
        cost_estimate=HEAVY,
        name="despread",
    )(source, jnp.asarray(table), *pieces, *totals, *after)


def on_device(channel, received, step_sizes, hop_offset, user_order):
    blocks = lax.axis_size("blk")
    groups = lax.axis_size("tones")
    pairs = blocks // 2
    half = channel.shape[0] // 2
    users = channel.shape[2]
    rows = received.shape[2] // blocks
    owners = blocks * groups
    position = lax.axis_index("blk")
    offset = hop_offset[lax.axis_index("tones")]
    side = position % 2
    pair = position // 2

    swap = [(p, p ^ 1) for p in range(blocks)]
    onward = [(p, (p + 2) % blocks) for p in range(blocks)]

    doubles = max((half - 4) // 2, 0)
    sizes = [1] + [2] * doubles + [1] * (half - 1 - 2 * doubles)
    starts = [sum(sizes[:c]) for c in range(len(sizes))]
    chunks = len(sizes)

    place = (pair.reshape(1), lax.axis_index("tones").reshape(1), hop_offset)
    side_alone = side.reshape(1)
    side_and_slot = jnp.stack([side, offset % 2])
    order = (user_order[:, None] == jnp.arange(users, dtype=jnp.int32)[None, :]).astype(BF16)

    begins = (jnp.arange(blocks, dtype=jnp.int32)[:, None] + hop_offset[None, :]) % blocks
    source = jnp.where(begins % 2 == 0, begins // 2 + pairs - 1, begins // 2) % pairs

    own, peer, odd, pieces = {}, {}, {}, []

    def ready(c, first_tone, carry, after):
        scalars = (first_tone.reshape(1),) + place
        return prepare(
            channel, received, step_sizes, scalars, starts[c], sizes[c], blocks, carry, after
        )

    def ready_peer(c, after):
        sent = ready(c, (1 - side) * half, 8 if c == 0 else 0, after)
        peer[c] = [lax.ppermute(value, "blk", swap) for value in sent]
        return sent[0]

    def ready_own(c, after):
        own[c] = ready(c, side * half, 0, after)
        return own[c][0]

    def complete(c, after):
        even, moved = odd[c]
        done = finish(rows, owners, side_and_slot, rates, own[c], peer[c], even, moved, order, after)
        pieces.append(
            lax.all_to_all(done, ("blk", "tones"), split_axis=0, concat_axis=0, tiled=True)
        )
        return done

    def bring_together(begin, end, total, last, after):
        return despread(
            pieces[begin:end],
            starts[begin:end],
            groups,
            half,
            blocks,
            rows,
            source.reshape(-1),
            total,
            last,
            after,
        )

    before = ready_peer(0, [])
    if chunks > 1:
        before = ready_peer(1, [before])
    before = ready_own(0, [before])
    peer_rates = peer[0][0][0, users + 4 * rows, :2].reshape(1, 2)
    rates = jnp.where(
        side == 0,
        jnp.concatenate([step_sizes, peer_rates], 0),
        jnp.concatenate([peer_rates, step_sizes], 0),
    )
    ahead = {c: [c + 1] for c in range(chunks - 1)}
    parts = {}
    if chunks > 8:
        for c in (chunks - 2, chunks - 1):
            ahead[c - 1].remove(c)
            ahead[c - 4].append(c)
        parts = {chunks - 4: chunks - 6, chunks - 2: chunks - 4}
    begin, total = 0, None
    for c in range(chunks):
        before = chain(0, False, rows, side_alone, rates, own[c], peer[c], [], [before])
        both = lax.ppermute(before, "blk", onward)
        if c in parts:
            total = bring_together(begin, parts[c], total, False, [before])
            begin, before = parts[c], total
        if c > 0:
            before = complete(c - 1, [before] + pieces[-1:])
        if c + 2 < chunks:
            before = ready_peer(c + 2, [before])
        for other in ahead.get(c, []):
            before = ready_own(other, [before])
        for r in range(1, pairs):
            done = chain(r, r == pairs - 1, rows, side_alone, rates, own[c], peer[c], [both], [before])
            if r < pairs - 1:
                both = lax.ppermute(done, "blk", onward)
                before = done
        even, moving = done
        odd[c] = (even, lax.ppermute(moving, "blk", onward))
        before = even
    before = complete(chunks - 1, [before] + pieces[-1:])
    if begin < chunks - 1:
        total = bring_together(begin, chunks - 1, total, False, [before])
    return bring_together(chunks - 1, chunks, total, True, [])


def solution(mesh):
    in_specs = (
        P("tones", None, None, "blk"),
        P("tones", None, None, "blk"),
        P("blk", None),
        P(),
        P(),
    )
    out_specs = P(("blk", "tones"), None, None, None)
    return jax.shard_map(
        on_device, mesh=mesh, in_specs=in_specs, out_specs=out_specs, check_vma=False
    )
```

```python
import functools

import jax
import jax.numpy as jnp
import ml_dtypes
import numpy as np
from jax import lax
from jax.experimental import pallas as pl
from jax.experimental.pallas import tpu as pltpu
from jax.sharding import PartitionSpec as P

F32 = jnp.float32
BF16 = jnp.bfloat16
VMEM_LIMIT = 56 * 1024 * 1024
HEAVY = pl.CostEstimate(flops=10**13, bytes_accessed=10**10, transcendentals=0)
ANY = pl.BlockSpec(memory_space=pl.ANY)
SMEM = pl.BlockSpec(memory_space=pltpu.SMEM)


def split(value):
    high = value.astype(BF16)
    return high, (value - high.astype(F32)).astype(BF16)


def dot(left, right, contract):
    return lax.dot_general(left, right, ((contract[:1], contract[1:]), ((), ())), preferred_element_type=F32)


def dot3(left, right, contract):
    left_high, left_low = left
    right_high, right_low = right
    return (
        dot(left_high, right_high, contract)
        + dot(left_high, right_low, contract)
        + dot(left_low, right_high, contract)
    )


def triangle(users):
    row = lax.broadcasted_iota(jnp.int32, (users, users), 0)
    column = lax.broadcasted_iota(jnp.int32, (users, users), 1)
    return row, column


def prepare_body(carry, blocks, base, pair, group, hop_offset, rates, chan, recv, *refs):
    outs = refs[len(refs) - blocks // 2 :]
    users = chan.shape[2]
    rows = recv.shape[2] // blocks

    def stacked(part):
        pieces = [chan[0, part]]
        for place in range(blocks):
            first_hop = 2 * pair[0] + (place % 2) - 2 * (place // 2)
            block = lax.rem(first_hop - hop_offset[group[0]] + 4 * blocks, blocks)
            first = pl.multiple_of(block * rows, 8)
            pieces.append(recv[0, part, pl.ds(first, rows), :])
        return split(jnp.concatenate(pieces, 0))

    left_real = stacked(0)
    left_imag = stacked(1)
    right = tuple(
        jnp.concatenate([real[:users], imag[:users]], 1) for real, imag in zip(left_real, left_imag)
    )
    real = dot3(tuple(jnp.concatenate(pair, 1) for pair in zip(left_real, left_imag)), right, (1, 1))
    imag = dot3(
        tuple(jnp.concatenate([b, -a], 1) for a, b in zip(left_real, left_imag)), right, (1, 1)
    )
    row, column = triangle(users)
    outs[0][0, :users] = jnp.where(row <= column, real[:users], imag[:users])
    for place in range(blocks):
        base = users if place < 2 else 0
        first = users + place * rows
        for part, value in enumerate((real, imag)):
            to = base + (2 * (place % 2) + part) * rows
            outs[place // 2][0, to : to + rows] = value[first : first + rows]
    if carry:
        lane = lax.broadcasted_iota(jnp.int32, (carry, users), 1)
        outs[0][0, users + 4 * rows :] = jnp.where(lane == 0, rates[0, 0], rates[0, 1])


def prepare(channel, received, step_sizes, scalars, start, count, blocks, carry, after):
    _, _, users, width = channel.shape
    symbols = received.shape[2]
    rows = symbols // blocks
    heights = [users + 4 * rows + carry] + [4 * rows] * (blocks // 2 - 1)
    return pl.pallas_call(
        functools.partial(prepare_body, carry, blocks),
        out_shape=[jax.ShapeDtypeStruct((count, height, users), F32) for height in heights],
        grid_spec=pltpu.PrefetchScalarGridSpec(
            num_scalar_prefetch=4,
            grid=(count,),
            in_specs=[
                SMEM,
                pl.BlockSpec((1, 2, users, width), lambda i, s, *_: (s[0] + start + i, 0, 0, 0)),
                pl.BlockSpec((1, 2, symbols, width), lambda i, s, *_: (s[0] + start + i, 0, 0, 0)),
            ]
            + [ANY] * len(after),
            out_specs=[pl.BlockSpec((1, height, users), lambda i, *_: (i, 0, 0)) for height in heights],
        ),
        compiler_params=pltpu.CompilerParams(vmem_limit_bytes=VMEM_LIMIT),
        cost_estimate=HEAVY,
        name="prepare",
    )(*scalars, step_sizes, channel, received, *after)


def unpack(packed, gram, sub):
    users = packed.shape[0]
    row, column = triangle(users)
    turned = packed.T
    real = split(jnp.where(row <= column, packed, turned))
    imag = split(jnp.where(row > column, packed, jnp.where(row < column, -turned, 0.0)))
    for part in range(2):
        gram[sub, part, :users, :users] = real[part]
        gram[sub, part, :users, users:] = imag[part]
        gram[sub, part, users:, :users] = -imag[part]
        gram[sub, part, users:, users:] = real[part]


def step(estimate, matched, gram, sub, rate):
    product = dot3(split(estimate), (gram[sub, 0], gram[sub, 1]), (1, 0))
    return jnp.tanh(estimate + rate * (matched - product))


def filtered(ref, base, rows, slot):
    first = base + 2 * slot * rows
    return jnp.concatenate([ref[0, first : first + rows], ref[0, first + rows : first + 2 * rows]], 1)


def chain_body(round_index, last, rows, side, rates, *refs):
    own, peer = refs[:2]
    users = own.shape[2]
    rest = refs[2:]
    base = users
    grams = (own, peer)
    if round_index:
        own, peer, came = rest[:3]
        base = 0
    gram, matched = refs[-2:]
    for packed, samples, sub in ((grams[0], own, side[0]), (grams[1], peer, 1 - side[0])):
        unpack(packed[0, :users], gram, sub)
        for slot in range(2):
            matched[sub, slot * rows : (slot + 1) * rows] = filtered(samples, base, rows, slot)

    if round_index == 0:
        even = jnp.tanh(rates[0, 0] * matched[0, :rows])
        even = step(even, matched[0, :rows], gram, 0, rates[0, 1])
        even = step(even, matched[1, :rows], gram, 1, rates[1, 0])
        odd = jnp.tanh(rates[1, 0] * matched[1, rows:])
        both = step(jnp.concatenate([even, odd], 0), matched[1], gram, 1, rates[1, 1])
    else:
        both = jnp.concatenate(
            [jnp.concatenate([came[0, slot, 0], came[0, slot, 1]], 1) for slot in range(2)], 0
        )
        for sub in range(2):
            for substep in range(2):
                both = step(both, matched[sub], gram, sub, rates[sub, substep])
    out = refs[-4:-2] if last else refs[-3:-2]
    for slot in range(2):
        for part in range(2):
            piece = both[slot * rows : (slot + 1) * rows, part * users : (part + 1) * users]
            if last:
                out[slot][0, part] = piece
            else:
                out[0][0, slot, part] = piece


def chain(round_index, last, rows, side, rates, own, peer, came, after):
    count, _, users = own[0].shape
    both_spec = pl.BlockSpec((1, 2, 2, rows, users), lambda i, s: (i, 0, 0, 0, 0))
    one_spec = pl.BlockSpec((1, 2, rows, users), lambda i, s: (i, 0, 0, 0))
    both_shape = jax.ShapeDtypeStruct((count, 2, 2, rows, users), F32)
    one_shape = jax.ShapeDtypeStruct((count, 2, rows, users), F32)
    inputs = [own[0], peer[0]]
    heights = [users if round_index else users + 4 * rows] * 2
    if round_index:
        inputs += [own[round_index], peer[round_index]]
        heights += [4 * rows] * 2
    specs = [pl.BlockSpec((1, height, users), lambda i, s: (i, 0, 0)) for height in heights]
    return pl.pallas_call(
        functools.partial(chain_body, round_index, last, rows),
        out_shape=[one_shape, one_shape] if last else both_shape,
        grid_spec=pltpu.PrefetchScalarGridSpec(
            num_scalar_prefetch=1,
            grid=(count,),
            in_specs=[SMEM] + specs + [both_spec] * len(came) + [ANY] * len(after),
            out_specs=[one_spec, one_spec] if last else both_spec,
            scratch_shapes=[
                pltpu.VMEM((2, 2, 2 * users, 2 * users), BF16),
                pltpu.VMEM((2, 2 * rows, 2 * users), F32),
            ],
        ),
        compiler_params=pltpu.CompilerParams(vmem_limit_bytes=VMEM_LIMIT),
        cost_estimate=HEAVY,
        name="chain%d" % round_index,
    )(side, rates, *inputs, *came, *after)


def finish_body(count, rows, scalars, rates, own, peer, even, odd, order, *refs):
    users = own.shape[2]
    out, gram, gathered = refs[-3:]
    tone = pl.program_id(0)
    side = scalars[0]
    even_slot = scalars[1]

    @pl.when(side == 0)
    def _():
        unpack(own[0, :users], gram, 0)

    @pl.when(side != 0)
    def _():
        unpack(peer[0, :users], gram, 0)

    matched = jnp.where(side == 0, filtered(own, users, rows, 1), filtered(peer, users, rows, 1))
    estimate = jnp.concatenate([odd[0, 0], odd[0, 1]], 1)
    for substep in range(2):
        estimate = step(estimate, matched, gram, 0, rates[0, substep])
    for part in range(2):
        first = (tone * 2 + part) * 2
        odd_row = pl.multiple_of((first + 1 - even_slot) * rows, 8)
        even_row = pl.multiple_of((first + even_slot) * rows, 8)
        gathered[pl.ds(odd_row, rows), :] = estimate[:, part * users : (part + 1) * users]
        gathered[pl.ds(even_row, rows), :] = even[0, part]

    @pl.when(tone == count - 1)
    def _():
        high, low = split(gathered[...])
        turned = dot(order[...], high, (1, 1)) + dot(order[...], low, (1, 1))
        out[...] = turned.reshape(out.shape)


def finish(rows, owners, scalars, rates, own, peer, even, odd, order, after):
    count, _, users = own[0].shape
    packed_spec = pl.BlockSpec((1, users + 4 * rows, users), lambda i, s: (i, 0, 0))
    one_spec = pl.BlockSpec((1, 2, rows, users), lambda i, s: (i, 0, 0, 0))
    shape = (owners, users // owners, count * 4 * rows)
    return pl.pallas_call(
        functools.partial(finish_body, count, rows),
        out_shape=jax.ShapeDtypeStruct(shape, F32),
        grid_spec=pltpu.PrefetchScalarGridSpec(
            num_scalar_prefetch=1,
            grid=(count,),
            in_specs=[
                SMEM,
                packed_spec,
                packed_spec,
                one_spec,
                one_spec,
                pl.BlockSpec((users, users), lambda i, s: (0, 0)),
            ]
            + [ANY] * len(after),
            out_specs=pl.BlockSpec(shape, lambda i, s: (0, 0, 0)),
            scratch_shapes=[
                pltpu.VMEM((1, 2, 2 * users, 2 * users), BF16),
                pltpu.VMEM((count * 4 * rows, users), F32),
            ],
        ),
        compiler_params=pltpu.CompilerParams(vmem_limit_bytes=VMEM_LIMIT),
        cost_estimate=HEAVY,
        name="finish",
    )(scalars, rates, own[0], peer[0], even, odd, order, *after)


def despread_body(groups, sizes, rows, folded, first, last, source, table, *refs):
    pieces = refs[: len(sizes)]
    if not first:
        total = refs[len(sizes)]
    out, tones_first, symbols_first, held, arrived, left = refs[-6:]
    tones = sum(sizes)
    items, _, _, length = held.shape
    blocks = tones_first.shape[0]

    def fetch(item):
        return pltpu.make_async_copy(total.at[item], held.at[item], arrived.at[item])

    def store(item):
        return pltpu.make_async_copy(held.at[item], out.at[item], left.at[item])

    if not first:
        for item in range(items):
            fetch(item).start()
    for block in range(blocks):

        def gather(group, carry):
            position = source[block * groups + group]
            for side in range(2):
                place = (group * 2 + side) * tones * 2
                src = (2 * position + side) * groups + group
                for piece, size in zip(pieces, sizes):
                    for tone in range(2 * size):
                        lane = (tone * 2 + block % 2) * rows
                        tones_first[block, place + tone, :, :rows] = piece[src, :, lane : lane + rows]
                    place = place + 2 * size
            return carry

        lax.fori_loop(0, groups, gather, 0)

    for item in range(items):
        despread_item(rows, folded, first, last, item, table, tones_first, symbols_first, held, fetch)
        store(item).start()
    for item in range(items):
        store(item).wait()


def despread_item(rows, folded, first, last, item, table, tones_first, symbols_first, held, fetch):
    length = held.shape[3]
    blocks = tones_first.shape[0]
    for block in range(blocks):
        value = tones_first[block, :, item, :]
        here = slice(block * rows, (block + 1) * rows)
        if folded:
            high = value.astype(BF16).astype(F32)
            joined = jnp.concatenate([high, high, value - high], 0)
            symbols_first[0, here] = joined.T[:rows].astype(BF16)
        else:
            high, low = split(value.T[:rows])
            symbols_first[0, here] = high
            symbols_first[1, here] = low
    if folded:
        result = dot(symbols_first[0], table[0], (1, 0))
    else:
        result = dot3((symbols_first[0], symbols_first[1]), (table[0], table[1]), (1, 0))
    if not first:
        fetch(item).wait()
    for part in range(2):
        value = result[:, part * length : (part + 1) * length]
        if not first:
            value = value + held[item, part]
        held[item, part] = jnp.tanh(value) if last else value


def despread(pieces, starts, groups, half, blocks, rows, source, total, last, after):
    items = pieces[0].shape[1]
    length = groups * 2 * half
    lanes = -(-rows // 128) * 128
    sizes = [piece.shape[2] // (4 * rows) for piece in pieces]
    local = np.concatenate([np.arange(begin, begin + size) for begin, size in zip(starts, sizes)])
    index = (np.arange(groups * 2)[:, None] * half + local[None, :]).reshape(-1)
    angle = 2.0 * np.pi / length * (index[:, None] * np.arange(length)[None, :] % length)
    cosine, sine = np.cos(angle) / np.sqrt(length), np.sin(angle) / np.sqrt(length)
    real, imag = np.concatenate([cosine, sine], 1), np.concatenate([-sine, cosine], 1)
    table = np.stack([real, imag], 1).reshape(1, 2 * len(index), 2 * length)
    high = table.astype(ml_dtypes.bfloat16)
    low = (table - high.astype(np.float64)).astype(ml_dtypes.bfloat16)
    depth = table.shape[1]
    folded = 3 * depth <= 256
    table = np.concatenate([high, low, high], 1) if folded else np.concatenate([high, low], 0)
    symbols = blocks * rows
    totals = [] if total is None else [total]
    return pl.pallas_call(
        functools.partial(despread_body, groups, sizes, rows, folded, total is None, last),
        out_shape=jax.ShapeDtypeStruct((items, 2, symbols, length), F32),
        grid_spec=pltpu.PrefetchScalarGridSpec(
            num_scalar_prefetch=1,
            grid=(1,),
            in_specs=[pl.BlockSpec(table.shape, lambda i, s: (0, 0, 0))]
            + [pl.BlockSpec(piece.shape, lambda i, s: (0, 0, 0)) for piece in pieces]
            + [ANY] * len(totals)
            + [ANY] * len(after),
            out_specs=ANY,
            scratch_shapes=[
                pltpu.VMEM((blocks, depth, items, lanes), F32),
                pltpu.VMEM((table.shape[0], symbols, table.shape[1]), BF16),
                pltpu.VMEM((items, 2, symbols, length), F32),
                pltpu.SemaphoreType.DMA((items,)),
                pltpu.SemaphoreType.DMA((items,)),
            ],
        ),
        compiler_params=pltpu.CompilerParams(vmem_limit_bytes=VMEM_LIMIT),
        cost_estimate=HEAVY,
        name="despread",
    )(source, jnp.asarray(table), *pieces, *totals, *after)


def on_device(channel, received, step_sizes, hop_offset, user_order):
    blocks = lax.axis_size("blk")
    groups = lax.axis_size("tones")
    pairs = blocks // 2
    half = channel.shape[0] // 2
    users = channel.shape[2]
    rows = received.shape[2] // blocks
    owners = blocks * groups
    position = lax.axis_index("blk")
    offset = hop_offset[lax.axis_index("tones")]
    side = position % 2
    pair = position // 2

    swap = [(p, p ^ 1) for p in range(blocks)]
    onward = [(p, (p + 2) % blocks) for p in range(blocks)]

    doubles = max((half - 4) // 2, 0)
    sizes = [1] + [2] * doubles + [1] * (half - 1 - 2 * doubles)
    starts = [sum(sizes[:c]) for c in range(len(sizes))]
    chunks = len(sizes)

    place = (pair.reshape(1), lax.axis_index("tones").reshape(1), hop_offset)
    side_alone = side.reshape(1)
    side_and_slot = jnp.stack([side, offset % 2])
    order = (user_order[:, None] == jnp.arange(users, dtype=jnp.int32)[None, :]).astype(BF16)

    begins = (jnp.arange(blocks, dtype=jnp.int32)[:, None] + hop_offset[None, :]) % blocks
    source = jnp.where(begins % 2 == 0, begins // 2 + pairs - 1, begins // 2) % pairs

    own, peer, odd, pieces = {}, {}, {}, []

    def ready(c, first_tone, carry, after):
        scalars = (first_tone.reshape(1),) + place
        return prepare(
            channel, received, step_sizes, scalars, starts[c], sizes[c], blocks, carry, after
        )

    def ready_peer(c, after):
        sent = ready(c, (1 - side) * half, 8 if c == 0 else 0, after)
        peer[c] = [lax.ppermute(value, "blk", swap) for value in sent]
        return sent[0]

    def ready_own(c, after):
        own[c] = ready(c, side * half, 0, after)
        return own[c][0]

    def complete(c, after):
        even, moved = odd[c]
        done = finish(rows, owners, side_and_slot, rates, own[c], peer[c], even, moved, order, after)
        pieces.append(
            lax.all_to_all(done, ("blk", "tones"), split_axis=0, concat_axis=0, tiled=True)
        )
        return done

    def bring_together(begin, end, total, last, after):
        return despread(
            pieces[begin:end],
            starts[begin:end],
            groups,
            half,
            blocks,
            rows,
            source.reshape(-1),
            total,
            last,
            after,
        )

    before = ready_peer(0, [])
    if chunks > 1:
        before = ready_peer(1, [before])
    before = ready_own(0, [before])
    peer_rates = peer[0][0][0, users + 4 * rows, :2].reshape(1, 2)
    rates = jnp.where(
        side == 0,
        jnp.concatenate([step_sizes, peer_rates], 0),
        jnp.concatenate([peer_rates, step_sizes], 0),
    )
    ahead = {c: [c + 1] for c in range(chunks - 1)}
    parts = {}
    if chunks > 8:
        for c in (chunks - 2, chunks - 1):
            ahead[c - 1].remove(c)
            ahead[c - 5].append(c)
        parts = {chunks - 5: chunks - 7}
    begin, total = 0, None
    for c in range(chunks):
        before = chain(0, False, rows, side_alone, rates, own[c], peer[c], [], [before])
        both = lax.ppermute(before, "blk", onward)
        if c in parts:
            total = bring_together(begin, parts[c], total, False, [before])
            begin, before = parts[c], total
        if c > 0:
            before = complete(c - 1, [before] + ([] if c >= chunks - 2 else pieces[-1:]))
        if c + 2 < chunks:
            before = ready_peer(c + 2, [before])
        for other in ahead.get(c, []):
            before = ready_own(other, [before])
        for r in range(1, pairs):
            after = [before] + (pieces[-2:-1] if c >= chunks - 2 else [])
            done = chain(r, r == pairs - 1, rows, side_alone, rates, own[c], peer[c], [both], after)
            if r < pairs - 1:
                both = lax.ppermute(done, "blk", onward)
                before = done
        even, moving = done
        odd[c] = (even, lax.ppermute(moving, "blk", onward))
        before = even
    before = complete(chunks - 1, [before] + pieces[-1:])
    if begin < chunks - 1:
        total = bring_together(begin, chunks - 1, total, False, [before])
    return bring_together(chunks - 1, chunks, total, True, [])


def solution(mesh):
    in_specs = (
        P("tones", None, None, "blk"),
        P("tones", None, None, "blk"),
        P("blk", None),
        P(),
        P(),
    )
    out_specs = P(("blk", "tones"), None, None, None)
    return jax.shard_map(
        on_device, mesh=mesh, in_specs=in_specs, out_specs=out_specs, check_vma=False
    )
```

```python
import functools

import jax
import jax.numpy as jnp
import ml_dtypes
import numpy as np
from jax import lax
from jax.experimental import pallas as pl
from jax.experimental.pallas import tpu as pltpu
from jax.sharding import PartitionSpec as P

F32 = jnp.float32
BF16 = jnp.bfloat16
VMEM_LIMIT = 56 * 1024 * 1024
HEAVY = pl.CostEstimate(flops=10**13, bytes_accessed=10**10, transcendentals=0)
ANY = pl.BlockSpec(memory_space=pl.ANY)
SMEM = pl.BlockSpec(memory_space=pltpu.SMEM)


def split(value):
    high = value.astype(BF16)
    return high, (value - high.astype(F32)).astype(BF16)


def dot(left, right, contract):
    return lax.dot_general(left, right, ((contract[:1], contract[1:]), ((), ())), preferred_element_type=F32)


def dot3(left, right, contract):
    left_high, left_low = left
    right_high, right_low = right
    return (
        dot(left_high, right_high, contract)
        + dot(left_high, right_low, contract)
        + dot(left_low, right_high, contract)
    )


def triangle(users):
    row = lax.broadcasted_iota(jnp.int32, (users, users), 0)
    column = lax.broadcasted_iota(jnp.int32, (users, users), 1)
    return row, column


def prepare_body(carry, blocks, base, pair, group, hop_offset, rates, chan, recv, *refs):
    outs = refs[len(refs) - blocks // 2 :]
    users = chan.shape[2]
    rows = recv.shape[2] // blocks

    def stacked(part):
        pieces = [chan[0, part]]
        for place in range(blocks):
            first_hop = 2 * pair[0] + (place % 2) - 2 * (place // 2)
            block = lax.rem(first_hop - hop_offset[group[0]] + 4 * blocks, blocks)
            first = pl.multiple_of(block * rows, 8)
            pieces.append(recv[0, part, pl.ds(first, rows), :])
        return split(jnp.concatenate(pieces, 0))

    left_real = stacked(0)
    left_imag = stacked(1)
    right = tuple(
        jnp.concatenate([real[:users], imag[:users]], 1) for real, imag in zip(left_real, left_imag)
    )
    real = dot3(tuple(jnp.concatenate(pair, 1) for pair in zip(left_real, left_imag)), right, (1, 1))
    imag = dot3(
        tuple(jnp.concatenate([b, -a], 1) for a, b in zip(left_real, left_imag)), right, (1, 1)
    )
    row, column = triangle(users)
    outs[0][0, :users] = jnp.where(row <= column, real[:users], imag[:users])
    for place in range(blocks):
        base = users if place < 2 else 0
        first = users + place * rows
        for part, value in enumerate((real, imag)):
            to = base + (2 * (place % 2) + part) * rows
            outs[place // 2][0, to : to + rows] = value[first : first + rows]
    if carry:
        lane = lax.broadcasted_iota(jnp.int32, (carry, users), 1)
        outs[0][0, users + 4 * rows :] = jnp.where(lane == 0, rates[0, 0], rates[0, 1])


def prepare(channel, received, step_sizes, scalars, start, count, blocks, carry, after):
    _, _, users, width = channel.shape
    symbols = received.shape[2]
    rows = symbols // blocks
    heights = [users + 4 * rows + carry] + [4 * rows] * (blocks // 2 - 1)
    return pl.pallas_call(
        functools.partial(prepare_body, carry, blocks),
        out_shape=[jax.ShapeDtypeStruct((count, height, users), F32) for height in heights],
        grid_spec=pltpu.PrefetchScalarGridSpec(
            num_scalar_prefetch=4,
            grid=(count,),
            in_specs=[
                SMEM,
                pl.BlockSpec((1, 2, users, width), lambda i, s, *_: (s[0] + start + i, 0, 0, 0)),
                pl.BlockSpec((1, 2, symbols, width), lambda i, s, *_: (s[0] + start + i, 0, 0, 0)),
            ]
            + [ANY] * len(after),
            out_specs=[pl.BlockSpec((1, height, users), lambda i, *_: (i, 0, 0)) for height in heights],
        ),
        compiler_params=pltpu.CompilerParams(vmem_limit_bytes=VMEM_LIMIT),
        cost_estimate=HEAVY,
        name="prepare",
    )(*scalars, step_sizes, channel, received, *after)


def unpack(packed, gram, sub):
    users = packed.shape[0]
    row, column = triangle(users)
    turned = packed.T
    real = split(jnp.where(row <= column, packed, turned))
    imag = split(jnp.where(row > column, packed, jnp.where(row < column, -turned, 0.0)))
    for part in range(2):
        gram[sub, part, :users, :users] = real[part]
        gram[sub, part, :users, users:] = imag[part]
        gram[sub, part, users:, :users] = -imag[part]
        gram[sub, part, users:, users:] = real[part]


def step(estimate, matched, gram, sub, rate):
    product = dot3(split(estimate), (gram[sub, 0], gram[sub, 1]), (1, 0))
    return jnp.tanh(estimate + rate * (matched - product))


def filtered(ref, base, rows, slot):
    first = base + 2 * slot * rows
    return jnp.concatenate([ref[0, first : first + rows], ref[0, first + rows : first + 2 * rows]], 1)


def chain_body(round_index, last, rows, side, rates, *refs):
    own, peer = refs[:2]
    users = own.shape[2]
    rest = refs[2:]
    base = users
    grams = (own, peer)
    if round_index:
        own, peer, came = rest[:3]
        base = 0
    gram, matched = refs[-2:]
    for packed, samples, sub in ((grams[0], own, side[0]), (grams[1], peer, 1 - side[0])):
        unpack(packed[0, :users], gram, sub)
        for slot in range(2):
            matched[sub, slot * rows : (slot + 1) * rows] = filtered(samples, base, rows, slot)

    if round_index == 0:
        even = jnp.tanh(rates[0, 0] * matched[0, :rows])
        even = step(even, matched[0, :rows], gram, 0, rates[0, 1])
        even = step(even, matched[1, :rows], gram, 1, rates[1, 0])
        odd = jnp.tanh(rates[1, 0] * matched[1, rows:])
        both = step(jnp.concatenate([even, odd], 0), matched[1], gram, 1, rates[1, 1])
    else:
        both = jnp.concatenate(
            [jnp.concatenate([came[0, slot, 0], came[0, slot, 1]], 1) for slot in range(2)], 0
        )
        for sub in range(2):
            for substep in range(2):
                both = step(both, matched[sub], gram, sub, rates[sub, substep])
    out = refs[-4:-2] if last else refs[-3:-2]
    for slot in range(2):
        for part in range(2):
            piece = both[slot * rows : (slot + 1) * rows, part * users : (part + 1) * users]
            if last:
                out[slot][0, part] = piece
            else:
                out[0][0, slot, part] = piece


def chain(round_index, last, rows, side, rates, own, peer, came, after):
    count, _, users = own[0].shape
    both_spec = pl.BlockSpec((1, 2, 2, rows, users), lambda i, s: (i, 0, 0, 0, 0))
    one_spec = pl.BlockSpec((1, 2, rows, users), lambda i, s: (i, 0, 0, 0))
    both_shape = jax.ShapeDtypeStruct((count, 2, 2, rows, users), F32)
    one_shape = jax.ShapeDtypeStruct((count, 2, rows, users), F32)
    inputs = [own[0], peer[0]]
    heights = [users if round_index else users + 4 * rows] * 2
    if round_index:
        inputs += [own[round_index], peer[round_index]]
        heights += [4 * rows] * 2
    specs = [pl.BlockSpec((1, height, users), lambda i, s: (i, 0, 0)) for height in heights]
    return pl.pallas_call(
        functools.partial(chain_body, round_index, last, rows),
        out_shape=[one_shape, one_shape] if last else both_shape,
        grid_spec=pltpu.PrefetchScalarGridSpec(
            num_scalar_prefetch=1,
            grid=(count,),
            in_specs=[SMEM] + specs + [both_spec] * len(came) + [ANY] * len(after),
            out_specs=[one_spec, one_spec] if last else both_spec,
            scratch_shapes=[
                pltpu.VMEM((2, 2, 2 * users, 2 * users), BF16),
                pltpu.VMEM((2, 2 * rows, 2 * users), F32),
            ],
        ),
        compiler_params=pltpu.CompilerParams(vmem_limit_bytes=VMEM_LIMIT),
        cost_estimate=HEAVY,
        name="chain%d" % round_index,
    )(side, rates, *inputs, *came, *after)


def finish_body(count, rows, scalars, rates, own, peer, even, odd, order, *refs):
    users = own.shape[2]
    out, gram, gathered = refs[-3:]
    tone = pl.program_id(0)
    side = scalars[0]
    even_slot = scalars[1]

    @pl.when(side == 0)
    def _():
        unpack(own[0, :users], gram, 0)

    @pl.when(side != 0)
    def _():
        unpack(peer[0, :users], gram, 0)

    matched = jnp.where(side == 0, filtered(own, users, rows, 1), filtered(peer, users, rows, 1))
    estimate = jnp.concatenate([odd[0, 0], odd[0, 1]], 1)
    for substep in range(2):
        estimate = step(estimate, matched, gram, 0, rates[0, substep])
    for part in range(2):
        first = (tone * 2 + part) * 2
        odd_row = pl.multiple_of((first + 1 - even_slot) * rows, 8)
        even_row = pl.multiple_of((first + even_slot) * rows, 8)
        gathered[pl.ds(odd_row, rows), :] = estimate[:, part * users : (part + 1) * users]
        gathered[pl.ds(even_row, rows), :] = even[0, part]

    @pl.when(tone == count - 1)
    def _():
        high, low = split(gathered[...])
        turned = dot(order[...], high, (1, 1)) + dot(order[...], low, (1, 1))
        out[...] = turned.reshape(out.shape)


def finish(rows, owners, scalars, rates, own, peer, even, odd, order, after):
    count, _, users = own[0].shape
    packed_spec = pl.BlockSpec((1, users + 4 * rows, users), lambda i, s: (i, 0, 0))
    one_spec = pl.BlockSpec((1, 2, rows, users), lambda i, s: (i, 0, 0, 0))
    shape = (owners, users // owners, count * 4 * rows)
    return pl.pallas_call(
        functools.partial(finish_body, count, rows),
        out_shape=jax.ShapeDtypeStruct(shape, F32),
        grid_spec=pltpu.PrefetchScalarGridSpec(
            num_scalar_prefetch=1,
            grid=(count,),
            in_specs=[
                SMEM,
                packed_spec,
                packed_spec,
                one_spec,
                one_spec,
                pl.BlockSpec((users, users), lambda i, s: (0, 0)),
            ]
            + [ANY] * len(after),
            out_specs=pl.BlockSpec(shape, lambda i, s: (0, 0, 0)),
            scratch_shapes=[
                pltpu.VMEM((1, 2, 2 * users, 2 * users), BF16),
                pltpu.VMEM((count * 4 * rows, users), F32),
            ],
        ),
        compiler_params=pltpu.CompilerParams(vmem_limit_bytes=VMEM_LIMIT),
        cost_estimate=HEAVY,
        name="finish",
    )(scalars, rates, own[0], peer[0], even, odd, order, *after)


def held_back(value, after):
    return pl.pallas_call(
        lambda *refs: None,
        out_shape=jax.ShapeDtypeStruct(value.shape, value.dtype),
        in_specs=[ANY] * (1 + len(after)),
        out_specs=ANY,
        input_output_aliases={0: 0},
        compiler_params=pltpu.CompilerParams(vmem_limit_bytes=VMEM_LIMIT),
        cost_estimate=HEAVY,
        name="held_back",
    )(value, *after)


def despread_body(groups, sizes, rows, folded, first, last, source, table, *refs):
    pieces = refs[: len(sizes)]
    if not first:
        total = refs[len(sizes)]
    out, tones_first, symbols_first, held, arrived, left = refs[-6:]
    tones = sum(sizes)
    items, _, _, length = held.shape
    blocks = tones_first.shape[0]

    def fetch(item):
        return pltpu.make_async_copy(total.at[item], held.at[item], arrived.at[item])

    def store(item):
        return pltpu.make_async_copy(held.at[item], out.at[item], left.at[item])

    if not first:
        for item in range(items):
            fetch(item).start()
    for block in range(blocks):

        def gather(group, carry):
            position = source[block * groups + group]
            for side in range(2):
                place = (group * 2 + side) * tones * 2
                src = (2 * position + side) * groups + group
                for piece, size in zip(pieces, sizes):
                    for tone in range(2 * size):
                        lane = (tone * 2 + block % 2) * rows
                        tones_first[block, place + tone, :, :rows] = piece[src, :, lane : lane + rows]
                    place = place + 2 * size
            return carry

        lax.fori_loop(0, groups, gather, 0)

    for item in range(items):
        despread_item(rows, folded, first, last, item, table, tones_first, symbols_first, held, fetch)
        store(item).start()
    for item in range(items):
        store(item).wait()


def despread_item(rows, folded, first, last, item, table, tones_first, symbols_first, held, fetch):
    length = held.shape[3]
    blocks = tones_first.shape[0]
    for block in range(blocks):
        value = tones_first[block, :, item, :]
        here = slice(block * rows, (block + 1) * rows)
        if folded:
            high = value.astype(BF16).astype(F32)
            joined = jnp.concatenate([high, high, value - high], 0)
            symbols_first[0, here] = joined.T[:rows].astype(BF16)
        else:
            high, low = split(value.T[:rows])
            symbols_first[0, here] = high
            symbols_first[1, here] = low
    if folded:
        result = dot(symbols_first[0], table[0], (1, 0))
    else:
        result = dot3((symbols_first[0], symbols_first[1]), (table[0], table[1]), (1, 0))
    if not first:
        fetch(item).wait()
    for part in range(2):
        value = result[:, part * length : (part + 1) * length]
        if not first:
            value = value + held[item, part]
        held[item, part] = jnp.tanh(value) if last else value


def despread(pieces, starts, groups, half, blocks, rows, source, total, last, after):
    items = pieces[0].shape[1]
    length = groups * 2 * half
    lanes = -(-rows // 128) * 128
    sizes = [piece.shape[2] // (4 * rows) for piece in pieces]
    local = np.concatenate([np.arange(begin, begin + size) for begin, size in zip(starts, sizes)])
    index = (np.arange(groups * 2)[:, None] * half + local[None, :]).reshape(-1)
    angle = 2.0 * np.pi / length * (index[:, None] * np.arange(length)[None, :] % length)
    cosine, sine = np.cos(angle) / np.sqrt(length), np.sin(angle) / np.sqrt(length)
    real, imag = np.concatenate([cosine, sine], 1), np.concatenate([-sine, cosine], 1)
    table = np.stack([real, imag], 1).reshape(1, 2 * len(index), 2 * length)
    high = table.astype(ml_dtypes.bfloat16)
    low = (table - high.astype(np.float64)).astype(ml_dtypes.bfloat16)
    depth = table.shape[1]
    folded = 3 * depth <= 256
    table = np.concatenate([high, low, high], 1) if folded else np.concatenate([high, low], 0)
    symbols = blocks * rows
    totals = [] if total is None else [total]
    return pl.pallas_call(
        functools.partial(despread_body, groups, sizes, rows, folded, total is None, last),
        out_shape=jax.ShapeDtypeStruct((items, 2, symbols, length), F32),
        grid_spec=pltpu.PrefetchScalarGridSpec(
            num_scalar_prefetch=1,
            grid=(1,),
            in_specs=[pl.BlockSpec(table.shape, lambda i, s: (0, 0, 0))]
            + [pl.BlockSpec(piece.shape, lambda i, s: (0, 0, 0)) for piece in pieces]
            + [ANY] * len(totals)
            + [ANY] * len(after),
            out_specs=ANY,
            scratch_shapes=[
                pltpu.VMEM((blocks, depth, items, lanes), F32),
                pltpu.VMEM((table.shape[0], symbols, table.shape[1]), BF16),
                pltpu.VMEM((items, 2, symbols, length), F32),
                pltpu.SemaphoreType.DMA((items,)),
                pltpu.SemaphoreType.DMA((items,)),
            ],
        ),
        compiler_params=pltpu.CompilerParams(vmem_limit_bytes=VMEM_LIMIT),
        cost_estimate=HEAVY,
        name="despread",
    )(source, jnp.asarray(table), *pieces, *totals, *after)


def on_device(channel, received, step_sizes, hop_offset, user_order):
    blocks = lax.axis_size("blk")
    groups = lax.axis_size("tones")
    pairs = blocks // 2
    half = channel.shape[0] // 2
    users = channel.shape[2]
    rows = received.shape[2] // blocks
    owners = blocks * groups
    position = lax.axis_index("blk")
    offset = hop_offset[lax.axis_index("tones")]
    side = position % 2
    pair = position // 2

    swap = [(p, p ^ 1) for p in range(blocks)]
    onward = [(p, (p + 2) % blocks) for p in range(blocks)]

    doubles = max((half - 4) // 2, 0)
    sizes = [1] + [2] * doubles + [1] * (half - 1 - 2 * doubles)
    starts = [sum(sizes[:c]) for c in range(len(sizes))]
    chunks = len(sizes)

    place = (pair.reshape(1), lax.axis_index("tones").reshape(1), hop_offset)
    side_alone = side.reshape(1)
    side_and_slot = jnp.stack([side, offset % 2])
    order = (user_order[:, None] == jnp.arange(users, dtype=jnp.int32)[None, :]).astype(BF16)

    begins = (jnp.arange(blocks, dtype=jnp.int32)[:, None] + hop_offset[None, :]) % blocks
    source = jnp.where(begins % 2 == 0, begins // 2 + pairs - 1, begins // 2) % pairs

    own, peer, later, odd, pieces = {}, {}, {}, {}, []

    def ready(c, first_tone, carry, after):
        scalars = (first_tone.reshape(1),) + place
        return prepare(
            channel, received, step_sizes, scalars, starts[c], sizes[c], blocks, carry, after
        )

    def ready_peer(c, after):
        sent = ready(c, (1 - side) * half, 8 if c == 0 else 0, after)
        peer[c] = [lax.ppermute(sent[0], "blk", swap)]
        later[c] = sent[1:]
        return sent[0]

    def send_later(c, after):
        for value in later[c]:
            value = held_back(value, after)
            peer[c].append(lax.ppermute(value, "blk", swap))
            after = [value]
        return after[0]

    def ready_own(c, after):
        own[c] = ready(c, side * half, 0, after)
        return own[c][0]

    def complete(c, after):
        even, moved = odd[c]
        done = finish(rows, owners, side_and_slot, rates, own[c], peer[c], even, moved, order, after)
        pieces.append(
            lax.all_to_all(done, ("blk", "tones"), split_axis=0, concat_axis=0, tiled=True)
        )
        return done

    def bring_together(begin, end, total, last, after):
        return despread(
            pieces[begin:end],
            starts[begin:end],
            groups,
            half,
            blocks,
            rows,
            source.reshape(-1),
            total,
            last,
            after,
        )

    before = ready_peer(0, [])
    before = send_later(0, [before])
    if chunks > 1:
        before = ready_peer(1, [before])
    before = ready_own(0, [before])
    peer_rates = peer[0][0][0, users + 4 * rows, :2].reshape(1, 2)
    rates = jnp.where(
        side == 0,
        jnp.concatenate([step_sizes, peer_rates], 0),
        jnp.concatenate([peer_rates, step_sizes], 0),
    )
    ahead = {c: [c + 1] for c in range(chunks - 1)}
    parts = {}
    if chunks > 8:
        for c in (chunks - 2, chunks - 1):
            ahead[c - 1].remove(c)
            ahead[c - 5].append(c)
        parts = {chunks - 5: chunks - 7, chunks - 4: chunks - 6}
    begin, total = 0, None
    for c in range(chunks):
        before = chain(0, False, rows, side_alone, rates, own[c], peer[c], [], [before])
        both = lax.ppermute(before, "blk", onward)
        if c in parts:
            total = bring_together(begin, parts[c], total, False, [before])
            begin, before = parts[c], total
        if c > 0:
            before = complete(c - 1, [before] + ([] if c >= chunks - 2 else pieces[-1:]))
        if c + 1 < chunks:
            before = send_later(c + 1, [before])
        if c + 2 < chunks:
            before = ready_peer(c + 2, [before])
        for other in ahead.get(c, []):
            before = ready_own(other, [before])
        for r in range(1, pairs):
            after = [before] + (pieces[-2:-1] if c >= chunks - 2 else [])
            done = chain(r, r == pairs - 1, rows, side_alone, rates, own[c], peer[c], [both], after)
            if r < pairs - 1:
                both = lax.ppermute(done, "blk", onward)
                before = done
        even, moving = done
        odd[c] = (even, lax.ppermute(moving, "blk", onward))
        before = even
    before = complete(chunks - 1, [before] + pieces[-1:])
    if begin < chunks - 1:
        total = bring_together(begin, chunks - 1, total, False, [before])
    return bring_together(chunks - 1, chunks, total, True, [])


def solution(mesh):
    in_specs = (
        P("tones", None, None, "blk"),
        P("tones", None, None, "blk"),
        P("blk", None),
        P(),
        P(),
    )
    out_specs = P(("blk", "tones"), None, None, None)
    return jax.shard_map(
        on_device, mesh=mesh, in_specs=in_specs, out_specs=out_specs, check_vma=False
    )
```

```python
import functools

import jax
import jax.numpy as jnp
import ml_dtypes
import numpy as np
from jax import lax
from jax.experimental import pallas as pl
from jax.experimental.pallas import tpu as pltpu
from jax.sharding import PartitionSpec as P

F32 = jnp.float32
BF16 = jnp.bfloat16
VMEM_LIMIT = 56 * 1024 * 1024
HEAVY = pl.CostEstimate(flops=10**13, bytes_accessed=10**10, transcendentals=0)
ANY = pl.BlockSpec(memory_space=pl.ANY)
SMEM = pl.BlockSpec(memory_space=pltpu.SMEM)


def split(value):
    high = value.astype(BF16)
    return high, (value - high.astype(F32)).astype(BF16)


def dot(left, right, contract):
    return lax.dot_general(left, right, ((contract[:1], contract[1:]), ((), ())), preferred_element_type=F32)


def dot3(left, right, contract):
    left_high, left_low = left
    right_high, right_low = right
    return (
        dot(left_high, right_high, contract)
        + dot(left_high, right_low, contract)
        + dot(left_low, right_high, contract)
    )


def triangle(users):
    row = lax.broadcasted_iota(jnp.int32, (users, users), 0)
    column = lax.broadcasted_iota(jnp.int32, (users, users), 1)
    return row, column


def prepare_body(carry, blocks, base, pair, group, hop_offset, rates, chan, recv, *refs):
    outs = refs[len(refs) - blocks // 2 :]
    users = chan.shape[2]
    rows = recv.shape[2] // blocks

    def stacked(part):
        pieces = [chan[0, part]]
        for place in range(blocks):
            first_hop = 2 * pair[0] + (place % 2) - 2 * (place // 2)
            block = lax.rem(first_hop - hop_offset[group[0]] + 4 * blocks, blocks)
            first = pl.multiple_of(block * rows, 8)
            pieces.append(recv[0, part, pl.ds(first, rows), :])
        return split(jnp.concatenate(pieces, 0))

    left_real = stacked(0)
    left_imag = stacked(1)
    right = tuple(
        jnp.concatenate([real[:users], imag[:users]], 1) for real, imag in zip(left_real, left_imag)
    )
    real = dot3(tuple(jnp.concatenate(pair, 1) for pair in zip(left_real, left_imag)), right, (1, 1))
    imag = dot3(
        tuple(jnp.concatenate([b, -a], 1) for a, b in zip(left_real, left_imag)), right, (1, 1)
    )
    row, column = triangle(users)
    outs[0][0, :users] = jnp.where(row <= column, real[:users], imag[:users])
    for place in range(blocks):
        base = users if place < 2 else 0
        first = users + place * rows
        for part, value in enumerate((real, imag)):
            to = base + (2 * (place % 2) + part) * rows
            outs[place // 2][0, to : to + rows] = value[first : first + rows]
    if carry:
        lane = lax.broadcasted_iota(jnp.int32, (carry, users), 1)
        outs[0][0, users + 4 * rows :] = jnp.where(lane == 0, rates[0, 0], rates[0, 1])


def prepare(channel, received, step_sizes, scalars, start, count, blocks, carry, after):
    _, _, users, width = channel.shape
    symbols = received.shape[2]
    rows = symbols // blocks
    heights = [users + 4 * rows + carry] + [4 * rows] * (blocks // 2 - 1)
    return pl.pallas_call(
        functools.partial(prepare_body, carry, blocks),
        out_shape=[jax.ShapeDtypeStruct((count, height, users), F32) for height in heights],
        grid_spec=pltpu.PrefetchScalarGridSpec(
            num_scalar_prefetch=4,
            grid=(count,),
            in_specs=[
                SMEM,
                pl.BlockSpec((1, 2, users, width), lambda i, s, *_: (s[0] + start + i, 0, 0, 0)),
                pl.BlockSpec((1, 2, symbols, width), lambda i, s, *_: (s[0] + start + i, 0, 0, 0)),
            ]
            + [ANY] * len(after),
            out_specs=[pl.BlockSpec((1, height, users), lambda i, *_: (i, 0, 0)) for height in heights],
        ),
        compiler_params=pltpu.CompilerParams(vmem_limit_bytes=VMEM_LIMIT),
        cost_estimate=HEAVY,
        name="prepare",
    )(*scalars, step_sizes, channel, received, *after)


def unpack(packed, gram, sub):
    users = packed.shape[0]
    row, column = triangle(users)
    turned = packed.T
    real = split(jnp.where(row <= column, packed, turned))
    imag = split(jnp.where(row > column, packed, jnp.where(row < column, -turned, 0.0)))
    for part in range(2):
        gram[sub, part, :users, :users] = real[part]
        gram[sub, part, :users, users:] = imag[part]
        gram[sub, part, users:, :users] = -imag[part]
        gram[sub, part, users:, users:] = real[part]


def step(estimate, matched, gram, sub, rate):
    product = dot3(split(estimate), (gram[sub, 0], gram[sub, 1]), (1, 0))
    return jnp.tanh(estimate + rate * (matched - product))


def filtered(ref, base, rows, slot):
    first = base + 2 * slot * rows
    return jnp.concatenate([ref[0, first : first + rows], ref[0, first + rows : first + 2 * rows]], 1)


def chain_body(round_index, last, rows, side, rates, *refs):
    own, peer = refs[:2]
    users = own.shape[2]
    rest = refs[2:]
    base = users
    grams = (own, peer)
    if round_index:
        own, peer, came = rest[:3]
        base = 0
    gram, matched = refs[-2:]
    for packed, samples, sub in ((grams[0], own, side[0]), (grams[1], peer, 1 - side[0])):
        unpack(packed[0, :users], gram, sub)
        for slot in range(2):
            matched[sub, slot * rows : (slot + 1) * rows] = filtered(samples, base, rows, slot)

    if round_index == 0:
        even = jnp.tanh(rates[0, 0] * matched[0, :rows])
        even = step(even, matched[0, :rows], gram, 0, rates[0, 1])
        even = step(even, matched[1, :rows], gram, 1, rates[1, 0])
        odd = jnp.tanh(rates[1, 0] * matched[1, rows:])
        both = step(jnp.concatenate([even, odd], 0), matched[1], gram, 1, rates[1, 1])
    else:
        both = jnp.concatenate(
            [jnp.concatenate([came[0, slot, 0], came[0, slot, 1]], 1) for slot in range(2)], 0
        )
        for sub in range(2):
            for substep in range(2):
                both = step(both, matched[sub], gram, sub, rates[sub, substep])
    out = refs[-4:-2] if last else refs[-3:-2]
    for slot in range(2):
        for part in range(2):
            piece = both[slot * rows : (slot + 1) * rows, part * users : (part + 1) * users]
            if last:
                out[slot][0, part] = piece
            else:
                out[0][0, slot, part] = piece


def chain(round_index, last, rows, side, rates, own, peer, came, after):
    count, _, users = own[0].shape
    both_spec = pl.BlockSpec((1, 2, 2, rows, users), lambda i, s: (i, 0, 0, 0, 0))
    one_spec = pl.BlockSpec((1, 2, rows, users), lambda i, s: (i, 0, 0, 0))
    both_shape = jax.ShapeDtypeStruct((count, 2, 2, rows, users), F32)
    one_shape = jax.ShapeDtypeStruct((count, 2, rows, users), F32)
    inputs = [own[0], peer[0]]
    heights = [users if round_index else users + 4 * rows] * 2
    if round_index:
        inputs += [own[round_index], peer[round_index]]
        heights += [4 * rows] * 2
    specs = [pl.BlockSpec((1, height, users), lambda i, s: (i, 0, 0)) for height in heights]
    return pl.pallas_call(
        functools.partial(chain_body, round_index, last, rows),
        out_shape=[one_shape, one_shape] if last else both_shape,
        grid_spec=pltpu.PrefetchScalarGridSpec(
            num_scalar_prefetch=1,
            grid=(count,),
            in_specs=[SMEM] + specs + [both_spec] * len(came) + [ANY] * len(after),
            out_specs=[one_spec, one_spec] if last else both_spec,
            scratch_shapes=[
                pltpu.VMEM((2, 2, 2 * users, 2 * users), BF16),
                pltpu.VMEM((2, 2 * rows, 2 * users), F32),
            ],
        ),
        compiler_params=pltpu.CompilerParams(vmem_limit_bytes=VMEM_LIMIT),
        cost_estimate=HEAVY,
        name="chain%d" % round_index,
    )(side, rates, *inputs, *came, *after)


def finish_body(count, rows, scalars, rates, own, peer, even, odd, order, *refs):
    users = own.shape[2]
    out, gram, gathered = refs[-3:]
    tone = pl.program_id(0)
    side = scalars[0]
    even_slot = scalars[1]

    @pl.when(side == 0)
    def _():
        unpack(own[0, :users], gram, 0)

    @pl.when(side != 0)
    def _():
        unpack(peer[0, :users], gram, 0)

    matched = jnp.where(side == 0, filtered(own, users, rows, 1), filtered(peer, users, rows, 1))
    estimate = jnp.concatenate([odd[0, 0], odd[0, 1]], 1)
    for substep in range(2):
        estimate = step(estimate, matched, gram, 0, rates[0, substep])
    for part in range(2):
        first = (tone * 2 + part) * 2
        odd_row = pl.multiple_of((first + 1 - even_slot) * rows, 8)
        even_row = pl.multiple_of((first + even_slot) * rows, 8)
        gathered[pl.ds(odd_row, rows), :] = estimate[:, part * users : (part + 1) * users]
        gathered[pl.ds(even_row, rows), :] = even[0, part]

    @pl.when(tone == count - 1)
    def _():
        high, low = split(gathered[...])
        turned = dot(order[...], high, (1, 1)) + dot(order[...], low, (1, 1))
        out[...] = turned.reshape(out.shape)


def finish(rows, owners, scalars, rates, own, peer, even, odd, order, after):
    count, _, users = own[0].shape
    packed_spec = pl.BlockSpec((1, users + 4 * rows, users), lambda i, s: (i, 0, 0))
    one_spec = pl.BlockSpec((1, 2, rows, users), lambda i, s: (i, 0, 0, 0))
    shape = (owners, users // owners, count * 4 * rows)
    return pl.pallas_call(
        functools.partial(finish_body, count, rows),
        out_shape=jax.ShapeDtypeStruct(shape, F32),
        grid_spec=pltpu.PrefetchScalarGridSpec(
            num_scalar_prefetch=1,
            grid=(count,),
            in_specs=[
                SMEM,
                packed_spec,
                packed_spec,
                one_spec,
                one_spec,
                pl.BlockSpec((users, users), lambda i, s: (0, 0)),
            ]
            + [ANY] * len(after),
            out_specs=pl.BlockSpec(shape, lambda i, s: (0, 0, 0)),
            scratch_shapes=[
                pltpu.VMEM((1, 2, 2 * users, 2 * users), BF16),
                pltpu.VMEM((count * 4 * rows, users), F32),
            ],
        ),
        compiler_params=pltpu.CompilerParams(vmem_limit_bytes=VMEM_LIMIT),
        cost_estimate=HEAVY,
        name="finish",
    )(scalars, rates, own[0], peer[0], even, odd, order, *after)


def held_back(value, after):
    return pl.pallas_call(
        lambda *refs: None,
        out_shape=jax.ShapeDtypeStruct(value.shape, value.dtype),
        in_specs=[ANY] * (1 + len(after)),
        out_specs=ANY,
        input_output_aliases={0: 0},
        compiler_params=pltpu.CompilerParams(vmem_limit_bytes=VMEM_LIMIT),
        cost_estimate=HEAVY,
        name="held_back",
    )(value, *after)


def despread_body(groups, sizes, rows, folded, first, last, source, table, *refs):
    pieces = refs[: len(sizes)]
    if not first:
        total = refs[len(sizes)]
    out, tones_first, symbols_first, held, arrived, left = refs[-6:]
    tones = sum(sizes)
    items, _, _, length = held.shape
    blocks = tones_first.shape[0]

    def fetch(item):
        return pltpu.make_async_copy(total.at[item], held.at[item], arrived.at[item])

    def store(item):
        return pltpu.make_async_copy(held.at[item], out.at[item], left.at[item])

    if not first:
        for item in range(items):
            fetch(item).start()
    for block in range(blocks):

        def gather(group, carry):
            position = source[block * groups + group]
            for side in range(2):
                place = (group * 2 + side) * tones * 2
                src = (2 * position + side) * groups + group
                for piece, size in zip(pieces, sizes):
                    for tone in range(2 * size):
                        lane = (tone * 2 + block % 2) * rows
                        tones_first[block, place + tone, :, :rows] = piece[src, :, lane : lane + rows]
                    place = place + 2 * size
            return carry

        lax.fori_loop(0, groups, gather, 0)

    for item in range(items):
        despread_item(rows, folded, first, last, item, table, tones_first, symbols_first, held, fetch)
        store(item).start()
    for item in range(items):
        store(item).wait()


def despread_item(rows, folded, first, last, item, table, tones_first, symbols_first, held, fetch):
    length = held.shape[3]
    blocks = tones_first.shape[0]
    for block in range(blocks):
        value = tones_first[block, :, item, :]
        here = slice(block * rows, (block + 1) * rows)
        if folded:
            high = value.astype(BF16).astype(F32)
            joined = jnp.concatenate([high, high, value - high], 0)
            symbols_first[0, here] = joined.T[:rows].astype(BF16)
        else:
            high, low = split(value.T[:rows])
            symbols_first[0, here] = high
            symbols_first[1, here] = low
    if folded:
        result = dot(symbols_first[0], table[0], (1, 0))
    else:
        result = dot3((symbols_first[0], symbols_first[1]), (table[0], table[1]), (1, 0))
    if not first:
        fetch(item).wait()
    for part in range(2):
        value = result[:, part * length : (part + 1) * length]
        if not first:
            value = value + held[item, part]
        held[item, part] = jnp.tanh(value) if last else value


def despread(pieces, starts, groups, half, blocks, rows, source, total, last, after):
    items = pieces[0].shape[1]
    length = groups * 2 * half
    lanes = -(-rows // 128) * 128
    sizes = [piece.shape[2] // (4 * rows) for piece in pieces]
    local = np.concatenate([np.arange(begin, begin + size) for begin, size in zip(starts, sizes)])
    index = (np.arange(groups * 2)[:, None] * half + local[None, :]).reshape(-1)
    angle = 2.0 * np.pi / length * (index[:, None] * np.arange(length)[None, :] % length)
    cosine, sine = np.cos(angle) / np.sqrt(length), np.sin(angle) / np.sqrt(length)
    real, imag = np.concatenate([cosine, sine], 1), np.concatenate([-sine, cosine], 1)
    table = np.stack([real, imag], 1).reshape(1, 2 * len(index), 2 * length)
    high = table.astype(ml_dtypes.bfloat16)
    low = (table - high.astype(np.float64)).astype(ml_dtypes.bfloat16)
    depth = table.shape[1]
    folded = 3 * depth <= 256
    table = np.concatenate([high, low, high], 1) if folded else np.concatenate([high, low], 0)
    symbols = blocks * rows
    totals = [] if total is None else [total]
    return pl.pallas_call(
        functools.partial(despread_body, groups, sizes, rows, folded, total is None, last),
        out_shape=jax.ShapeDtypeStruct((items, 2, symbols, length), F32),
        grid_spec=pltpu.PrefetchScalarGridSpec(
            num_scalar_prefetch=1,
            grid=(1,),
            in_specs=[pl.BlockSpec(table.shape, lambda i, s: (0, 0, 0))]
            + [pl.BlockSpec(piece.shape, lambda i, s: (0, 0, 0)) for piece in pieces]
            + [ANY] * len(totals)
            + [ANY] * len(after),
            out_specs=ANY,
            scratch_shapes=[
                pltpu.VMEM((blocks, depth, items, lanes), F32),
                pltpu.VMEM((table.shape[0], symbols, table.shape[1]), BF16),
                pltpu.VMEM((items, 2, symbols, length), F32),
                pltpu.SemaphoreType.DMA((items,)),
                pltpu.SemaphoreType.DMA((items,)),
            ],
        ),
        compiler_params=pltpu.CompilerParams(vmem_limit_bytes=VMEM_LIMIT),
        cost_estimate=HEAVY,
        name="despread",
    )(source, jnp.asarray(table), *pieces, *totals, *after)


def on_device(channel, received, step_sizes, hop_offset, user_order):
    blocks = lax.axis_size("blk")
    groups = lax.axis_size("tones")
    pairs = blocks // 2
    half = channel.shape[0] // 2
    users = channel.shape[2]
    rows = received.shape[2] // blocks
    owners = blocks * groups
    position = lax.axis_index("blk")
    offset = hop_offset[lax.axis_index("tones")]
    side = position % 2
    pair = position // 2

    swap = [(p, p ^ 1) for p in range(blocks)]
    onward = [(p, (p + 2) % blocks) for p in range(blocks)]

    doubles = max((half - 4) // 2, 0)
    sizes = [1] + [2] * doubles + [1] * (half - 1 - 2 * doubles)
    starts = [sum(sizes[:c]) for c in range(len(sizes))]
    chunks = len(sizes)

    place = (pair.reshape(1), lax.axis_index("tones").reshape(1), hop_offset)
    side_alone = side.reshape(1)
    side_and_slot = jnp.stack([side, offset % 2])
    order = (user_order[:, None] == jnp.arange(users, dtype=jnp.int32)[None, :]).astype(BF16)

    begins = (jnp.arange(blocks, dtype=jnp.int32)[:, None] + hop_offset[None, :]) % blocks
    source = jnp.where(begins % 2 == 0, begins // 2 + pairs - 1, begins // 2) % pairs

    own, peer, later, odd, pieces = {}, {}, {}, {}, []

    def ready(c, first_tone, carry, after):
        scalars = (first_tone.reshape(1),) + place
        return prepare(
            channel, received, step_sizes, scalars, starts[c], sizes[c], blocks, carry, after
        )

    def ready_peer(c, after):
        sent = ready(c, (1 - side) * half, 8 if c == 0 else 0, after)
        peer[c] = [lax.ppermute(sent[0], "blk", swap)]
        later[c] = sent[1:]
        return sent[0]

    def send_later(c, after):
        for value in later[c]:
            value = held_back(value, after)
            peer[c].append(lax.ppermute(value, "blk", swap))
            after = [value]
        return after[0]

    def ready_own(c, after):
        own[c] = ready(c, side * half, 0, after)
        return own[c][0]

    def complete(c, after):
        even, moved = odd[c]
        done = finish(rows, owners, side_and_slot, rates, own[c], peer[c], even, moved, order, after)
        pieces.append(
            lax.all_to_all(done, ("blk", "tones"), split_axis=0, concat_axis=0, tiled=True)
        )
        return done

    def bring_together(begin, end, total, last, after):
        return despread(
            pieces[begin:end],
            starts[begin:end],
            groups,
            half,
            blocks,
            rows,
            source.reshape(-1),
            total,
            last,
            after,
        )

    before = ready_peer(0, [])
    before = send_later(0, [before])
    if chunks > 1:
        before = ready_peer(1, [before])
    before = ready_own(0, [before])
    peer_rates = peer[0][0][0, users + 4 * rows, :2].reshape(1, 2)
    rates = jnp.where(
        side == 0,
        jnp.concatenate([step_sizes, peer_rates], 0),
        jnp.concatenate([peer_rates, step_sizes], 0),
    )
    ahead = {c: [c + 1] for c in range(chunks - 1)}
    parts = {}
    if chunks > 8:
        for c in range(chunks - 3, chunks):
            ahead[c - 1].remove(c)
            ahead[c - 5].append(c)
        parts = {chunks - 5: chunks - 6}
    begin, total = 0, None
    for c in range(chunks):
        before = chain(0, False, rows, side_alone, rates, own[c], peer[c], [], [before])
        both = lax.ppermute(before, "blk", onward)
        if c > 0:
            before = complete(c - 1, [before] + ([] if c >= chunks - 2 else pieces[-1:]))
        if c + 1 < chunks:
            before = send_later(c + 1, [before])
        if c + 2 < chunks:
            before = ready_peer(c + 2, [before])
        for other in ahead.get(c, []):
            before = ready_own(other, [before])
        for r in range(1, pairs):
            after = [before] + (pieces[-2:-1] if c >= chunks - 2 else [])
            done = chain(r, r == pairs - 1, rows, side_alone, rates, own[c], peer[c], [both], after)
            if r < pairs - 1:
                both = lax.ppermute(done, "blk", onward)
                before = done
        even, moving = done
        odd[c] = (even, lax.ppermute(moving, "blk", onward))
        before = even
        if c in parts:
            total = bring_together(begin, parts[c], total, False, [before])
            begin, before = parts[c], total
    before = complete(chunks - 1, [before] + pieces[-1:])
    if begin < chunks - 1:
        total = bring_together(begin, chunks - 1, total, False, [before])
    return bring_together(chunks - 1, chunks, total, True, [])


def solution(mesh):
    in_specs = (
        P("tones", None, None, "blk"),
        P("tones", None, None, "blk"),
        P("blk", None),
        P(),
        P(),
    )
    out_specs = P(("blk", "tones"), None, None, None)
    return jax.shard_map(
        on_device, mesh=mesh, in_specs=in_specs, out_specs=out_specs, check_vma=False
    )
```

```python
import functools

import jax
import jax.numpy as jnp
import ml_dtypes
import numpy as np
from jax import lax
from jax.experimental import pallas as pl
from jax.experimental.pallas import tpu as pltpu
from jax.sharding import PartitionSpec as P

F32 = jnp.float32
BF16 = jnp.bfloat16
VMEM_LIMIT = 56 * 1024 * 1024
HEAVY = pl.CostEstimate(flops=10**13, bytes_accessed=10**10, transcendentals=0)
ANY = pl.BlockSpec(memory_space=pl.ANY)
SMEM = pl.BlockSpec(memory_space=pltpu.SMEM)


def split(value):
    high = value.astype(BF16)
    return high, (value - high.astype(F32)).astype(BF16)


def dot(left, right, contract):
    return lax.dot_general(left, right, ((contract[:1], contract[1:]), ((), ())), preferred_element_type=F32)


def dot3(left, right, contract):
    left_high, left_low = left
    right_high, right_low = right
    return (
        dot(left_high, right_high, contract)
        + dot(left_high, right_low, contract)
        + dot(left_low, right_high, contract)
    )


def triangle(users):
    row = lax.broadcasted_iota(jnp.int32, (users, users), 0)
    column = lax.broadcasted_iota(jnp.int32, (users, users), 1)
    return row, column


def prepare_body(carry, blocks, base, pair, group, hop_offset, rates, chan, recv, *refs):
    outs = refs[len(refs) - blocks // 2 :]
    users = chan.shape[2]
    rows = recv.shape[2] // blocks

    def stacked(part):
        pieces = [chan[0, part]]
        for place in range(blocks):
            first_hop = 2 * pair[0] + (place % 2) - 2 * (place // 2)
            block = lax.rem(first_hop - hop_offset[group[0]] + 4 * blocks, blocks)
            first = pl.multiple_of(block * rows, 8)
            pieces.append(recv[0, part, pl.ds(first, rows), :])
        return split(jnp.concatenate(pieces, 0))

    left_real = stacked(0)
    left_imag = stacked(1)
    right = tuple(
        jnp.concatenate([real[:users], imag[:users]], 1) for real, imag in zip(left_real, left_imag)
    )
    real = dot3(tuple(jnp.concatenate(pair, 1) for pair in zip(left_real, left_imag)), right, (1, 1))
    imag = dot3(
        tuple(jnp.concatenate([b, -a], 1) for a, b in zip(left_real, left_imag)), right, (1, 1)
    )
    row, column = triangle(users)
    outs[0][0, :users] = jnp.where(row <= column, real[:users], imag[:users])
    for place in range(blocks):
        base = users if place < 2 else 0
        first = users + place * rows
        for part, value in enumerate((real, imag)):
            to = base + (2 * (place % 2) + part) * rows
            outs[place // 2][0, to : to + rows] = value[first : first + rows]
    if carry:
        lane = lax.broadcasted_iota(jnp.int32, (carry, users), 1)
        outs[0][0, users + 4 * rows :] = jnp.where(lane == 0, rates[0, 0], rates[0, 1])


def prepare(channel, received, step_sizes, scalars, start, count, blocks, carry, after):
    _, _, users, width = channel.shape
    symbols = received.shape[2]
    rows = symbols // blocks
    heights = [users + 4 * rows + carry] + [4 * rows] * (blocks // 2 - 1)
    return pl.pallas_call(
        functools.partial(prepare_body, carry, blocks),
        out_shape=[jax.ShapeDtypeStruct((count, height, users), F32) for height in heights],
        grid_spec=pltpu.PrefetchScalarGridSpec(
            num_scalar_prefetch=4,
            grid=(count,),
            in_specs=[
                SMEM,
                pl.BlockSpec((1, 2, users, width), lambda i, s, *_: (s[0] + start + i, 0, 0, 0)),
                pl.BlockSpec((1, 2, symbols, width), lambda i, s, *_: (s[0] + start + i, 0, 0, 0)),
            ]
            + [ANY] * len(after),
            out_specs=[pl.BlockSpec((1, height, users), lambda i, *_: (i, 0, 0)) for height in heights],
        ),
        compiler_params=pltpu.CompilerParams(vmem_limit_bytes=VMEM_LIMIT),
        cost_estimate=HEAVY,
        name="prepare",
    )(*scalars, step_sizes, channel, received, *after)


def unpack(packed, gram, sub):
    users = packed.shape[0]
    row, column = triangle(users)
    turned = packed.T
    real = split(jnp.where(row <= column, packed, turned))
    imag = split(jnp.where(row > column, packed, jnp.where(row < column, -turned, 0.0)))
    for part in range(2):
        gram[sub, part, :users, :users] = real[part]
        gram[sub, part, :users, users:] = imag[part]
        gram[sub, part, users:, :users] = -imag[part]
        gram[sub, part, users:, users:] = real[part]


def step(estimate, matched, gram, sub, rate):
    product = dot3(split(estimate), (gram[sub, 0], gram[sub, 1]), (1, 0))
    return jnp.tanh(estimate + rate * (matched - product))


def filtered(ref, base, rows, slot):
    first = base + 2 * slot * rows
    return jnp.concatenate([ref[0, first : first + rows], ref[0, first + rows : first + 2 * rows]], 1)


def chain_body(round_index, last, rows, side, rates, *refs):
    own, peer = refs[:2]
    users = own.shape[2]
    rest = refs[2:]
    base = users
    grams = (own, peer)
    if round_index:
        own, peer, came = rest[:3]
        base = 0
    gram, matched = refs[-2:]
    for packed, samples, sub in ((grams[0], own, side[0]), (grams[1], peer, 1 - side[0])):
        unpack(packed[0, :users], gram, sub)
        for slot in range(2):
            matched[sub, slot * rows : (slot + 1) * rows] = filtered(samples, base, rows, slot)

    if round_index == 0:
        even = jnp.tanh(rates[0, 0] * matched[0, :rows])
        even = step(even, matched[0, :rows], gram, 0, rates[0, 1])
        even = step(even, matched[1, :rows], gram, 1, rates[1, 0])
        odd = jnp.tanh(rates[1, 0] * matched[1, rows:])
        both = step(jnp.concatenate([even, odd], 0), matched[1], gram, 1, rates[1, 1])
    else:
        both = jnp.concatenate(
            [jnp.concatenate([came[0, slot, 0], came[0, slot, 1]], 1) for slot in range(2)], 0
        )
        for sub in range(2):
            for substep in range(2):
                both = step(both, matched[sub], gram, sub, rates[sub, substep])
    out = refs[-4:-2] if last else refs[-3:-2]
    for slot in range(2):
        for part in range(2):
            piece = both[slot * rows : (slot + 1) * rows, part * users : (part + 1) * users]
            if last:
                out[slot][0, part] = piece
            else:
                out[0][0, slot, part] = piece


def chain(round_index, last, rows, side, rates, own, peer, came, after):
    count, _, users = own[0].shape
    both_spec = pl.BlockSpec((1, 2, 2, rows, users), lambda i, s: (i, 0, 0, 0, 0))
    one_spec = pl.BlockSpec((1, 2, rows, users), lambda i, s: (i, 0, 0, 0))
    both_shape = jax.ShapeDtypeStruct((count, 2, 2, rows, users), F32)
    one_shape = jax.ShapeDtypeStruct((count, 2, rows, users), F32)
    inputs = [own[0], peer[0]]
    heights = [users if round_index else users + 4 * rows] * 2
    if round_index:
        inputs += [own[round_index], peer[round_index]]
        heights += [4 * rows] * 2
    specs = [pl.BlockSpec((1, height, users), lambda i, s: (i, 0, 0)) for height in heights]
    return pl.pallas_call(
        functools.partial(chain_body, round_index, last, rows),
        out_shape=[one_shape, one_shape] if last else both_shape,
        grid_spec=pltpu.PrefetchScalarGridSpec(
            num_scalar_prefetch=1,
            grid=(count,),
            in_specs=[SMEM] + specs + [both_spec] * len(came) + [ANY] * len(after),
            out_specs=[one_spec, one_spec] if last else both_spec,
            scratch_shapes=[
                pltpu.VMEM((2, 2, 2 * users, 2 * users), BF16),
                pltpu.VMEM((2, 2 * rows, 2 * users), F32),
            ],
        ),
        compiler_params=pltpu.CompilerParams(vmem_limit_bytes=VMEM_LIMIT),
        cost_estimate=HEAVY,
        name="chain%d" % round_index,
    )(side, rates, *inputs, *came, *after)


def finish_body(count, rows, scalars, rates, own, peer, even, odd, order, *refs):
    users = own.shape[2]
    out, gram, gathered = refs[-3:]
    tone = pl.program_id(0)
    side = scalars[0]
    even_slot = scalars[1]

    @pl.when(side == 0)
    def _():
        unpack(own[0, :users], gram, 0)

    @pl.when(side != 0)
    def _():
        unpack(peer[0, :users], gram, 0)

    matched = jnp.where(side == 0, filtered(own, users, rows, 1), filtered(peer, users, rows, 1))
    estimate = jnp.concatenate([odd[0, 0], odd[0, 1]], 1)
    for substep in range(2):
        estimate = step(estimate, matched, gram, 0, rates[0, substep])
    for part in range(2):
        first = (tone * 2 + part) * 2
        odd_row = pl.multiple_of((first + 1 - even_slot) * rows, 8)
        even_row = pl.multiple_of((first + even_slot) * rows, 8)
        gathered[pl.ds(odd_row, rows), :] = estimate[:, part * users : (part + 1) * users]
        gathered[pl.ds(even_row, rows), :] = even[0, part]

    @pl.when(tone == count - 1)
    def _():
        high, low = split(gathered[...])
        turned = dot(order[...], high, (1, 1)) + dot(order[...], low, (1, 1))
        out[...] = turned.reshape(out.shape)


def finish(rows, owners, scalars, rates, own, peer, even, odd, order, after):
    count, _, users = own[0].shape
    packed_spec = pl.BlockSpec((1, users + 4 * rows, users), lambda i, s: (i, 0, 0))
    one_spec = pl.BlockSpec((1, 2, rows, users), lambda i, s: (i, 0, 0, 0))
    shape = (owners, users // owners, count * 4 * rows)
    return pl.pallas_call(
        functools.partial(finish_body, count, rows),
        out_shape=jax.ShapeDtypeStruct(shape, F32),
        grid_spec=pltpu.PrefetchScalarGridSpec(
            num_scalar_prefetch=1,
            grid=(count,),
            in_specs=[
                SMEM,
                packed_spec,
                packed_spec,
                one_spec,
                one_spec,
                pl.BlockSpec((users, users), lambda i, s: (0, 0)),
            ]
            + [ANY] * len(after),
            out_specs=pl.BlockSpec(shape, lambda i, s: (0, 0, 0)),
            scratch_shapes=[
                pltpu.VMEM((1, 2, 2 * users, 2 * users), BF16),
                pltpu.VMEM((count * 4 * rows, users), F32),
            ],
        ),
        compiler_params=pltpu.CompilerParams(vmem_limit_bytes=VMEM_LIMIT),
        cost_estimate=HEAVY,
        name="finish",
    )(scalars, rates, own[0], peer[0], even, odd, order, *after)


def held_back(value, after):
    return pl.pallas_call(
        lambda *refs: None,
        out_shape=jax.ShapeDtypeStruct(value.shape, value.dtype),
        in_specs=[ANY] * (1 + len(after)),
        out_specs=ANY,
        input_output_aliases={0: 0},
        compiler_params=pltpu.CompilerParams(vmem_limit_bytes=VMEM_LIMIT),
        cost_estimate=HEAVY,
        name="held_back",
    )(value, *after)


def despread_body(groups, sizes, rows, folded, first, last, source, table, *refs):
    pieces = refs[: len(sizes)]
    if not first:
        total = refs[len(sizes)]
    out, tones_first, symbols_first, held, arrived, left = refs[-6:]
    tones = sum(sizes)
    items, _, _, length = held.shape
    blocks = tones_first.shape[0]

    def fetch(item):
        return pltpu.make_async_copy(total.at[item], held.at[item], arrived.at[item])

    def store(item):
        return pltpu.make_async_copy(held.at[item], out.at[item], left.at[item])

    if not first:
        for item in range(items):
            fetch(item).start()
    for block in range(blocks):

        def gather(group, carry):
            position = source[block * groups + group]
            for side in range(2):
                place = (group * 2 + side) * tones * 2
                src = (2 * position + side) * groups + group
                for piece, size in zip(pieces, sizes):
                    for tone in range(2 * size):
                        lane = (tone * 2 + block % 2) * rows
                        tones_first[block, place + tone, :, :rows] = piece[src, :, lane : lane + rows]
                    place = place + 2 * size
            return carry

        lax.fori_loop(0, groups, gather, 0)

    for item in range(items):
        despread_item(rows, folded, first, last, item, table, tones_first, symbols_first, held, fetch)
        store(item).start()
    for item in range(items):
        store(item).wait()


def despread_item(rows, folded, first, last, item, table, tones_first, symbols_first, held, fetch):
    length = held.shape[3]
    blocks = tones_first.shape[0]
    for block in range(blocks):
        value = tones_first[block, :, item, :]
        here = slice(block * rows, (block + 1) * rows)
        if folded:
            high = value.astype(BF16).astype(F32)
            joined = jnp.concatenate([high, high, value - high], 0)
            symbols_first[0, here] = joined.T[:rows].astype(BF16)
        else:
            high, low = split(value.T[:rows])
            symbols_first[0, here] = high
            symbols_first[1, here] = low
    if folded:
        result = dot(symbols_first[0], table[0], (1, 0))
    else:
        result = dot3((symbols_first[0], symbols_first[1]), (table[0], table[1]), (1, 0))
    if not first:
        fetch(item).wait()
    for part in range(2):
        value = result[:, part * length : (part + 1) * length]
        if not first:
            value = value + held[item, part]
        held[item, part] = jnp.tanh(value) if last else value


def despread(pieces, starts, groups, half, blocks, rows, source, total, last, after):
    items = pieces[0].shape[1]
    length = groups * 2 * half
    lanes = -(-rows // 128) * 128
    sizes = [piece.shape[2] // (4 * rows) for piece in pieces]
    local = np.concatenate([np.arange(begin, begin + size) for begin, size in zip(starts, sizes)])
    index = (np.arange(groups * 2)[:, None] * half + local[None, :]).reshape(-1)
    angle = 2.0 * np.pi / length * (index[:, None] * np.arange(length)[None, :] % length)
    cosine, sine = np.cos(angle) / np.sqrt(length), np.sin(angle) / np.sqrt(length)
    real, imag = np.concatenate([cosine, sine], 1), np.concatenate([-sine, cosine], 1)
    table = np.stack([real, imag], 1).reshape(1, 2 * len(index), 2 * length)
    high = table.astype(ml_dtypes.bfloat16)
    low = (table - high.astype(np.float64)).astype(ml_dtypes.bfloat16)
    depth = table.shape[1]
    folded = 3 * depth <= 256
    table = np.concatenate([high, low, high], 1) if folded else np.concatenate([high, low], 0)
    symbols = blocks * rows
    totals = [] if total is None else [total]
    return pl.pallas_call(
        functools.partial(despread_body, groups, sizes, rows, folded, total is None, last),
        out_shape=jax.ShapeDtypeStruct((items, 2, symbols, length), F32),
        grid_spec=pltpu.PrefetchScalarGridSpec(
            num_scalar_prefetch=1,
            grid=(1,),
            in_specs=[pl.BlockSpec(table.shape, lambda i, s: (0, 0, 0))]
            + [pl.BlockSpec(piece.shape, lambda i, s: (0, 0, 0)) for piece in pieces]
            + [ANY] * len(totals)
            + [ANY] * len(after),
            out_specs=ANY,
            scratch_shapes=[
                pltpu.VMEM((blocks, depth, items, lanes), F32),
                pltpu.VMEM((table.shape[0], symbols, table.shape[1]), BF16),
                pltpu.VMEM((items, 2, symbols, length), F32),
                pltpu.SemaphoreType.DMA((items,)),
                pltpu.SemaphoreType.DMA((items,)),
            ],
        ),
        compiler_params=pltpu.CompilerParams(vmem_limit_bytes=VMEM_LIMIT),
        cost_estimate=HEAVY,
        name="despread",
    )(source, jnp.asarray(table), *pieces, *totals, *after)


def on_device(channel, received, step_sizes, hop_offset, user_order):
    blocks = lax.axis_size("blk")
    groups = lax.axis_size("tones")
    pairs = blocks // 2
    half = channel.shape[0] // 2
    users = channel.shape[2]
    rows = received.shape[2] // blocks
    owners = blocks * groups
    position = lax.axis_index("blk")
    offset = hop_offset[lax.axis_index("tones")]
    side = position % 2
    pair = position // 2

    swap = [(p, p ^ 1) for p in range(blocks)]
    onward = [(p, (p + 2) % blocks) for p in range(blocks)]

    doubles = max((half - 2) // 2, 0)
    sizes = [1] + [2] * doubles + [1] * (half - 1 - 2 * doubles)
    starts = [sum(sizes[:c]) for c in range(len(sizes))]
    chunks = len(sizes)

    place = (pair.reshape(1), lax.axis_index("tones").reshape(1), hop_offset)
    side_alone = side.reshape(1)
    side_and_slot = jnp.stack([side, offset % 2])
    order = (user_order[:, None] == jnp.arange(users, dtype=jnp.int32)[None, :]).astype(BF16)

    begins = (jnp.arange(blocks, dtype=jnp.int32)[:, None] + hop_offset[None, :]) % blocks
    source = jnp.where(begins % 2 == 0, begins // 2 + pairs - 1, begins // 2) % pairs

    own, peer, later, odd, pieces = {}, {}, {}, {}, []

    def ready(c, first_tone, carry, after):
        scalars = (first_tone.reshape(1),) + place
        return prepare(
            channel, received, step_sizes, scalars, starts[c], sizes[c], blocks, carry, after
        )

    def ready_peer(c, after):
        sent = ready(c, (1 - side) * half, 8 if c == 0 else 0, after)
        peer[c] = [lax.ppermute(sent[0], "blk", swap)]
        later[c] = sent[1:]
        return sent[0]

    def send_later(c, after):
        for value in later[c]:
            value = held_back(value, after)
            peer[c].append(lax.ppermute(value, "blk", swap))
            after = [value]
        return after[0]

    def ready_own(c, after):
        own[c] = ready(c, side * half, 0, after)
        return own[c][0]

    def complete(c, after):
        even, moved = odd[c]
        done = finish(rows, owners, side_and_slot, rates, own[c], peer[c], even, moved, order, after)
        pieces.append(
            lax.all_to_all(done, ("blk", "tones"), split_axis=0, concat_axis=0, tiled=True)
        )
        return done

    def bring_together(begin, end, total, last, after):
        return despread(
            pieces[begin:end],
            starts[begin:end],
            groups,
            half,
            blocks,
            rows,
            source.reshape(-1),
            total,
            last,
            after,
        )

    before = ready_peer(0, [])
    before = send_later(0, [before])
    if chunks > 1:
        before = ready_peer(1, [before])
    before = ready_own(0, [before])
    peer_rates = peer[0][0][0, users + 4 * rows, :2].reshape(1, 2)
    rates = jnp.where(
        side == 0,
        jnp.concatenate([step_sizes, peer_rates], 0),
        jnp.concatenate([peer_rates, step_sizes], 0),
    )
    ahead = {c: [c + 1] for c in range(chunks - 1)}
    parts = {}
    if chunks > 8:
        for c in range(chunks - 3, chunks):
            ahead[c - 1].remove(c)
            ahead[c - 5].append(c)
        parts = {chunks - 4: chunks - 5}
    begin, total = 0, None
    for c in range(chunks):
        before = chain(0, False, rows, side_alone, rates, own[c], peer[c], [], [before])
        both = lax.ppermute(before, "blk", onward)
        if c > 0:
            before = complete(c - 1, [before] + ([] if c >= chunks - 2 else pieces[-1:]))
        if c + 1 < chunks:
            before = send_later(c + 1, [before])
        if c + 2 < chunks:
            before = ready_peer(c + 2, [before])
        for other in ahead.get(c, []):
            before = ready_own(other, [before])
        for r in range(1, pairs):
            after = [before] + (pieces[-2:-1] if c >= chunks - 2 else [])
            done = chain(r, r == pairs - 1, rows, side_alone, rates, own[c], peer[c], [both], after)
            if r < pairs - 1:
                both = lax.ppermute(done, "blk", onward)
                before = done
        even, moving = done
        odd[c] = (even, lax.ppermute(moving, "blk", onward))
        before = even
        if c in parts:
            total = bring_together(begin, parts[c], total, False, [before])
            begin, before = parts[c], total
    before = complete(chunks - 1, [before] + pieces[-1:])
    if begin < chunks - 1:
        total = bring_together(begin, chunks - 1, total, False, [before])
    return bring_together(chunks - 1, chunks, total, True, [])


def solution(mesh):
    in_specs = (
        P("tones", None, None, "blk"),
        P("tones", None, None, "blk"),
        P("blk", None),
        P(),
        P(),
    )
    out_specs = P(("blk", "tones"), None, None, None)
    return jax.shard_map(
        on_device, mesh=mesh, in_specs=in_specs, out_specs=out_specs, check_vma=False
    )
```

```python
import functools

import jax
import jax.numpy as jnp
import ml_dtypes
import numpy as np
from jax import lax
from jax.experimental import pallas as pl
from jax.experimental.pallas import tpu as pltpu
from jax.sharding import PartitionSpec as P

F32 = jnp.float32
BF16 = jnp.bfloat16
VMEM_LIMIT = 56 * 1024 * 1024
HEAVY = pl.CostEstimate(flops=10**13, bytes_accessed=10**10, transcendentals=0)
ANY = pl.BlockSpec(memory_space=pl.ANY)
SMEM = pl.BlockSpec(memory_space=pltpu.SMEM)


def split(value):
    high = value.astype(BF16)
    return high, (value - high.astype(F32)).astype(BF16)


def dot(left, right, contract):
    return lax.dot_general(left, right, ((contract[:1], contract[1:]), ((), ())), preferred_element_type=F32)


def dot3(left, right, contract):
    left_high, left_low = left
    right_high, right_low = right
    return (
        dot(left_high, right_high, contract)
        + dot(left_high, right_low, contract)
        + dot(left_low, right_high, contract)
    )


def triangle(users):
    row = lax.broadcasted_iota(jnp.int32, (users, users), 0)
    column = lax.broadcasted_iota(jnp.int32, (users, users), 1)
    return row, column


def prepare_body(carry, blocks, base, pair, group, hop_offset, rates, chan, recv, *refs):
    outs = refs[len(refs) - blocks // 2 :]
    users = chan.shape[2]
    rows = recv.shape[2] // blocks

    def stacked(part):
        pieces = [chan[0, part]]
        for place in range(blocks):
            first_hop = 2 * pair[0] + (place % 2) - 2 * (place // 2)
            block = lax.rem(first_hop - hop_offset[group[0]] + 4 * blocks, blocks)
            first = pl.multiple_of(block * rows, 8)
            pieces.append(recv[0, part, pl.ds(first, rows), :])
        return split(jnp.concatenate(pieces, 0))

    left_real = stacked(0)
    left_imag = stacked(1)
    right = tuple(
        jnp.concatenate([real[:users], imag[:users]], 1) for real, imag in zip(left_real, left_imag)
    )
    real = dot3(tuple(jnp.concatenate(pair, 1) for pair in zip(left_real, left_imag)), right, (1, 1))
    imag = dot3(
        tuple(jnp.concatenate([b, -a], 1) for a, b in zip(left_real, left_imag)), right, (1, 1)
    )
    row, column = triangle(users)
    outs[0][0, :users] = jnp.where(row <= column, real[:users], imag[:users])
    for place in range(blocks):
        base = users if place < 2 else 0
        first = users + place * rows
        for part, value in enumerate((real, imag)):
            to = base + (2 * (place % 2) + part) * rows
            outs[place // 2][0, to : to + rows] = value[first : first + rows]
    if carry:
        lane = lax.broadcasted_iota(jnp.int32, (carry, users), 1)
        outs[0][0, users + 4 * rows :] = jnp.where(lane == 0, rates[0, 0], rates[0, 1])


def prepare(channel, received, step_sizes, scalars, start, count, blocks, carry, after):
    _, _, users, width = channel.shape
    symbols = received.shape[2]
    rows = symbols // blocks
    heights = [users + 4 * rows + carry] + [4 * rows] * (blocks // 2 - 1)
    return pl.pallas_call(
        functools.partial(prepare_body, carry, blocks),
        out_shape=[jax.ShapeDtypeStruct((count, height, users), F32) for height in heights],
        grid_spec=pltpu.PrefetchScalarGridSpec(
            num_scalar_prefetch=4,
            grid=(count,),
            in_specs=[
                SMEM,
                pl.BlockSpec((1, 2, users, width), lambda i, s, *_: (s[0] + start + i, 0, 0, 0)),
                pl.BlockSpec((1, 2, symbols, width), lambda i, s, *_: (s[0] + start + i, 0, 0, 0)),
            ]
            + [ANY] * len(after),
            out_specs=[pl.BlockSpec((1, height, users), lambda i, *_: (i, 0, 0)) for height in heights],
        ),
        compiler_params=pltpu.CompilerParams(vmem_limit_bytes=VMEM_LIMIT),
        cost_estimate=HEAVY,
        name="prepare",
    )(*scalars, step_sizes, channel, received, *after)


def unpack(packed, gram, sub):
    users = packed.shape[0]
    row, column = triangle(users)
    turned = packed.T
    real = split(jnp.where(row <= column, packed, turned))
    imag = split(jnp.where(row > column, packed, jnp.where(row < column, -turned, 0.0)))
    for part in range(2):
        gram[sub, part, :users, :users] = real[part]
        gram[sub, part, :users, users:] = imag[part]
        gram[sub, part, users:, :users] = -imag[part]
        gram[sub, part, users:, users:] = real[part]


def step(estimate, matched, gram, sub, rate):
    product = dot3(split(estimate), (gram[sub, 0], gram[sub, 1]), (1, 0))
    return jnp.tanh(estimate + rate * (matched - product))


def filtered(ref, base, rows, slot):
    first = base + 2 * slot * rows
    return jnp.concatenate([ref[0, first : first + rows], ref[0, first + rows : first + 2 * rows]], 1)


def chain_body(round_index, last, rows, side, rates, *refs):
    own, peer = refs[:2]
    users = own.shape[2]
    rest = refs[2:]
    base = users
    grams = (own, peer)
    if round_index:
        own, peer, came = rest[:3]
        base = 0
    gram, matched = refs[-2:]
    for packed, samples, sub in ((grams[0], own, side[0]), (grams[1], peer, 1 - side[0])):
        unpack(packed[0, :users], gram, sub)
        for slot in range(2):
            matched[sub, slot * rows : (slot + 1) * rows] = filtered(samples, base, rows, slot)

    if round_index == 0:
        even = jnp.tanh(rates[0, 0] * matched[0, :rows])
        even = step(even, matched[0, :rows], gram, 0, rates[0, 1])
        even = step(even, matched[1, :rows], gram, 1, rates[1, 0])
        odd = jnp.tanh(rates[1, 0] * matched[1, rows:])
        both = step(jnp.concatenate([even, odd], 0), matched[1], gram, 1, rates[1, 1])
    else:
        both = jnp.concatenate(
            [jnp.concatenate([came[0, slot, 0], came[0, slot, 1]], 1) for slot in range(2)], 0
        )
        for sub in range(2):
            for substep in range(2):
                both = step(both, matched[sub], gram, sub, rates[sub, substep])
    out = refs[-4:-2] if last else refs[-3:-2]
    for slot in range(2):
        for part in range(2):
            piece = both[slot * rows : (slot + 1) * rows, part * users : (part + 1) * users]
            if last:
                out[slot][0, part] = piece
            else:
                out[0][0, slot, part] = piece


def chain(round_index, last, rows, side, rates, own, peer, came, after):
    count, _, users = own[0].shape
    both_spec = pl.BlockSpec((1, 2, 2, rows, users), lambda i, s: (i, 0, 0, 0, 0))
    one_spec = pl.BlockSpec((1, 2, rows, users), lambda i, s: (i, 0, 0, 0))
    both_shape = jax.ShapeDtypeStruct((count, 2, 2, rows, users), F32)
    one_shape = jax.ShapeDtypeStruct((count, 2, rows, users), F32)
    inputs = [own[0], peer[0]]
    heights = [users if round_index else users + 4 * rows] * 2
    if round_index:
        inputs += [own[round_index], peer[round_index]]
        heights += [4 * rows] * 2
    specs = [pl.BlockSpec((1, height, users), lambda i, s: (i, 0, 0)) for height in heights]
    return pl.pallas_call(
        functools.partial(chain_body, round_index, last, rows),
        out_shape=[one_shape, one_shape] if last else both_shape,
        grid_spec=pltpu.PrefetchScalarGridSpec(
            num_scalar_prefetch=1,
            grid=(count,),
            in_specs=[SMEM] + specs + [both_spec] * len(came) + [ANY] * len(after),
            out_specs=[one_spec, one_spec] if last else both_spec,
            scratch_shapes=[
                pltpu.VMEM((2, 2, 2 * users, 2 * users), BF16),
                pltpu.VMEM((2, 2 * rows, 2 * users), F32),
            ],
        ),
        compiler_params=pltpu.CompilerParams(vmem_limit_bytes=VMEM_LIMIT),
        cost_estimate=HEAVY,
        name="chain%d" % round_index,
    )(side, rates, *inputs, *came, *after)


def finish_body(count, rows, scalars, rates, own, peer, even, odd, order, *refs):
    users = own.shape[2]
    out, gram, gathered = refs[-3:]
    tone = pl.program_id(0)
    side = scalars[0]
    even_slot = scalars[1]

    @pl.when(side == 0)
    def _():
        unpack(own[0, :users], gram, 0)

    @pl.when(side != 0)
    def _():
        unpack(peer[0, :users], gram, 0)

    matched = jnp.where(side == 0, filtered(own, users, rows, 1), filtered(peer, users, rows, 1))
    estimate = jnp.concatenate([odd[0, 0], odd[0, 1]], 1)
    for substep in range(2):
        estimate = step(estimate, matched, gram, 0, rates[0, substep])
    for part in range(2):
        first = (tone * 2 + part) * 2
        odd_row = pl.multiple_of((first + 1 - even_slot) * rows, 8)
        even_row = pl.multiple_of((first + even_slot) * rows, 8)
        gathered[pl.ds(odd_row, rows), :] = estimate[:, part * users : (part + 1) * users]
        gathered[pl.ds(even_row, rows), :] = even[0, part]

    @pl.when(tone == count - 1)
    def _():
        high, low = split(gathered[...])
        turned = dot(order[...], high, (1, 1)) + dot(order[...], low, (1, 1))
        out[...] = turned.reshape(out.shape)


def finish(rows, owners, scalars, rates, own, peer, even, odd, order, after):
    count, _, users = own[0].shape
    packed_spec = pl.BlockSpec((1, users + 4 * rows, users), lambda i, s: (i, 0, 0))
    one_spec = pl.BlockSpec((1, 2, rows, users), lambda i, s: (i, 0, 0, 0))
    shape = (owners, users // owners, count * 4 * rows)
    return pl.pallas_call(
        functools.partial(finish_body, count, rows),
        out_shape=jax.ShapeDtypeStruct(shape, F32),
        grid_spec=pltpu.PrefetchScalarGridSpec(
            num_scalar_prefetch=1,
            grid=(count,),
            in_specs=[
                SMEM,
                packed_spec,
                packed_spec,
                one_spec,
                one_spec,
                pl.BlockSpec((users, users), lambda i, s: (0, 0)),
            ]
            + [ANY] * len(after),
            out_specs=pl.BlockSpec(shape, lambda i, s: (0, 0, 0)),
            scratch_shapes=[
                pltpu.VMEM((1, 2, 2 * users, 2 * users), BF16),
                pltpu.VMEM((count * 4 * rows, users), F32),
            ],
        ),
        compiler_params=pltpu.CompilerParams(vmem_limit_bytes=VMEM_LIMIT),
        cost_estimate=HEAVY,
        name="finish",
    )(scalars, rates, own[0], peer[0], even, odd, order, *after)


def held_back(value, after):
    return pl.pallas_call(
        lambda *refs: None,
        out_shape=jax.ShapeDtypeStruct(value.shape, value.dtype),
        in_specs=[ANY] * (1 + len(after)),
        out_specs=ANY,
        input_output_aliases={0: 0},
        compiler_params=pltpu.CompilerParams(vmem_limit_bytes=VMEM_LIMIT),
        cost_estimate=HEAVY,
        name="held_back",
    )(value, *after)


def despread_body(groups, sizes, rows, folded, first, last, source, table, *refs):
    pieces = refs[: len(sizes)]
    if not first:
        total = refs[len(sizes)]
    out, tones_first, symbols_first, held, arrived, left = refs[-6:]
    tones = sum(sizes)
    items, _, _, length = held.shape
    blocks = tones_first.shape[0]

    def fetch(item):
        return pltpu.make_async_copy(total.at[item], held.at[item], arrived.at[item])

    def store(item):
        return pltpu.make_async_copy(held.at[item], out.at[item], left.at[item])

    if not first:
        for item in range(items):
            fetch(item).start()
    for block in range(blocks):

        def gather(group, carry):
            position = source[block * groups + group]
            for side in range(2):
                place = (group * 2 + side) * tones * 2
                src = (2 * position + side) * groups + group
                for piece, size in zip(pieces, sizes):
                    for tone in range(2 * size):
                        lane = (tone * 2 + block % 2) * rows
                        tones_first[block, place + tone, :, :rows] = piece[src, :, lane : lane + rows]
                    place = place + 2 * size
            return carry

        lax.fori_loop(0, groups, gather, 0, unroll=folded)

    for item in range(items):
        despread_item(rows, folded, first, last, item, table, tones_first, symbols_first, held, fetch)
        store(item).start()
    for item in range(items):
        store(item).wait()


def despread_item(rows, folded, first, last, item, table, tones_first, symbols_first, held, fetch):
    length = held.shape[3]
    blocks = tones_first.shape[0]
    for block in range(blocks):
        value = tones_first[block, :, item, :]
        here = slice(block * rows, (block + 1) * rows)
        if folded:
            high = value.astype(BF16).astype(F32)
            joined = jnp.concatenate([high, high, value - high], 0)
            symbols_first[0, here] = joined.T[:rows].astype(BF16)
        else:
            high, low = split(value.T[:rows])
            symbols_first[0, here] = high
            symbols_first[1, here] = low
    if folded:
        result = dot(symbols_first[0], table[0], (1, 0))
    else:
        result = dot3((symbols_first[0], symbols_first[1]), (table[0], table[1]), (1, 0))
    if not first:
        fetch(item).wait()
    for part in range(2):
        value = result[:, part * length : (part + 1) * length]
        if not first:
            value = value + held[item, part]
        held[item, part] = jnp.tanh(value) if last else value


def despread(pieces, starts, groups, half, blocks, rows, source, total, last, after):
    items = pieces[0].shape[1]
    length = groups * 2 * half
    lanes = -(-rows // 128) * 128
    sizes = [piece.shape[2] // (4 * rows) for piece in pieces]
    local = np.concatenate([np.arange(begin, begin + size) for begin, size in zip(starts, sizes)])
    index = (np.arange(groups * 2)[:, None] * half + local[None, :]).reshape(-1)
    angle = 2.0 * np.pi / length * (index[:, None] * np.arange(length)[None, :] % length)
    cosine, sine = np.cos(angle) / np.sqrt(length), np.sin(angle) / np.sqrt(length)
    real, imag = np.concatenate([cosine, sine], 1), np.concatenate([-sine, cosine], 1)
    table = np.stack([real, imag], 1).reshape(1, 2 * len(index), 2 * length)
    high = table.astype(ml_dtypes.bfloat16)
    low = (table - high.astype(np.float64)).astype(ml_dtypes.bfloat16)
    depth = table.shape[1]
    folded = 3 * depth <= 256
    table = np.concatenate([high, low, high], 1) if folded else np.concatenate([high, low], 0)
    symbols = blocks * rows
    totals = [] if total is None else [total]
    return pl.pallas_call(
        functools.partial(despread_body, groups, sizes, rows, folded, total is None, last),
        out_shape=jax.ShapeDtypeStruct((items, 2, symbols, length), F32),
        grid_spec=pltpu.PrefetchScalarGridSpec(
            num_scalar_prefetch=1,
            grid=(1,),
            in_specs=[pl.BlockSpec(table.shape, lambda i, s: (0, 0, 0))]
            + [pl.BlockSpec(piece.shape, lambda i, s: (0, 0, 0)) for piece in pieces]
            + [ANY] * len(totals)
            + [ANY] * len(after),
            out_specs=ANY,
            scratch_shapes=[
                pltpu.VMEM((blocks, depth, items, lanes), F32),
                pltpu.VMEM((table.shape[0], symbols, table.shape[1]), BF16),
                pltpu.VMEM((items, 2, symbols, length), F32),
                pltpu.SemaphoreType.DMA((items,)),
                pltpu.SemaphoreType.DMA((items,)),
            ],
        ),
        compiler_params=pltpu.CompilerParams(vmem_limit_bytes=VMEM_LIMIT),
        cost_estimate=HEAVY,
        name="despread",
    )(source, jnp.asarray(table), *pieces, *totals, *after)


def on_device(channel, received, step_sizes, hop_offset, user_order):
    blocks = lax.axis_size("blk")
    groups = lax.axis_size("tones")
    pairs = blocks // 2
    half = channel.shape[0] // 2
    users = channel.shape[2]
    rows = received.shape[2] // blocks
    owners = blocks * groups
    position = lax.axis_index("blk")
    offset = hop_offset[lax.axis_index("tones")]
    side = position % 2
    pair = position // 2

    swap = [(p, p ^ 1) for p in range(blocks)]
    onward = [(p, (p + 2) % blocks) for p in range(blocks)]

    doubles = max((half - 4) // 2, 0)
    sizes = [1] + [2] * doubles + [1] * (half - 1 - 2 * doubles)
    starts = [sum(sizes[:c]) for c in range(len(sizes))]
    chunks = len(sizes)

    place = (pair.reshape(1), lax.axis_index("tones").reshape(1), hop_offset)
    side_alone = side.reshape(1)
    side_and_slot = jnp.stack([side, offset % 2])
    order = (user_order[:, None] == jnp.arange(users, dtype=jnp.int32)[None, :]).astype(BF16)

    begins = (jnp.arange(blocks, dtype=jnp.int32)[:, None] + hop_offset[None, :]) % blocks
    source = jnp.where(begins % 2 == 0, begins // 2 + pairs - 1, begins // 2) % pairs

    own, peer, later, odd, pieces = {}, {}, {}, {}, []

    def ready(c, first_tone, carry, after):
        scalars = (first_tone.reshape(1),) + place
        return prepare(
            channel, received, step_sizes, scalars, starts[c], sizes[c], blocks, carry, after
        )

    def ready_peer(c, after):
        sent = ready(c, (1 - side) * half, 8 if c == 0 else 0, after)
        peer[c] = [lax.ppermute(sent[0], "blk", swap)]
        later[c] = sent[1:]
        return sent[0]

    def send_later(c, after):
        for value in later[c]:
            value = held_back(value, after)
            peer[c].append(lax.ppermute(value, "blk", swap))
            after = [value]
        return after[0]

    def ready_own(c, after):
        own[c] = ready(c, side * half, 0, after)
        return own[c][0]

    def complete(c, after):
        even, moved = odd[c]
        done = finish(rows, owners, side_and_slot, rates, own[c], peer[c], even, moved, order, after)
        pieces.append(
            lax.all_to_all(done, ("blk", "tones"), split_axis=0, concat_axis=0, tiled=True)
        )
        return done

    def bring_together(begin, end, total, last, after):
        return despread(
            pieces[begin:end],
            starts[begin:end],
            groups,
            half,
            blocks,
            rows,
            source.reshape(-1),
            total,
            last,
            after,
        )

    before = ready_peer(0, [])
    before = send_later(0, [before])
    if chunks > 1:
        before = ready_peer(1, [before])
    before = ready_own(0, [before])
    peer_rates = peer[0][0][0, users + 4 * rows, :2].reshape(1, 2)
    rates = jnp.where(
        side == 0,
        jnp.concatenate([step_sizes, peer_rates], 0),
        jnp.concatenate([peer_rates, step_sizes], 0),
    )
    ahead = {c: [c + 1] for c in range(chunks - 1)}
    parts = {}
    if chunks > 8:
        for c in range(chunks - 3, chunks):
            ahead[c - 1].remove(c)
            ahead[c - 5].append(c)
        parts = {chunks - 5: chunks - 6}
    begin, total = 0, None
    for c in range(chunks):
        before = chain(0, False, rows, side_alone, rates, own[c], peer[c], [], [before])
        both = lax.ppermute(before, "blk", onward)
        if c > 0:
            before = complete(c - 1, [before] + ([] if c >= chunks - 2 else pieces[-1:]))
        if c + 1 < chunks:
            before = send_later(c + 1, [before])
        if c + 2 < chunks:
            before = ready_peer(c + 2, [before])
        for other in ahead.get(c, []):
            before = ready_own(other, [before])
        for r in range(1, pairs):
            after = [before] + (pieces[-2:-1] if c >= chunks - 2 else [])
            done = chain(r, r == pairs - 1, rows, side_alone, rates, own[c], peer[c], [both], after)
            if r < pairs - 1:
                both = lax.ppermute(done, "blk", onward)
                before = done
        even, moving = done
        odd[c] = (even, lax.ppermute(moving, "blk", onward))
        before = even
        if c in parts:
            total = bring_together(begin, parts[c], total, False, [before])
            begin, before = parts[c], total
    before = complete(chunks - 1, [before] + pieces[-1:])
    if begin < chunks - 1:
        total = bring_together(begin, chunks - 1, total, False, [before])
    return bring_together(chunks - 1, chunks, total, True, [])


def solution(mesh):
    in_specs = (
        P("tones", None, None, "blk"),
        P("tones", None, None, "blk"),
        P("blk", None),
        P(),
        P(),
    )
    out_specs = P(("blk", "tones"), None, None, None)
    return jax.shard_map(
        on_device, mesh=mesh, in_specs=in_specs, out_specs=out_specs, check_vma=False
    )
```
